32 devices in a mesh: seq: 8 (over z, x), rep: 4 (over y, core).
Axes of the slice: x: 2, y: 2, z: 4, core: 2. Of those that a mesh axis runs over, the one named last changes fastest.
Arguments:
- layer_incoming: bfloat16 [4, 2048, 1024], P('rep', 'seq'), may hold values from -6 to 6
- series_extents: int32 [4, 8], P('rep'), may hold values from 0 to 2048, as said below
- emitted_adjoint: bfloat16 [4, 2048, 1024], P('rep', 'seq'), may hold values from -6 to 6
- norm1_scaling: bfloat16 [1024], P(('seq', 'rep')), may hold values from 0.5 to 1.5
- norm1_offset: bfloat16 [1024], P(('seq', 'rep')), may hold values from -1.75 to 1.75
- mixer_lookup_portion: bfloat16 [1024], P(('seq', 'rep')), may hold values from 0 to 1
- mixer_payload_portion: bfloat16 [1024], P(('seq', 'rep')), may hold values from 0 to 1
- mixer_accept_portion: bfloat16 [1024], P(('seq', 'rep')), may hold values from 0 to 1
- temporal_fading_log: bfloat16 [1024], P(('seq', 'rep')), may hold values from -14 to -2
- present_step_reward: bfloat16 [1024], P(('seq', 'rep')), may hold values from -1 to 1
- mixer_lookup_matrix: bfloat16 [1024, 1024], P(('seq', 'rep')), may hold values from -0.1875 to 0.1875
- mixer_payload_matrix: bfloat16 [1024, 1024], P(('seq', 'rep')), may hold values from -0.1875 to 0.1875
- mixer_accept_matrix: bfloat16 [1024, 1024], P(('seq', 'rep')), may hold values from -0.1875 to 0.1875
- mixer_emit_matrix: bfloat16 [1024, 1024], P(('seq', 'rep')), may hold values from -1.5 to 1.5
- norm2_scaling: bfloat16 [1024], P(('seq', 'rep')), may hold values from 0.5 to 1.5
- norm2_offset: bfloat16 [1024], P(('seq', 'rep')), may hold values from -1.75 to 1.75
- feedforward_lookup_portion: bfloat16 [1024], P(('seq', 'rep')), may hold values from 0 to 1
- feedforward_accept_portion: bfloat16 [1024], P(('seq', 'rep')), may hold values from 0 to 1
- feedforward_lookup_matrix: bfloat16 [1024, 4096], P(('seq', 'rep')), may hold values from -0.1875 to 0.1875
- feedforward_payload_matrix: bfloat16 [4096, 1024], P(('seq', 'rep')), may hold values from -0.09375 to 0.09375
- feedforward_accept_matrix: bfloat16 [1024, 1024], P(('seq', 'rep')), may hold values from -0.1875 to 0.1875
Outputs:
- block_output: bfloat16 [4, 2048, 1024], P('rep', 'seq')
- input_grad: float32 [4, 2048, 1024], P('rep', 'seq')
- ln1_gain_grad: float32 [1024], P(('seq', 'rep'))
- ln1_bias_grad: float32 [1024], P(('seq', 'rep'))
- att_mix_k_grad: float32 [1024], P(('seq', 'rep'))
- att_mix_v_grad: float32 [1024], P(('seq', 'rep'))
- att_mix_r_grad: float32 [1024], P(('seq', 'rep'))
- time_decay_grad: float32 [1024], P(('seq', 'rep'))
- time_first_grad: float32 [1024], P(('seq', 'rep'))
- att_key_grad: float32 [1024, 1024], P(('seq', 'rep'))
- att_value_grad: float32 [1024, 1024], P(('seq', 'rep'))
- att_receptance_grad: float32 [1024, 1024], P(('seq', 'rep'))
- att_output_grad: float32 [1024, 1024], P(('seq', 'rep'))
- ln2_gain_grad: float32 [1024], P(('seq', 'rep'))
- ln2_bias_grad: float32 [1024], P(('seq', 'rep'))
- ffn_mix_k_grad: float32 [1024], P(('seq', 'rep'))
- ffn_mix_r_grad: float32 [1024], P(('seq', 'rep'))
- ffn_key_grad: float32 [1024, 4096], P(('seq', 'rep'))
- ffn_value_grad: float32 [4096, 1024], P(('seq', 'rep'))
- ffn_receptance_grad: float32 [1024, 1024], P(('seq', 'rep'))
The draws below stay inside these ranges and needn't reach their ends.
Inputs may be any that keep to these rules, and one draw needn't show every extreme that they name: `series_extents`: row g lists, in order, the lengths of the sequences that lie end to end over the 2048 tokens of group g, each 256, 1024 or 2048, followed by zeros; they sum to 2048, and at least one is 2048.
All inputs are finite; a program needn't handle non-finite values.
Results may differ from the reference program's by a relative error of at most 0.014.
Values may be sent and summed in bfloat16 or wider, within the bound.
No kernel may reach another device: no remote copies, remote signals or barrier semaphores. Data moves between devices by JAX's collectives and lax.ppermute only.
A program may use at most 192 MiB of HBM per device.

```python
import math
import jax
import jax.numpy as jnp
from jax import lax

MODEL_BREADTH = 1024
FF = 4096
LEN_SHORT = 256
LEN_MID = 1024
LEN_LONG = 2048
GROUP = 2048
GROUPS = 4
SEQS = 8


def draw_series_extents(key, part):
    key = jax.random.fold_in(key, 5)
    units_all = GROUP // LEN_SHORT
    mid_units = LEN_MID // LEN_SHORT
    long_units = LEN_LONG // LEN_SHORT
    table = jnp.array([1, mid_units, long_units], jnp.int32)

    def one_row(row_key):
        pick_key, order_key = jax.random.split(row_key, 2)
        picks = jax.random.randint(pick_key, (SEQS,), 0, 3)

        def step(left, inputs):
            index, pick = inputs
            wanted = jnp.where(index == 0, long_units, jnp.take(table, pick)).astype(jnp.int32)
            taken = jnp.where(wanted <= left, wanted, jnp.where(mid_units <= left, mid_units, jnp.minimum(left, 1))).astype(jnp.int32)
            return ((left - taken).astype(jnp.int32), (taken * LEN_SHORT).astype(jnp.int32))
        slots = jnp.arange(SEQS, dtype=jnp.int32)
        final_left, lengths = lax.scan(step, jnp.array(units_all, jnp.int32), (slots, picks))
        shuffled = jnp.take(lengths, jax.random.permutation(order_key, SEQS))
        order = jnp.argsort((shuffled == 0).astype(jnp.int32), stable=True)
        return jnp.take(shuffled, order).astype(jnp.int32)
    return jax.vmap(one_row)(jax.random.split(key, GROUPS))


def draw_temporal_fading_log(key, part):
    key = jax.random.fold_in(key, 11)
    pick_key, slow_key, fast_key = jax.random.split(key, 3)
    portion_quantity = 0.5
    slow_pick = jax.random.uniform(pick_key, (MODEL_BREADTH,)) < portion_quantity
    slow_log = jax.random.uniform(slow_key, (MODEL_BREADTH,), minval=math.log(0.2 / LEN_LONG), maxval=math.log(2.0 / LEN_LONG))
    fast_log = jax.random.uniform(fast_key, (MODEL_BREADTH,), minval=math.log(0.04), maxval=math.log(0.1))
    return jnp.where(slow_pick, slow_log, fast_log).astype(jnp.bfloat16)


def levels(rng, shape, cuts, least, top_value):
    def one(dim, blocks):
        draws = jax.random.uniform(jax.random.fold_in(jax.random.fold_in(rng, 6), dim), (blocks,), jnp.float32, least / len(cuts), top_value / len(cuts))
        return jnp.repeat(jnp.exp(draws), shape[dim] // blocks).reshape((-1,) + (1,) * (len(shape) - dim - 1))

    level = one(*cuts[0])
    for cut in cuts[1:]:
        level = level * one(*cut)
    return level


def centred(own_key, extent, spread, most, shards=(), held_as=jnp.bfloat16):
    result = spread * jax.random.normal(own_key, extent, jnp.float32)
    if shards:
        result = result * levels(own_key, extent, shards, -0.22, 0.18)
    return jnp.clip(result, -most, most).astype(held_as)


def setup_inputs(seed: int = 0) -> dict:
    key_of = jax.random.split(jax.random.key(seed), 22)
    return {
        "layer_incoming": centred(key_of[0], (GROUPS, GROUP, MODEL_BREADTH), 1.0, 6.0, ((0, 4), (1, 8))),
        "series_extents": draw_series_extents(jax.random.fold_in(key_of[21], 71), 0),
        "emitted_adjoint": centred(key_of[2], (GROUPS, GROUP, MODEL_BREADTH), 1.0, 6.0, ((0, 4), (1, 8))),
        "norm1_scaling": jnp.clip(1.0 + 0.1 * jax.random.normal(key_of[3], (MODEL_BREADTH,), jnp.float32), 0.5, 1.5).astype(jnp.bfloat16),
        "norm1_offset": centred(key_of[4], (MODEL_BREADTH,), 0.3, 1.75, ((0, 32),)),
        "mixer_lookup_portion": jnp.clip(1.0 * jax.random.uniform(key_of[5], (MODEL_BREADTH,), jnp.float32) ** levels(key_of[5], (MODEL_BREADTH,), ((0, 32),), -0.2, 0.2), 0.0, 1.0).astype(jnp.bfloat16),
        "mixer_payload_portion": jnp.clip(1.0 * jax.random.uniform(key_of[6], (MODEL_BREADTH,), jnp.float32) ** levels(key_of[6], (MODEL_BREADTH,), ((0, 32),), -0.2, 0.2), 0.0, 1.0).astype(jnp.bfloat16),
        "mixer_accept_portion": jnp.clip(1.0 * jax.random.uniform(key_of[7], (MODEL_BREADTH,), jnp.float32) ** levels(key_of[7], (MODEL_BREADTH,), ((0, 32),), -0.2, 0.2), 0.0, 1.0).astype(jnp.bfloat16),
        "temporal_fading_log": draw_temporal_fading_log(jax.random.fold_in(key_of[21], 71), 0),
        "present_step_reward": jnp.clip(jax.random.uniform(key_of[9], (MODEL_BREADTH,), jnp.float32, -1.0, 1.0) * levels(key_of[9], (MODEL_BREADTH,), ((0, 32),), -0.4, 0.0), -1.0, 1.0).astype(jnp.bfloat16),
        "mixer_lookup_matrix": centred(key_of[10], (MODEL_BREADTH, MODEL_BREADTH), MODEL_BREADTH ** -0.5, 0.1875, ((0, 32),)),
        "mixer_payload_matrix": centred(key_of[11], (MODEL_BREADTH, MODEL_BREADTH), MODEL_BREADTH ** -0.5, 0.1875, ((0, 32),)),
        "mixer_accept_matrix": centred(key_of[12], (MODEL_BREADTH, MODEL_BREADTH), MODEL_BREADTH ** -0.5, 0.1875, ((0, 32),)),
        "mixer_emit_matrix": centred(key_of[13], (MODEL_BREADTH, MODEL_BREADTH), (MODEL_BREADTH // 64) ** -0.5, 1.5, ((0, 32),)),
        "norm2_scaling": jnp.clip(1.0 + 0.1 * jax.random.normal(key_of[14], (MODEL_BREADTH,), jnp.float32), 0.5, 1.5).astype(jnp.bfloat16),
        "norm2_offset": centred(key_of[15], (MODEL_BREADTH,), 0.3, 1.75, ((0, 32),)),
        "feedforward_lookup_portion": jnp.clip(1.0 * jax.random.uniform(key_of[16], (MODEL_BREADTH,), jnp.float32) ** levels(key_of[16], (MODEL_BREADTH,), ((0, 32),), -0.2, 0.2), 0.0, 1.0).astype(jnp.bfloat16),
        "feedforward_accept_portion": jnp.clip(1.0 * jax.random.uniform(key_of[17], (MODEL_BREADTH,), jnp.float32) ** levels(key_of[17], (MODEL_BREADTH,), ((0, 32),), -0.2, 0.2), 0.0, 1.0).astype(jnp.bfloat16),
        "feedforward_lookup_matrix": centred(key_of[18], (MODEL_BREADTH, FF), MODEL_BREADTH ** -0.5, 0.1875, ((0, 32),)),
        "feedforward_payload_matrix": centred(key_of[19], (FF, MODEL_BREADTH), FF ** -0.5, 0.09375, ((0, 32),)),
        "feedforward_accept_matrix": centred(key_of[20], (MODEL_BREADTH, MODEL_BREADTH), MODEL_BREADTH ** -0.5, 0.1875, ((0, 32),)),
    }


@jax.custom_vjp
def reduced_matrix(v):
    return lax.optimization_barrier(v.astype(jnp.bfloat16)).astype(jnp.float32)

@jax.custom_vjp
def reduced_reverse(v):
    return v

def low_keep(v):
    return (reduced_matrix(v), None)

def low_pass(kept, grad):
    return (grad,)

def back_keep(v):
    return (v, None)

def back_low(kept, grad):
    return (reduced_matrix(grad),)
reduced_matrix.defvjp(low_keep, low_pass)
reduced_reverse.defvjp(back_keep, back_low)
EPSILON = 1e-05

def matmul(left, right):
    return jnp.dot(left, right, precision=lax.Precision.HIGHEST, preferred_element_type=jnp.float32)

def layer_norm(inputs, gain, bias):
    center = lax.optimization_barrier(jnp.mean(inputs, axis=-1, keepdims=True))
    deviation = inputs - center
    variance = lax.optimization_barrier(jnp.mean(deviation * deviation, axis=-1, keepdims=True))
    return deviation * lax.rsqrt(variance + EPSILON) * gain + bias

def token_shift(normed, retain_mask):
    shifted = jnp.concatenate([jnp.zeros_like(normed[:1]), normed[:-1]], axis=0)
    return shifted * retain_mask[:, None]

def keep_mask(lengths, rows):
    begins = (jnp.cumsum(lengths) - lengths).astype(jnp.int32)
    places = jnp.arange(rows, dtype=jnp.int32)
    starting = jnp.any(places[:, None] == begins[None, :], axis=1)
    return jnp.where(starting, 0.0, 1.0).astype(jnp.float32)

def recurrent_average_sweep(lookup_rows, payload_rows, temporal_fading_log, present_step_reward, retain_mask):
    rows, breadth_count = lookup_rows.shape
    span_length = math.gcd(rows, 128)
    fade = jnp.exp(-jnp.exp(temporal_fading_log))
    reward_array = jnp.exp(present_step_reward)

    def token_step(carry, row):
        num_state, den_state = carry
        key_row, payload_element, keep_row = row
        earlier_dividend = num_state * keep_row
        earlier_divisor = den_state * keep_row
        scaling_coefficient = jnp.exp(key_row)
        outcome_quantity = (earlier_dividend + reward_array * scaling_coefficient * payload_element) / (earlier_divisor + reward_array * scaling_coefficient)
        return ((fade * earlier_dividend + scaling_coefficient * payload_element, fade * earlier_divisor + scaling_coefficient), outcome_quantity)

    @jax.checkpoint
    def block_step(carry, block):
        return lax.scan(token_step, carry, block)
    zero_filled = jnp.zeros((breadth_count,), lookup_rows.dtype)
    block_list = (lookup_rows.reshape(-1, span_length, breadth_count), payload_rows.reshape(-1, span_length, breadth_count), retain_mask.reshape(-1, span_length))
    final_state, outputs = lax.scan(block_step, (zero_filled, zero_filled), block_list)
    return outputs.reshape(rows, breadth_count)

def block_forward(inputs, retain_mask, model_settings):
    norm1_scaling, norm1_offset, mixer_lookup_portion, mixer_payload_portion, mixer_accept_portion, temporal_fading_log, present_step_reward, mixer_lookup_matrix, mixer_payload_matrix, mixer_accept_matrix, mixer_emit_matrix, norm2_scaling, norm2_offset, feedforward_lookup_portion, feedforward_accept_portion, feedforward_lookup_matrix, feedforward_payload_matrix, feedforward_accept_matrix = model_settings
    normed = layer_norm(inputs, norm1_scaling, norm1_offset)
    shifted = token_shift(normed, retain_mask)
    mixed_key = reduced_matrix(normed * mixer_lookup_portion + shifted * (1.0 - mixer_lookup_portion))
    mixed_value = reduced_matrix(normed * mixer_payload_portion + shifted * (1.0 - mixer_payload_portion))
    mixed_recept = reduced_matrix(normed * mixer_accept_portion + shifted * (1.0 - mixer_accept_portion))
    lookup_rows = reduced_reverse(reduced_matrix(matmul(mixed_key, mixer_lookup_matrix)))
    payload_rows = reduced_reverse(reduced_matrix(matmul(mixed_value, mixer_payload_matrix)))
    recept = jax.nn.sigmoid(reduced_reverse(matmul(mixed_recept, mixer_accept_matrix)))
    scaled_combination = reduced_reverse(reduced_matrix(recurrent_average_sweep(lookup_rows, payload_rows, temporal_fading_log, present_step_reward, retain_mask)))
    attended = reduced_reverse(matmul(reduced_matrix(recept * scaled_combination), mixer_emit_matrix))
    middle = inputs + attended
    normed2 = layer_norm(middle, norm2_scaling, norm2_offset)
    shifted2 = token_shift(normed2, retain_mask)
    ffn_in_key = reduced_matrix(normed2 * feedforward_lookup_portion + shifted2 * (1.0 - feedforward_lookup_portion))
    ffn_in_recept = reduced_matrix(normed2 * feedforward_accept_portion + shifted2 * (1.0 - feedforward_accept_portion))
    pre_hidden = reduced_reverse(matmul(ffn_in_key, feedforward_lookup_matrix))
    hidden = reduced_matrix(jnp.square(jax.nn.relu(pre_hidden)))
    value_out = reduced_reverse(matmul(hidden, feedforward_payload_matrix))
    gate = jax.nn.sigmoid(reduced_reverse(matmul(ffn_in_recept, feedforward_accept_matrix)))
    return middle + gate * value_out

def reference(layer_incoming, series_extents, emitted_adjoint, norm1_scaling, norm1_offset, mixer_lookup_portion, mixer_payload_portion, mixer_accept_portion, temporal_fading_log, present_step_reward, mixer_lookup_matrix, mixer_payload_matrix, mixer_accept_matrix, mixer_emit_matrix, norm2_scaling, norm2_offset, feedforward_lookup_portion, feedforward_accept_portion, feedforward_lookup_matrix, feedforward_payload_matrix, feedforward_accept_matrix):
    model_settings = tuple((element_item.astype(jnp.float32) for element_item in (norm1_scaling, norm1_offset, mixer_lookup_portion, mixer_payload_portion, mixer_accept_portion, temporal_fading_log, present_step_reward, mixer_lookup_matrix, mixer_payload_matrix, mixer_accept_matrix, mixer_emit_matrix, norm2_scaling, norm2_offset, feedforward_lookup_portion, feedforward_accept_portion, feedforward_lookup_matrix, feedforward_payload_matrix, feedforward_accept_matrix)))

    def per_group(totals, group):
        inputs, lengths, cotangent = group
        retain_mask = keep_mask(lengths, inputs.shape[0])

        def forward(block_rows, weights):
            return block_forward(block_rows, retain_mask, weights)
        output, pullback = jax.vjp(forward, inputs.astype(jnp.float32), model_settings)
        grad_rows, grad_params = pullback(cotangent.astype(jnp.float32))
        totals = jax.tree.map(jnp.add, totals, grad_params)
        return (totals, (output.astype(jnp.bfloat16), grad_rows))
    zero_filled = tuple((jnp.zeros_like(element_item) for element_item in model_settings))
    totals, (outputs, input_grads) = lax.scan(per_group, zero_filled, (layer_incoming, series_extents, emitted_adjoint))
    return (outputs, input_grads, totals[0], totals[1], totals[2], totals[3], totals[4], totals[5], totals[6], totals[7], totals[8], totals[9], totals[10], totals[11], totals[12], totals[13], totals[14], totals[15], totals[16], totals[17])
```

```python
from functools import partial

import jax
import jax.numpy as jnp
from jax import lax
from jax.experimental import pallas as pl
from jax.experimental.pallas import tpu as pltpu
from jax.sharding import Mesh, PartitionSpec as P

EPSILON = 1e-05
F32 = jnp.float32
BF16 = jnp.bfloat16
CHIPS = ("z", "x", "y")
SEQ = ("z", "x")
ALL = ("z", "x", "y", "c")
TILE = 16


def ring(count, step=1):
    return [(i, (i + step) % count) for i in range(count)]


def swap(block):
    return lax.ppermute(block, "c", ring(2))


def along_seq(block, step):
    count = lax.axis_size(SEQ)
    pairs = [(i, i + step) for i in range(count) if 0 <= i + step < count]
    return lax.ppermute(block, SEQ, pairs)


def gather(shard, order):
    have = []
    block = shard
    for axis in order:
        count = lax.axis_size(axis)
        me = lax.axis_index(axis)
        place = sum(1 for other in have if CHIPS.index(other) < CHIPS.index(axis))
        have.append(axis)
        whole = jnp.zeros(block.shape[:place] + (count,) + block.shape[place:], block.dtype)
        piece = block
        for step in range(count):
            if step:
                piece = lax.ppermute(piece, axis, ring(count))
            whole = lax.dynamic_update_index_in_dim(whole, piece, lax.rem(me - step + count, count), place)
        block = whole
    return block.reshape(-1, shard.shape[-1])


def scatter_sum(whole, order):
    columns = whole.shape[-1]
    left = list(CHIPS)
    block = whole.reshape(tuple(lax.axis_size(axis) for axis in CHIPS) + (-1, columns))
    for axis in order:
        count = lax.axis_size(axis)
        me = lax.axis_index(axis)
        place = left.index(axis)
        left.remove(axis)

        def part(step):
            return lax.dynamic_index_in_dim(
                block, lax.rem(me - step + count, count), place, keepdims=False
            )

        total = part(1)
        for step in range(2, count + 1):
            moved = lax.ppermute(total.astype(BF16), axis, ring(count))
            total = moved.astype(F32) + part(step).astype(F32)
        block = total
    return block


def dot(left, right):
    return jnp.dot(left, right, preferred_element_type=F32)


def dot_back(grad, weight):
    return lax.dot_general(grad, weight, (((1,), (1,)), ((), ())), preferred_element_type=F32)


def outer(left, right):
    return lax.dot_general(left, right, (((0,), (0,)), ((), ())), preferred_element_type=F32)


def norm_parts(rows):
    center = jnp.mean(rows, axis=-1, keepdims=True)
    deviation = rows - center
    variance = jnp.mean(deviation * deviation, axis=-1, keepdims=True)
    inverse = lax.rsqrt(variance + EPSILON)
    return deviation * inverse, inverse


def norm_back(grad, zhat, inverse, gain):
    scaled = grad * gain
    return inverse * (
        scaled
        - jnp.mean(scaled, axis=-1, keepdims=True)
        - zhat * jnp.mean(scaled * zhat, axis=-1, keepdims=True)
    )


def shift_down(rows, first):
    return jnp.concatenate([first, rows[:, :-1]], axis=1)


def shift_up(rows, last):
    return jnp.concatenate([rows[:, 1:], last], axis=1)


def shift_rows(rows, distance):
    return pltpu.roll(rows, distance % rows.shape[0], 0)


def fade_tables(rate, reverse):
    breadth = rate.shape[-1]
    place = lax.broadcasted_iota(jnp.int32, (TILE, breadth), 0)
    if reverse:
        place = TILE - 1 - place
    steps = []
    distance = 1
    while distance < TILE:
        factor = jnp.where(place >= distance, jnp.exp(-rate * float(distance)), 0.0)
        steps.append((distance, factor))
        distance *= 2
    passed = jnp.exp(-rate * place.astype(F32))
    before = (place >= 1).astype(F32)
    return steps, passed, before


def scan_tile(terms, steps, reverse):
    for distance, factor in steps:
        terms = terms + factor * shift_rows(terms, -distance if reverse else distance)
    return terms


def wkv_kernel(
    groups, key_ref, value_ref, recept_ref, rate_ref, bonus_ref, num_ref, den_ref,
    gated_ref, prior_num_ref, prior_den_ref,
):
    rows = key_ref.shape[0] // groups
    rate = rate_ref[...]
    bonus = bonus_ref[...]
    steps, passed, before = fade_tables(rate, False)
    tile_fade = jnp.exp(-rate * float(TILE))

    def body(index, carry):
        states = []
        for group in range(groups):
            num, den = carry[2 * group], carry[2 * group + 1]
            at = pl.ds(pl.multiple_of(group * rows + index * TILE, TILE), TILE)
            grown = jnp.exp(key_ref[at, :].astype(F32))
            product = grown * value_ref[at, :].astype(F32)
            inner_num = scan_tile(product, steps, False)
            inner_den = scan_tile(grown, steps, False)
            prior_num = shift_rows(inner_num, 1) * before + passed * num
            prior_den = shift_rows(inner_den, 1) * before + passed * den
            prior_num_ref[at, :] = prior_num
            prior_den_ref[at, :] = prior_den
            wkv = (prior_num + bonus * product) / (prior_den + bonus * grown)
            gated_ref[at, :] = (recept_ref[at, :] * wkv.astype(BF16).astype(F32)).astype(BF16)
            states.append(inner_num[TILE - 1 :, :] + tile_fade * num)
            states.append(inner_den[TILE - 1 :, :] + tile_fade * den)
        return tuple(states)

    start = []
    for group in range(groups):
        start += [num_ref[group : group + 1, :], den_ref[group : group + 1, :]]
    lax.fori_loop(0, rows // TILE, body, tuple(start))


def wkv_back_kernel(
    groups, key_ref, value_ref, prior_num_ref, prior_den_ref, weighted_ref, rate_ref, bonus_ref,
    num_ref, den_ref, dkey_ref, dvalue_ref, decay_ref, first_ref,
):
    rows = key_ref.shape[0] // groups
    rate = rate_ref[...]
    bonus = bonus_ref[...]
    steps, passed, before = fade_tables(rate, True)
    tile_fade = jnp.exp(-rate * float(TILE))
    decay_ref[...] = jnp.zeros_like(decay_ref)
    first_ref[...] = jnp.zeros_like(first_ref)

    def body(step, carry):
        index = rows // TILE - 1 - step
        states = []
        for group in range(groups):
            num, den = carry[2 * group], carry[2 * group + 1]
            at = pl.ds(pl.multiple_of(group * rows + index * TILE, TILE), TILE)
            grown = jnp.exp(key_ref[at, :].astype(F32))
            value = value_ref[at, :].astype(F32)
            prior_num = prior_num_ref[at, :]
            prior_den = prior_den_ref[at, :]
            wkv_den = prior_den + bonus * grown
            wkv = (prior_num + bonus * grown * value) / wkv_den
            grad = weighted_ref[at, :].astype(F32) / wkv_den
            inner_num = scan_tile(grad, steps, True)
            inner_den = scan_tile(-grad * wkv, steps, True)
            lam_num = shift_rows(inner_num, -1) * before + passed * num
            lam_den = shift_rows(inner_den, -1) * before + passed * den
            bonus_grad = bonus * grad
            dvalue_ref[at, :] = (grown * (bonus_grad + lam_num)).astype(BF16)
            direct = bonus_grad * (value - wkv)
            dkey_ref[at, :] = (grown * (direct + lam_num * value + lam_den)).astype(BF16)
            first_ref[...] += grown * direct
            decay_ref[...] += lam_num * prior_num + lam_den * prior_den
            states.append(inner_num[:1, :] + tile_fade * num)
            states.append(inner_den[:1, :] + tile_fade * den)
        return tuple(states)

    start = []
    for group in range(groups):
        start += [num_ref[group : group + 1, :], den_ref[group : group + 1, :]]
    lax.fori_loop(0, rows // TILE, body, tuple(start))


def wkv_call(kernel, groups, shapes, operands):
    return pl.pallas_call(
        partial(kernel, groups),
        out_shape=shapes,
        compiler_params=pltpu.CompilerParams(vmem_limit_bytes=32 << 20),
    )(*operands)


def per_device(
    layer_incoming,
    series_extents,
    emitted_adjoint,
    norm1_scaling,
    norm1_offset,
    mixer_lookup_portion,
    mixer_payload_portion,
    mixer_accept_portion,
    temporal_fading_log,
    present_step_reward,
    mixer_lookup_matrix,
    mixer_payload_matrix,
    mixer_accept_matrix,
    mixer_emit_matrix,
    norm2_scaling,
    norm2_offset,
    feedforward_lookup_portion,
    feedforward_accept_portion,
    feedforward_lookup_matrix,
    feedforward_payload_matrix,
    feedforward_accept_matrix,
):
    devices = lax.axis_size(ALL)
    chips = lax.axis_size(CHIPS)
    parts = lax.axis_size(SEQ)
    core = lax.axis_index("c")
    place = lax.axis_index(SEQ)
    rows, breadth = layer_incoming.shape[1:]
    own_rows = mixer_lookup_matrix.shape[0]
    hidden_rows = feedforward_payload_matrix.shape[0]

    vectors = jnp.stack(
        [
            norm1_scaling, norm1_offset, mixer_lookup_portion, mixer_payload_portion,
            mixer_accept_portion, norm2_scaling, norm2_offset, feedforward_lookup_portion,
            feedforward_accept_portion, temporal_fading_log, present_step_reward,
        ]
    )
    vectors = lax.all_to_all(
        jnp.broadcast_to(vectors[None], (devices,) + vectors.shape), ALL, 0, 0, tiled=True
    )
    vectors = vectors.astype(F32).transpose(1, 0, 2)
    gain1, bias1, mix_k, mix_v, mix_r, gain2, bias2, mix_fk, mix_fr = vectors[:9].reshape(9, breadth)
    channel = lax.dynamic_index_in_dim(
        vectors[9:].reshape(2, chips, 2, own_rows), core, 2, keepdims=False
    ).reshape(2, 1, -1)
    rate, bonus = jnp.exp(channel[0]), jnp.exp(channel[1])

    def by_core(matrix, width):
        return matrix.reshape(own_rows, -1, 2, width).swapaxes(0, 2)

    halves = jnp.concatenate(
        [
            by_core(matrix, width).swapaxes(1, 2).reshape(2, own_rows, -1)
            for matrix, width in (
                (mixer_lookup_matrix, own_rows),
                (mixer_payload_matrix, own_rows),
                (mixer_accept_matrix, own_rows),
                (feedforward_lookup_matrix, hidden_rows),
                (feedforward_accept_matrix, breadth // 2),
            )
        ],
        axis=-1,
    )
    mine = lax.dynamic_index_in_dim(halves, core, 0, keepdims=False)
    other = swap(lax.dynamic_index_in_dim(halves, 1 - core, 0, keepdims=False))
    both = lambda own, other: jnp.where(core == 0, jnp.stack([own, other]), jnp.stack([other, own]))
    mine_of = lambda pair: lax.dynamic_index_in_dim(pair, core, 0, keepdims=False)
    other_of = lambda pair: lax.dynamic_index_in_dim(pair, 1 - core, 0, keepdims=False)
    pair = both(mine, other).reshape(2 * own_rows, -1)
    half = breadth // 2
    hidden = pair.shape[1] - 4 * half
    weights_att = gather(pair[:, : 3 * half], ("z", "x", "y"))
    weight_o = gather(mixer_emit_matrix, ("z", "y", "x"))
    weight_fr = gather(pair[:, 3 * half + hidden :], ("z", "y", "x"))
    weight_fk = gather(pair[:, 3 * half : 3 * half + hidden], ("x", "z", "y"))
    weight_fv = gather(feedforward_payload_matrix, ("y", "z", "x"))
    weight_k, weight_v, weight_r = (weights_att[:, i * half : (i + 1) * half] for i in range(3))

    begins = jnp.cumsum(series_extents[0]) - series_extents[0]
    starts = jnp.any(jnp.arange(parts)[:, None] * rows == begins[None, :], axis=1)
    joined = jnp.where(starts, 0.0, 1.0).astype(F32)
    joined = both(joined, swap(joined))
    keep = lax.dynamic_index_in_dim(joined, place, 1)[:, :, None]
    after = jnp.concatenate([joined[:, 1:], jnp.zeros((2, 1), F32)], axis=1)
    keep_after = lax.dynamic_index_in_dim(after, place, 1)[:, :, None]
    index = jnp.arange(parts)
    began = jnp.where((joined == 0.0) & (index[None] <= place), index[None], -1).max(axis=1)
    reach = ((index[None] < place) & (index[None] >= began[:, None])).astype(F32)
    begun = jnp.where((joined == 0.0) & (index[None] > place), index[None], parts).min(axis=1)
    reach_back = ((index[None] > place) & (index[None] < begun[:, None])).astype(F32)

    def entering(ends, reached, distance):
        fades = jnp.exp(-rate[None] * (float(rows) * jnp.maximum(distance, 0).astype(F32))[:, None, None])
        return jnp.sum(ends * (reached.T[:, None, :, None] * fades[:, :, None]), axis=0)

    def spread(ends):
        return lax.all_to_all(
            jnp.broadcast_to(ends[None], (parts,) + ends.shape), SEQ, 0, 0, tiled=True
        )

    own_in = jnp.concatenate([layer_incoming, emitted_adjoint], axis=0)
    both_in = both(own_in, swap(own_in))
    inputs = both_in[:, 0].astype(F32)
    cotangent = both_in[:, 1].astype(F32)
    behind = along_seq(both_in[:, 0, rows - 1 :], 1).astype(F32)
    flat = lambda element: element.reshape(2 * rows, -1)

    zhat1, inverse1 = norm_parts(inputs)
    normed = zhat1 * gain1 + bias1
    normed_behind = (norm_parts(behind)[0] * gain1 + bias1) * keep
    step1 = normed - shift_down(normed, normed_behind)
    mixed = lambda value, step, share: flat(value - step * (1.0 - share)).astype(BF16)
    mixed_k, mixed_v, mixed_r = (mixed(normed, step1, share) for share in (mix_k, mix_v, mix_r))
    keys = dot(mixed_k, weight_k).astype(BF16)
    values = dot(mixed_v, weight_v).astype(BF16)
    recept = jax.nn.sigmoid(dot(mixed_r, weight_r))

    token = jnp.arange(rows, dtype=F32)[:, None]
    grown = jnp.exp(keys.astype(F32)).reshape(2, rows, half)
    product = grown * values.astype(F32).reshape(2, rows, half)
    to_end = jnp.exp(-rate * (rows - 1.0 - token))[None]
    ends = jnp.stack([(product * to_end).sum(axis=1), (grown * to_end).sum(axis=1)])
    enter = entering(spread(ends), reach, place - 1 - index)
    shape = lambda kind: jax.ShapeDtypeStruct((2 * rows, half), kind)
    gated, prior_num, prior_den = wkv_call(
        wkv_kernel, 2, (shape(BF16), shape(F32), shape(F32)),
        (keys, values, recept, rate, bonus, enter[0], enter[1]),
    )

    attended = dot(gated, weight_o)
    middle = inputs + (attended + swap(attended)).reshape(2, rows, breadth)
    zhat2, inverse2 = norm_parts(middle)
    normed2 = zhat2 * gain2 + bias2
    step2 = normed2 - shift_down(normed2, along_seq(normed2[:, rows - 1 :], 1) * keep)
    ffn_k, ffn_r = (mixed(normed2, step2, share) for share in (mix_fk, mix_fr))
    pre_hidden = jax.nn.relu(dot(ffn_k, weight_fk))
    hidden_act = jnp.square(pre_hidden).astype(BF16)
    gate_half = jax.nn.sigmoid(dot(ffn_r, weight_fr))
    gate_other = swap(gate_half)
    gate = jnp.concatenate(
        [jnp.where(core == 0, gate_half, gate_other), jnp.where(core == 0, gate_other, gate_half)], axis=1
    )
    value_part = dot(hidden_act, weight_fv)
    value_out = value_part + swap(value_part)
    block_output = mine_of(
        (middle + (gate * value_out).reshape(2, rows, breadth)).astype(BF16)
    )

    d_value_out = (flat(cotangent) * gate).astype(BF16)
    d_gate_pre = flat(cotangent) * value_out * gate * (1.0 - gate)
    d_gate_pre = lax.dynamic_slice_in_dim(d_gate_pre, core * half, half, 1).astype(BF16)
    d_hidden = dot_back(d_value_out, weight_fv)
    d_pre_hidden = (d_hidden * 2.0 * pre_hidden).astype(BF16)
    grad_fv = outer(hidden_act, d_value_out).astype(BF16)
    grad_fk = outer(ffn_k, d_pre_hidden).astype(BF16)
    grad_fr = outer(ffn_r, d_gate_pre).astype(BF16)
    back = lambda grad, weight: dot_back(grad, weight).reshape(2, rows, breadth)

    def mix_back(grads, shares, step):
        share_grads = [jnp.sum(grad * step, axis=(0, 1)) for grad in grads]
        direct = sum(grad * share for grad, share in zip(grads, shares))
        shifted = sum(grad * (1.0 - share) for grad, share in zip(grads, shares))
        return share_grads, direct, shifted

    grads2 = (back(d_pre_hidden, weight_fk), back(d_gate_pre, weight_fr))
    (share_fk, share_fr), direct2, shifted2 = mix_back(grads2, (mix_fk, mix_fr), step2)
    returned2 = along_seq(shifted2[:, :1] * keep, -1)
    part2 = direct2 + shift_up(shifted2, returned2)
    d_normed2 = part2 + swap(part2)
    d_middle = cotangent + norm_back(d_normed2, zhat2, inverse2, gain2)
    grad_gain2 = jnp.sum(mine_of(d_normed2 * zhat2), axis=0)
    grad_bias2 = jnp.sum(mine_of(d_normed2), axis=0)

    d_attended = flat(d_middle).astype(BF16)
    grad_o = outer(gated, d_attended).astype(BF16)
    d_gated = dot_back(d_attended, weight_o)
    d_weighted = (d_gated * recept).astype(BF16)
    wkv_den = prior_den + bonus * flat(grown)
    wkv = (prior_num + bonus * flat(product)) / wkv_den
    d_recept_pre = (
        d_gated * wkv.astype(BF16).astype(F32) * recept * (1.0 - recept)
    ).astype(BF16)
    from_begin = jnp.exp(-rate * token)[None]
    per_den = d_weighted.astype(F32) / wkv_den
    begin_num = (per_den.reshape(2, rows, half) * from_begin).sum(axis=1)
    begin_den = -((per_den * wkv).reshape(2, rows, half) * from_begin).sum(axis=1)
    enter_back = entering(spread(jnp.stack([begin_num, begin_den])), reach_back, index - place - 1)
    small = jax.ShapeDtypeStruct((TILE, half), F32)
    d_keys, d_values, decay_sum, first_sum = wkv_call(
        wkv_back_kernel, 2, (shape(BF16), shape(BF16), small, small),
        (keys, values, prior_num, prior_den, d_weighted, rate, bonus, enter_back[0], enter_back[1]),
    )
    grad_decay = -rate[0] * jnp.exp(-rate[0]) * decay_sum.sum(axis=0)
    grad_first = first_sum.sum(axis=0)

    grad_att = jnp.concatenate(
        [outer(mixed_k, d_keys), outer(mixed_v, d_values), outer(mixed_r, d_recept_pre)], axis=1
    ).astype(BF16)
    grads1 = (back(d_keys, weight_k), back(d_values, weight_v), back(d_recept_pre, weight_r))
    (share_k, share_v, share_r), direct1, shifted1 = mix_back(grads1, (mix_k, mix_v, mix_r), step1)
    returned1 = along_seq(shifted1[:, :1] * keep, -1)
    part1 = direct1 + shift_up(shifted1, returned1)
    d_normed = mine_of(part1) + swap(other_of(part1))
    own_zhat = mine_of(zhat1)
    input_grad = mine_of(d_middle) + norm_back(d_normed, own_zhat, mine_of(inverse1), gain1)
    grad_gain1 = jnp.sum(d_normed * own_zhat, axis=0)
    grad_bias1 = jnp.sum(d_normed, axis=0)

    def by_channel(grad):
        whole = jnp.zeros((chips, 2, own_rows), F32)
        return lax.dynamic_update_index_in_dim(
            whole, grad.reshape(chips, own_rows), core, 1
        ).reshape(breadth)

    grads = jnp.stack(
        [
            grad_gain1, grad_bias1, share_k, share_v, share_r, by_channel(grad_decay),
            by_channel(grad_first), grad_gain2, grad_bias2, share_fk, share_fr,
        ]
    )
    grads = grads.reshape(11, devices, own_rows).swapaxes(0, 1)
    grads = lax.all_to_all(grads, ALL, 0, 0, tiled=True).sum(axis=0)

    sum_fv = scatter_sum(grad_fv, ("x", "z", "y"))
    sum_fk = scatter_sum(grad_fk, ("y", "z", "x"))
    sum_fr = scatter_sum(grad_fr, ("x", "y", "z"))
    sum_o = scatter_sum(grad_o, ("x", "y", "z"))
    sum_att = scatter_sum(grad_att, ("y", "x", "z"))

    sums = jnp.concatenate([sum_att, sum_fk, sum_fr], axis=1).reshape(2, own_rows, -1)
    mine = lax.dynamic_index_in_dim(sums, core, 0, keepdims=False)
    other = swap(lax.dynamic_index_in_dim(sums, 1 - core, 0, keepdims=False))
    low, high = jnp.where(core == 0, mine, other), jnp.where(core == 0, other, mine)

    def columns(start, size, width):
        pieces = [piece[:, start : start + size].reshape(own_rows, -1, 1, width) for piece in (low, high)]
        return jnp.concatenate(pieces, axis=2).reshape(own_rows, 2 * size)

    return (
        block_output[None],
        input_grad[None],
        *(grads[i] for i in range(7)),
        columns(0, half, own_rows),
        columns(half, half, own_rows),
        columns(2 * half, half, own_rows),
        sum_o,
        *(grads[i] for i in range(7, 11)),
        columns(3 * half, hidden, hidden_rows),
        sum_fv,
        columns(3 * half + hidden, half, half),
    )


def solution(mesh):
    parts, groups = mesh.shape["seq"], mesh.shape["rep"]
    width = groups // 2
    fine = Mesh(mesh.devices.reshape(parts // width, width, width, 2), ALL)
    tokens = P(("y", "c"), SEQ, None)
    vector = P(ALL)
    matrix = P(ALL, None)
    return jax.shard_map(
        per_device,
        mesh=fine,
        in_specs=(
            (tokens, P(("y", "c"), None), tokens)
            + (vector,) * 7
            + (matrix,) * 4
            + (vector,) * 4
            + (matrix,) * 3
        ),
        out_specs=(
            (tokens, tokens) + (vector,) * 7 + (matrix,) * 4 + (vector,) * 4 + (matrix,) * 3
        ),
        check_vma=False,
    )
```

```python
from functools import partial

import jax
import jax.numpy as jnp
from jax import lax
from jax.experimental import pallas as pl
from jax.experimental.pallas import tpu as pltpu
from jax.sharding import Mesh, PartitionSpec as P

EPSILON = 1e-05
F32 = jnp.float32
BF16 = jnp.bfloat16
CHIPS = ("z", "x", "y")
SEQ = ("z", "x")
ALL = ("z", "x", "y", "c")
TILE = 16
FREE = pl.CostEstimate(flops=0, bytes_accessed=0, transcendentals=0)


def ring(count, step=1):
    return [(i, (i + step) % count) for i in range(count)]


def swap(block):
    return lax.ppermute(block, "c", ring(2))


def along_seq(block, step):
    count = lax.axis_size(SEQ)
    pairs = [(i, i + step) for i in range(count) if 0 <= i + step < count]
    return lax.ppermute(block, SEQ, pairs)


ROUNDS = (
    (("x", (0, 0, 0), (0, 1, 0)), ("y", (0, 0, 0), (0, 0, 1)), ("z", (0, 0, 0), (1, 0, 0))),
    (("x", (0, 0, 1), (0, 1, 1)), ("y", (1, 0, 0), (1, 0, 1)), ("z", (1, 0, 0), (2, 0, 0))),
    (("x", (1, 0, 0), (1, 1, 0)), ("y", (2, 0, 0), (2, 0, 1)), ("z", (2, 0, 0), (3, 0, 0))),
    (("x", (3, 0, 0), (3, 1, 0)), ("y", (3, 0, 0), (3, 0, 1)), ("z", (0, 1, 1), (1, 1, 1))),
    (("x", (2, 0, 0), (2, 1, 0)), ("y", (3, 1, 0), (3, 1, 1)), ("z", (1, 1, 1), (2, 1, 1))),
)


def in_rounds():
    return tuple(lax.axis_size(axis) for axis in CHIPS) == (4, 2, 2)


RELATIVES = tuple((z, x, y) for z in range(4) for x in range(2) for y in range(2))
ANYWHERE = pl.BlockSpec(memory_space=pl.ANY)


def chip_table():
    whole = jnp.asarray(RELATIVES, jnp.int32)
    total = jnp.zeros((len(RELATIVES),), jnp.int32)
    for i, axis in enumerate(CHIPS):
        count = lax.axis_size(axis)
        total = total * count + lax.rem(lax.axis_index(axis) + (count - whole[:, i]), count)
    return jnp.concatenate([total, lax.axis_index("c")[None]]).astype(jnp.int32)


def whole_block(shape):
    return pl.BlockSpec(shape, lambda *g: (0,) * len(shape))


def in_hbm(array):
    return pltpu.with_memory_space_constraint(array, pltpu.HBM)


LAST = []


def run(kernel, *, out_shape, vmem=16, grid=(1,), in_specs=None, out_specs=None, grid_spec=None, **settings):
    spec = grid_spec or dict(num_scalar_prefetch=0, grid=grid, in_specs=in_specs, out_specs=out_specs)
    spec.setdefault("scratch_shapes", settings.pop("scratch_shapes", ()))

    def call(*operands):
        marks = list(LAST)
        count = len(operands)

        def body(*refs):
            kernel(*refs[:count], *refs[count + len(marks) :])

        inputs = list(spec["in_specs"]) + [ANYWHERE] * len(marks)
        outs = pl.pallas_call(
            body,
            grid_spec=pltpu.PrefetchScalarGridSpec(**{**spec, "in_specs": inputs}),
            out_shape=out_shape,
            cost_estimate=FREE,
            **settings,
        )(*operands, *marks)
        LAST[:] = [min(jax.tree.leaves(outs), key=lambda out: out.size)]
        return outs

    return call


def hold_kernel(*refs):
    refs[-1][...] = jnp.zeros_like(refs[-1])


def hold(*arrays):
    *arrays, _ = run(
        hold_kernel,
        out_shape=[jax.ShapeDtypeStruct(array.shape, array.dtype) for array in arrays]
        + [jax.ShapeDtypeStruct((8, 128), F32)],
        in_specs=[ANYWHERE] * len(arrays),
        out_specs=[ANYWHERE] * len(arrays) + [whole_block((8, 128))],
        input_output_aliases={i: i for i in range(len(arrays))},
    )(*arrays)
    return arrays


def place_kernel(first, views, aliased, table_ref, *refs):
    blocks = refs[: len(first)]
    outs = refs[len(first) + aliased : -2]
    refs[-2][...] = jnp.zeros_like(refs[-2])
    copies = []
    for i, block in enumerate(blocks):
        for number, (out, source, target) in enumerate(views[0]):
            copies.append(
                pltpu.make_async_copy(
                    block.at[source],
                    outs[out].at[(table_ref[first[i]],) + target],
                    refs[-1].at[i, number],
                )
            )
    for copy in copies:
        copy.start()
    for copy in copies:
        copy.wait()


def place_blocks(table, held, blocks, relatives, views):
    moves, shapes, _ = views
    chips = lax.axis_size(CHIPS)
    first = [RELATIVES.index(relative) for relative in relatives]
    operands = [table, *blocks]
    aliases = {}
    if held is not None:
        aliases = {len(operands) + i: i for i in range(len(shapes))}
        operands += held
    hbm = pl.BlockSpec(memory_space=pltpu.HBM)
    *held, _ = run(
        partial(place_kernel, first, views, len(aliases)),
        grid=(1,),
        in_specs=[pl.BlockSpec(memory_space=pltpu.SMEM)]
        + [whole_block(block.shape) for block in blocks]
        + [hbm] * len(aliases),
        out_specs=[hbm] * len(shapes) + [whole_block((8, 128))],
        out_shape=[jax.ShapeDtypeStruct((chips,) + shape, BF16) for shape in shapes]
        + [jax.ShapeDtypeStruct((8, 128), F32)],
        scratch_shapes=[pltpu.SemaphoreType.DMA((len(blocks), len(moves)))],
        input_output_aliases=aliases,
    )(*operands)
    return held


class GatherRounds:
    def __init__(self, table, block, views):
        self.table, self.views = table, views
        self.have = {(0, 0, 0): block}
        self.held = None

    def place(self, number):
        names = [(0, 0, 0)] if number < 0 else [received for _, _, received in ROUNDS[number]]
        blocks = [self.have[name] for name in names]
        self.held = place_blocks(self.table, self.held, blocks, names, self.views)

    def step(self, number):
        if number:
            names = list({sent: None for _, sent, _ in ROUNDS[number]})
            self.have.update(zip(names, hold(*(self.have[name] for name in names))))
        for axis, sent, received in ROUNDS[number]:
            self.have[received] = lax.ppermute(self.have[sent], axis, ring(lax.axis_size(axis)))


class GatherRings:
    def __init__(self, table, block, views):
        self.held = gather_rings(block, views)

    def place(self, number):
        pass

    def step(self, number):
        pass


def gather_rings(block, views):
    have = []
    shape = block.shape
    for axis in CHIPS:
        count = lax.axis_size(axis)
        me = lax.axis_index(axis)
        have.append(axis)
        place = len(have) - 1
        whole = jnp.zeros(block.shape[:place] + (count,) + block.shape[place:], block.dtype)
        piece = block
        for step in range(count):
            if step:
                piece = lax.ppermute(piece, axis, ring(count))
            whole = lax.dynamic_update_index_in_dim(whole, piece, lax.rem(me - step + count, count), place)
        block = whole
    block = block.reshape((-1,) + shape)
    held = [jnp.zeros(block.shape[:1] + view, block.dtype) for view in views[1]]
    for out, source, target in views[0]:
        held[out] = held[out].at[(slice(None),) + target].set(block[(slice(None),) + source])
    return held


def sum_kernel(counts, views, table_ref, *refs):
    arrays = len(views[1])
    wanted = len(counts)
    grads = refs[: wanted * arrays]
    received = refs[wanted * arrays : wanted * arrays + sum(counts)]
    outs = refs[wanted * arrays + sum(counts) :]
    at = 0
    for i, count in enumerate(counts):
        for out, source, target in views[0]:
            total = grads[i * arrays + out][(0,) + target].astype(F32)
            for j in range(at, at + count):
                total += received[j][source].astype(F32)
            outs[i][source] = total.astype(outs[i].dtype)
        at += count


def sum_blocks(table, grads, relatives, received, views, kind=BF16):
    _, shapes, block_shape = views
    first = [RELATIVES.index(relative) for relative in relatives]
    counts = [len(blocks) for blocks in received]
    flat = [block for blocks in received for block in blocks]
    outs = [jax.ShapeDtypeStruct(block_shape, kind) for _ in relatives]

    def pick(i, shape):
        zeros = (0,) * len(shape)
        return pl.BlockSpec((1,) + shape, lambda g, table: (table[first[i]],) + zeros)

    whole = pl.BlockSpec(block_shape, lambda g, table: (0, 0))
    return run(
        partial(sum_kernel, counts, views),
        grid_spec=dict(
            num_scalar_prefetch=1,
            grid=(1,),
            in_specs=[pick(i, shape) for i in range(len(relatives)) for shape in shapes]
            + [whole] * len(flat),
            out_specs=[whole for _ in outs],
        ),
        out_shape=outs,
        compiler_params=pltpu.CompilerParams(vmem_limit_bytes=14 << 20),
    )(table, *(list(grads) * len(relatives)), *flat)


class ScatterRounds:
    def __init__(self, table, grads, views):
        self.table, self.views = table, views
        self.grads = [in_hbm(grad) for grad in grads]
        self.arrived = {}

    def step(self, number):
        moves = ROUNDS[len(ROUNDS) - 1 - number]
        names = [received for _, _, received in moves]
        came = [self.arrived.pop(name, []) for name in names]
        blocks = sum_blocks(self.table, self.grads, names, came, self.views)
        for (axis, target, _), block in zip(moves, blocks):
            got = lax.ppermute(block, axis, ring(lax.axis_size(axis), -1))
            self.arrived.setdefault(target, []).append(got)

    def result(self):
        came = [self.arrived.pop((0, 0, 0))]
        return sum_blocks(self.table, self.grads, [(0, 0, 0)], came, self.views, kind=F32)[0]


class ScatterRings:
    def __init__(self, table, grads, views):
        self.sums = scatter_rings(grads, views)
        self.views = views

    def step(self, number):
        pass

    def result(self):
        moves, _, block_shape = self.views
        block = jnp.zeros(block_shape, F32)
        for out, source, target in moves:
            block = block.at[source].set(self.sums[out][target])
        return block


def picked(width, core):
    source = lax.broadcasted_iota(jnp.int32, (256, 128), 0)
    target = lax.broadcasted_iota(jnp.int32, (256, 128), 1)
    wanted = (target // width) * (2 * width) + core * width + target % width
    return jnp.where(source == wanted, 1.0, 0.0).astype(BF16)


def pick_kernel(widths, core_ref, *refs):
    matrices, outs = refs[: len(widths)], refs[len(widths) :]
    core = core_ref[0]
    for out, wanted in zip(outs, (core, 1 - core)):
        at = 0
        for width, matrix in zip(widths, matrices):
            half = matrix.shape[1] // 2
            if width == half:
                out[:, at : at + half] = jnp.where(wanted == 0, matrix[:, :half], matrix[:, half:])
            else:
                choice = picked(width, wanted)
                for i in range(half // 128):
                    columns = dot(matrix[:, i * 256 : (i + 1) * 256], choice)
                    out[:, at + i * 128 : at + (i + 1) * 128] = columns.astype(BF16)
            at += half


def pack_mix_kernel(half, core_ref, mine, other, emit, mix):
    rows = emit.shape[0]
    core = core_ref[0]
    for i, (own, its) in enumerate(((mine, other), (other, mine))):
        here = pl.ds(i * rows, rows)
        mix[here, : 3 * half] = jnp.where(core == 0, own[:, : 3 * half], its[:, : 3 * half])
        mix[here, 3 * half :] = emit[:, i * half : (i + 1) * half]


def pack_ffn_kernel(half, spans, core_ref, mine, other, payload, ffn):
    rows = mine.shape[0]
    core = core_ref[0]
    breadth = payload.shape[1]
    last = 2 * spans * rows
    for i, (own, its) in enumerate(((mine, other), (other, mine))):
        pick = lambda start, size: jnp.where(
            core == 0, own[:, start : start + size], its[:, start : start + size]
        )
        for j in range(spans):
            ffn[pl.ds((2 * j + i) * rows, rows), :] = pick(3 * half + j * breadth, breadth)
        ffn[pl.ds(last + payload.shape[0], rows), pl.ds(i * half, half)] = pick(3 * half + spans * breadth, half)
    ffn[pl.ds(last, payload.shape[0]), :] = payload[...]


def stack_kernel(*refs):
    for i, piece in enumerate(refs[:-1]):
        for device in range(refs[-1].shape[0]):
            refs[-1][device, i : i + 1, :] = piece[...]


def split_kernel(rows, pieces, core_ref, block, mine, other):
    core = core_ref[0]
    at = 0
    for low_at, high_at, size in pieces:
        low, high = (block[row : row + rows, start : start + size] for row, start in (low_at, high_at))
        mine[:, at : at + size] = jnp.where(core == 0, low, high)
        other[:, at : at + size] = jnp.where(core == 0, high, low)
        at += size


def join_kernel(widths, core_ref, mine, other, *outs):
    core = core_ref[0]
    rows = mine.shape[0]
    at = 0
    for width, out in zip(widths, outs):
        half = out.shape[1] // 2
        low = jnp.where(core == 0, mine[:, at : at + half], other[:, at : at + half])
        high = jnp.where(core == 0, other[:, at : at + half], mine[:, at : at + half])
        if width == half:
            out[:, :half] = low
            out[:, half:] = high
        elif width == 128:
            for i in range(half // 128):
                out[:, i * 256 : i * 256 + 128] = low[:, i * 128 : (i + 1) * 128]
                out[:, i * 256 + 128 : (i + 1) * 256] = high[:, i * 128 : (i + 1) * 128]
        else:
            for i in range(half // 128):
                total = jnp.zeros((rows, 256), F32)
                for number, part in enumerate((low, high)):
                    rest = part[:, i * 128 : (i + 1) * 128]
                    for _ in range(3):
                        piece = rest.astype(BF16)
                        total += dot_back(piece, picked(width, number))
                        rest = rest - piece.astype(F32)
                out[:, i * 256 : (i + 1) * 256] = total
        at += half


def whole_call(kernel, shapes, scalar, operands):
    return run(
        kernel,
        grid=(1,),
        out_shape=shapes,
        in_specs=[pl.BlockSpec(memory_space=pltpu.SMEM)] + [whole_block(operand.shape) for operand in operands],
        out_specs=jax.tree.map(lambda out: whole_block(out.shape), shapes),
        compiler_params=pltpu.CompilerParams(vmem_limit_bytes=16 << 20),
    )(scalar.astype(jnp.int32).reshape(1), *operands)


def sum_axis(block, axis, place):
    count = lax.axis_size(axis)
    me = lax.axis_index(axis)

    def part(step):
        return lax.dynamic_index_in_dim(block, lax.rem(me + step, count), place, keepdims=False)

    total = part(1)
    for step in range(2, count + 1):
        moved = lax.ppermute(total.astype(BF16), axis, ring(count, -1))
        total = moved.astype(F32) + part(step).astype(F32)
    return total


def sum_along_z(block):
    return lax.psum_scatter(block.astype(BF16), "z", scatter_dimension=0).astype(F32)


def scatter_rings(grads, views):
    sizes = tuple(lax.axis_size(axis) for axis in CHIPS)
    sums = []
    for grad in grads:
        block = grad.reshape(sizes + grad.shape[1:])
        sums.append(sum_along_z(sum_axis(sum_axis(block, "x", 1), "y", 1)))
    return sums


def dot(left, right):
    return jnp.dot(left, right, preferred_element_type=F32)


def dot_back(grad, weight):
    return lax.dot_general(grad, weight, (((1,), (1,)), ((), ())), preferred_element_type=F32)


def outer(left, right):
    return lax.dot_general(left, right, (((0,), (0,)), ((), ())), preferred_element_type=F32)


def norm_parts(rows):
    center = jnp.mean(rows, axis=-1, keepdims=True)
    deviation = rows - center
    variance = jnp.mean(deviation * deviation, axis=-1, keepdims=True)
    inverse = lax.rsqrt(variance + EPSILON)
    return deviation * inverse, inverse


def last_row(rows):
    return lax.broadcasted_iota(jnp.int32, rows.shape, 0) == rows.shape[0] - 1


def first_row(rows):
    return lax.broadcasted_iota(jnp.int32, rows.shape, 0) == 0


def both_kernel(core_ref, *refs):
    count = len(refs) // 3
    for i in range(count):
        refs[2 * count + i][...] = jnp.where(core_ref[0] == pl.program_id(0), refs[2 * i][...], refs[2 * i + 1][...])


def both_groups(core, *pairs):
    rows, breadth = pairs[0][0].shape
    return run(
        both_kernel,
        grid=(2,),
        in_specs=[pl.BlockSpec(memory_space=pltpu.SMEM)]
        + [pl.BlockSpec((rows, breadth), lambda g: (0, 0))] * (2 * len(pairs)),
        out_specs=[pl.BlockSpec((rows, breadth), lambda g: (g, 0))] * len(pairs),
        out_shape=[jax.ShapeDtypeStruct((2 * rows, breadth), pair[0].dtype) for pair in pairs],
        compiler_params=pltpu.CompilerParams(vmem_limit_bytes=16 << 20),
    )(core.astype(jnp.int32).reshape(1), *(part for pair in pairs for part in pair))


def norm_mix_kernel(terms, behind, gain, bias, shares, *refs):
    rows = terms[0][...].astype(F32)
    for term in terms[1:]:
        rows = rows + term[...]
    outs = list(refs)
    if len(terms) > 1:
        outs.pop(0)[...] = rows
    zhat, inverse = norm_parts(rows)
    outs.pop(0)[...] = zhat
    outs.pop(0)[...] = inverse
    normed = zhat * gain[...] + bias[...]
    group = pl.program_id(0)
    before = jnp.where(group == 0, behind[:1, :], behind[1:, :])
    step = normed - jnp.where(first_row(normed), before, shift_rows(normed, 1))
    for i, out in enumerate(outs):
        out[...] = (normed - step * (1.0 - shares[i : i + 1, :])).astype(BF16)


def norm_mix(terms, behind, gain, bias, shares):
    rows, breadth = terms[0].shape
    block = pl.BlockSpec((rows // 2, breadth), lambda g: (g, 0))
    whole = lambda element: pl.BlockSpec(element.shape, lambda g: (0, 0))
    shape = lambda kind: jax.ShapeDtypeStruct((rows, breadth), kind)
    wide = [shape(F32)] * (2 if len(terms) > 1 else 1)

    def body(*refs):
        norm_mix_kernel(refs[: len(terms)], *refs[len(terms) :])

    return run(
        body,
        grid=(2,),
        in_specs=[block] * len(terms) + [whole(element) for element in (behind, gain, bias, shares)],
        out_specs=[block] * len(wide)
        + [pl.BlockSpec((rows // 2, 1), lambda g: (g, 0))]
        + [block] * shares.shape[0],
        out_shape=wide + [jax.ShapeDtypeStruct((rows, 1), F32)] + [shape(BF16)] * shares.shape[0],
        compiler_params=pltpu.CompilerParams(vmem_limit_bytes=24 << 20),
    )(*terms, behind, gain, bias, shares)


def norm_back_kernel(count, table, *refs):
    parts = refs[:count]
    came, zhat_ref, inverse_ref, gain, base = refs[count : count + 5]
    outs = refs[count + 5 :]
    grad = parts[0][...]
    for part in parts[1:]:
        grad = grad + part[...]
    group = pl.program_id(0)
    grad = grad + jnp.where(last_row(grad), jnp.where(group == 0, came[:1, :], came[-1:, :]), 0.0)
    zhat = zhat_ref[...]
    scaled = grad * gain[...]
    middle = jnp.mean(scaled, axis=-1, keepdims=True)
    slope = jnp.mean(scaled * zhat, axis=-1, keepdims=True)
    total = base[...].astype(F32) + inverse_ref[...] * (scaled - middle - zhat * slope)
    for out in outs[:-1]:
        out[...] = total.astype(out.dtype)
    outs[-1][0, :1, :] = jnp.sum(grad * zhat, axis=0, keepdims=True)
    outs[-1][0, 1:, :] = jnp.sum(grad, axis=0, keepdims=True)


def norm_back(core, parts, came, zhat, inverse, gain, base, kinds, own):
    breadth = zhat.shape[1]
    rows = zhat.shape[0] // 2
    groups = 1 if own else 2
    pick = lambda width: pl.BlockSpec((rows, width), lambda g, table: (table[0] if own else g, 0))
    block = pl.BlockSpec((rows, breadth), lambda g, table: (g, 0))
    whole = lambda element: pl.BlockSpec(element.shape, lambda g, table: (0, 0))
    return run(
        partial(norm_back_kernel, len(parts)),
        grid_spec=dict(
            num_scalar_prefetch=1,
            grid=(groups,),
            in_specs=[block] * len(parts)
            + [whole(came), pick(breadth), pick(1), whole(gain), pick(breadth)],
            out_specs=[block] * len(kinds) + [pl.BlockSpec((1, 2, breadth), lambda g, table: (g, 0, 0))],
        ),
        out_shape=[jax.ShapeDtypeStruct((groups * rows, breadth), kind) for kind in kinds]
        + [jax.ShapeDtypeStruct((groups, 2, breadth), F32)],
        compiler_params=pltpu.CompilerParams(vmem_limit_bytes=24 << 20),
    )(core.astype(jnp.int32).reshape(1), *parts, came, zhat, inverse, gain, base)


def output_kernel(core_ref, part, swapped, gate_own, gate_other, cot_ref, middle, out, d_value, d_gate):
    core = core_ref[0]
    half = gate_own.shape[1]
    value = part[...] + swapped[...]
    cot = cot_ref[...].astype(F32)
    own, other = gate_own[...], gate_other[...]
    for i in range(2):
        gate = jnp.where(core == i, own, other)
        here = pl.ds(i * half, half)
        out[:, here] = (middle[:, here] + gate * value[:, i * half : (i + 1) * half]).astype(BF16)
        d_value[:, here] = (cot[:, i * half : (i + 1) * half] * gate).astype(BF16)
    mine = lambda rows: jnp.where(core == 0, rows[:, :half], rows[:, half:])
    d_gate[...] = (mine(cot) * mine(value) * own * (1.0 - own)).astype(BF16)


def output(core, part, swapped, gate_own, gate_other, cot, middle):
    rows, breadth = part.shape
    block = lambda width: pl.BlockSpec((rows // 2, width), lambda g: (g, 0))
    half = breadth // 2
    return run(
        output_kernel,
        grid=(2,),
        in_specs=[pl.BlockSpec(memory_space=pltpu.SMEM)]
        + [block(width) for width in (breadth, breadth, half, half, breadth, breadth)],
        out_specs=[block(breadth), block(breadth), block(half)],
        out_shape=[jax.ShapeDtypeStruct((rows, width), BF16) for width in (breadth, breadth, half)],
        compiler_params=pltpu.CompilerParams(vmem_limit_bytes=20 << 20),
    )(core.astype(jnp.int32).reshape(1), part, swapped, gate_own, gate_other, cot, middle)


def shift_rows(rows, distance):
    return pltpu.roll(rows, distance % rows.shape[0], 0)


def fade_tables(rate, reverse):
    breadth = rate.shape[-1]
    place = lax.broadcasted_iota(jnp.int32, (TILE, breadth), 0)
    if reverse:
        place = TILE - 1 - place
    steps = []
    distance = 1
    while distance < TILE:
        factor = jnp.where(place >= distance, jnp.exp(-rate * float(distance)), 0.0)
        steps.append((distance, factor))
        distance *= 2
    passed = jnp.exp(-rate * place.astype(F32))
    before = (place >= 1).astype(F32)
    return steps, passed, before


def scan_tile(terms, steps, reverse):
    for distance, factor in steps:
        terms = terms + factor * shift_rows(terms, -distance if reverse else distance)
    return terms


def wkv_kernel(
    groups, key_ref, value_ref, recept_ref, rate_ref, bonus_ref, num_ref, den_ref, emit_ref,
    attended_ref, gated_ref, prior_num_ref, prior_den_ref,
):
    rows = key_ref.shape[0] // groups
    rate = rate_ref[...]
    bonus = bonus_ref[...]
    steps, passed, before = fade_tables(rate, False)
    tile_fade = jnp.exp(-rate * float(TILE))

    def body(index, carry):
        states = []
        for group in range(groups):
            num, den = carry[2 * group], carry[2 * group + 1]
            at = pl.ds(pl.multiple_of(group * rows + index * TILE, TILE), TILE)
            grown = jnp.exp(key_ref[at, :].astype(F32))
            product = grown * value_ref[at, :].astype(F32)
            inner_num = scan_tile(product, steps, False)
            inner_den = scan_tile(grown, steps, False)
            prior_num = shift_rows(inner_num, 1) * before + passed * num
            prior_den = shift_rows(inner_den, 1) * before + passed * den
            prior_num_ref[at, :] = prior_num
            prior_den_ref[at, :] = prior_den
            wkv = (prior_num + bonus * product) / (prior_den + bonus * grown)
            gated_ref[at, :] = (recept_ref[at, :] * wkv.astype(BF16).astype(F32)).astype(BF16)
            states.append(inner_num[TILE - 1 :, :] + tile_fade * num)
            states.append(inner_den[TILE - 1 :, :] + tile_fade * den)
        return tuple(states)

    start = []
    for group in range(groups):
        start += [num_ref[group : group + 1, :], den_ref[group : group + 1, :]]
    lax.fori_loop(0, rows // TILE, body, tuple(start))
    attended_ref[...] = dot(gated_ref[...], emit_ref[...])


def wkv_back_kernel(
    groups, key_ref, value_ref, prior_num_ref, prior_den_ref, weighted_ref, rate_ref, bonus_ref,
    num_ref, den_ref, dkey_ref, dvalue_ref, decay_ref, first_ref,
):
    rows = key_ref.shape[0] // groups
    rate = rate_ref[...]
    bonus = bonus_ref[...]
    steps, passed, before = fade_tables(rate, True)
    tile_fade = jnp.exp(-rate * float(TILE))
    decay_ref[...] = jnp.zeros_like(decay_ref)
    first_ref[...] = jnp.zeros_like(first_ref)

    def body(step, carry):
        index = rows // TILE - 1 - step
        states = []
        for group in range(groups):
            num, den = carry[2 * group], carry[2 * group + 1]
            at = pl.ds(pl.multiple_of(group * rows + index * TILE, TILE), TILE)
            grown = jnp.exp(key_ref[at, :].astype(F32))
            value = value_ref[at, :].astype(F32)
            prior_num = prior_num_ref[at, :]
            prior_den = prior_den_ref[at, :]
            wkv_den = prior_den + bonus * grown
            wkv = (prior_num + bonus * grown * value) / wkv_den
            grad = weighted_ref[at, :].astype(F32) / wkv_den
            inner_num = scan_tile(grad, steps, True)
            inner_den = scan_tile(-grad * wkv, steps, True)
            lam_num = shift_rows(inner_num, -1) * before + passed * num
            lam_den = shift_rows(inner_den, -1) * before + passed * den
            bonus_grad = bonus * grad
            dvalue_ref[at, :] = (grown * (bonus_grad + lam_num)).astype(BF16)
            direct = bonus_grad * (value - wkv)
            dkey_ref[at, :] = (grown * (direct + lam_num * value + lam_den)).astype(BF16)
            first_ref[...] += grown * direct
            decay_ref[...] += lam_num * prior_num + lam_den * prior_den
            states.append(inner_num[:1, :] + tile_fade * num)
            states.append(inner_den[:1, :] + tile_fade * den)
        return tuple(states)

    start = []
    for group in range(groups):
        start += [num_ref[group : group + 1, :], den_ref[group : group + 1, :]]
    lax.fori_loop(0, rows // TILE, body, tuple(start))


def wkv_start_kernel(
    groups, grad_ref, recept_ref, key_ref, value_ref, prior_num_ref, prior_den_ref, rate_ref, bonus_ref,
    weighted_ref, accept_ref, begin_ref,
):
    rows = key_ref.shape[0] // groups
    rate = rate_ref[...]
    bonus = bonus_ref[...]
    place = lax.broadcasted_iota(jnp.int32, (TILE, rate.shape[-1]), 0).astype(F32)
    tile_fade = jnp.exp(-rate * float(TILE))

    def body(index, carry):
        fade, sums = carry[0], []
        for group in range(groups):
            at = pl.ds(pl.multiple_of(group * rows + index * TILE, TILE), TILE)
            grown = bonus * jnp.exp(key_ref[at, :].astype(F32))
            wkv_den = prior_den_ref[at, :] + grown
            wkv = (prior_num_ref[at, :] + grown * value_ref[at, :].astype(F32)) / wkv_den
            recept = recept_ref[at, :]
            grad = grad_ref[at, :]
            kept = grad * recept
            weighted = kept.astype(BF16)
            weighted_ref[at, :] = weighted
            accept_ref[at, :] = (kept * wkv.astype(BF16).astype(F32) * (1.0 - recept)).astype(BF16)
            faded = fade * (weighted.astype(F32) / wkv_den)
            sums += [carry[1 + 2 * group] + faded, carry[2 + 2 * group] - faded * wkv]
        return (fade * tile_fade, *sums)

    zero = jnp.zeros((TILE, rate.shape[-1]), F32)
    _, *sums = lax.fori_loop(0, rows // TILE, body, (jnp.exp(-rate * place),) + (zero,) * (2 * groups))
    for group in range(groups):
        for i in range(2):
            begin_ref[i, group : group + 1, :] = jnp.sum(sums[2 * group + i], axis=0, keepdims=True)


def keys_kernel(groups, mixed_k, mixed_v, mixed_r, weight_k, weight_v, weight_r, rate, keys, values, recept, ends):
    keys[...] = dot(mixed_k[...], weight_k[...]).astype(BF16)
    values[...] = dot(mixed_v[...], weight_v[...]).astype(BF16)
    recept[...] = jax.nn.sigmoid(dot(mixed_r[...], weight_r[...]))
    rows = keys.shape[0] // groups
    left = (rows - 1 - lax.broadcasted_iota(jnp.int32, (rows, keys.shape[1]), 0)).astype(F32)
    fades = jnp.exp(-rate[...] * left)
    for group in range(groups):
        here = pl.ds(group * rows, rows)
        grown = jnp.exp(keys[here, :].astype(F32)) * fades
        ends[0, group : group + 1, :] = jnp.sum(grown * values[here, :].astype(F32), axis=0, keepdims=True)
        ends[1, group : group + 1, :] = jnp.sum(grown, axis=0, keepdims=True)


def keys_call(mixes, weights, rate):
    rows, breadth = mixes[0].shape
    columns = weights[0].shape[1]
    block = min(256, columns)
    wide = lambda height: pl.BlockSpec((height, block), lambda i: (0, i))
    shape = lambda kind: jax.ShapeDtypeStruct((rows, columns), kind)
    return run(
        partial(keys_kernel, 2),
        grid=(columns // block,),
        in_specs=[whole_block((rows, breadth))] * 3 + [wide(breadth)] * 3 + [wide(1)],
        out_specs=[wide(rows)] * 3 + [pl.BlockSpec((2, 2, block), lambda i: (0, 0, i))],
        out_shape=[shape(BF16), shape(BF16), shape(F32), jax.ShapeDtypeStruct((2, 2, columns), F32)],
        compiler_params=pltpu.CompilerParams(vmem_limit_bytes=24 << 20),
    )(*mixes, *weights, rate)


def wkv_call(kernel, groups, shapes, operands):
    return run(
        partial(kernel, groups),
        out_shape=shapes,
        in_specs=[whole_block(operand.shape) for operand in operands],
        out_specs=[whole_block(out.shape) for out in shapes],
        compiler_params=pltpu.CompilerParams(vmem_limit_bytes=16 << 20),
    )(*operands)


def mix_back_kernel(groups, count, core_ref, *refs):
    grads = refs[:count]
    zhat, behind, gain, bias, shares = refs[count : count + 5]
    *parts, first, sums = refs[count + 5 :]
    rows = zhat.shape[0] // groups
    totals = [0.0] * count
    for group in range(groups):
        here = pl.ds(group * rows, rows)
        normed = zhat[here, :] * gain[...] + bias[...]
        step = normed - jnp.where(first_row(normed), behind[group : group + 1, :], shift_rows(normed, 1))
        direct, shifted = 0.0, 0.0
        for i in range(count):
            grad = grads[i][here, :]
            moved = grad * (1.0 - shares[i : i + 1, :])
            direct += grad - moved
            shifted += moved
            totals[i] += jnp.sum(grad * step, axis=0, keepdims=True)
        first[group : group + 1, :] = shifted[:1, :]
        part = direct + jnp.where(last_row(shifted), 0.0, shift_rows(shifted, -1))
        if len(parts) == 1:
            parts[0][here, :] = part
        else:
            for i in range(2):

                @pl.when((core_ref[0] == group) == (i == 0))
                def _():
                    parts[i][...] = part
    for i in range(count):
        sums[i : i + 1, :] = totals[i]


def mix_back(core, grads, zhat, behind, gain, bias, shares, apart):
    rows, breadth = zhat.shape
    count = len(grads)
    block = min(256, breadth)
    column = lambda height: pl.BlockSpec((height, block), lambda i: (0, i))
    heights = ([rows // 2] * 2 if apart else [rows]) + [2, count]
    return run(
        partial(mix_back_kernel, 2, count),
        grid=(breadth // block,),
        in_specs=[pl.BlockSpec(memory_space=pltpu.SMEM)]
        + [column(rows)] * (count + 1)
        + [column(2), column(1), column(1), column(count)],
        out_specs=[column(height) for height in heights],
        out_shape=[jax.ShapeDtypeStruct((height, breadth), F32) for height in heights],
        compiler_params=pltpu.CompilerParams(vmem_limit_bytes=14 << 20),
    )(core.astype(jnp.int32).reshape(1), *grads, zhat, behind, gain, bias, shares)


def per_device(
    layer_incoming,
    series_extents,
    emitted_adjoint,
    norm1_scaling,
    norm1_offset,
    mixer_lookup_portion,
    mixer_payload_portion,
    mixer_accept_portion,
    temporal_fading_log,
    present_step_reward,
    mixer_lookup_matrix,
    mixer_payload_matrix,
    mixer_accept_matrix,
    mixer_emit_matrix,
    norm2_scaling,
    norm2_offset,
    feedforward_lookup_portion,
    feedforward_accept_portion,
    feedforward_lookup_matrix,
    feedforward_payload_matrix,
    feedforward_accept_matrix,
):
    LAST.clear()
    devices = lax.axis_size(ALL)
    chips = lax.axis_size(CHIPS)
    parts = lax.axis_size(SEQ)
    core = lax.axis_index("c")
    place = lax.axis_index(SEQ)
    rows, breadth = layer_incoming.shape[1:]
    own_rows = mixer_lookup_matrix.shape[0]
    hidden_rows = feedforward_payload_matrix.shape[0]

    half = breadth // 2
    hidden = feedforward_lookup_matrix.shape[1] // 2
    both = lambda own, other: jnp.where(core == 0, jnp.stack([own, other]), jnp.stack([other, own]))
    mine_of = lambda pair: lax.dynamic_index_in_dim(pair, core, 0, keepdims=False)
    other_of = lambda pair: lax.dynamic_index_in_dim(pair, 1 - core, 0, keepdims=False)
    pair_rows = 2 * own_rows
    spans = hidden // breadth
    every = slice(None)
    mix_views = (
        tuple((i, (every, pl.ds(i * half, half)), (every, every)) for i in range(3))
        + tuple(
            (3, (pl.ds(i * own_rows, own_rows), pl.ds(3 * half, half)), (every, pl.ds(i * half, half)))
            for i in range(2)
        ),
        ((pair_rows, half),) * 3 + ((own_rows, breadth),),
        (pair_rows, 4 * half),
    )
    last = spans * pair_rows
    ffn_views = (
        tuple(
            (0, (pl.ds(i * pair_rows, pair_rows), every), (every, pl.ds(i * breadth, breadth)))
            for i in range(spans)
        )
        + ((1, (pl.ds(last, hidden_rows), every), (every, every)),)
        + tuple(
            (2, (pl.ds(last + hidden_rows, own_rows), pl.ds(i * half, half)), (pl.ds(i * own_rows, own_rows), every))
            for i in range(2)
        ),
        ((pair_rows, hidden), (hidden_rows, breadth), (pair_rows, half)),
        (last + hidden_rows + own_rows, breadth),
    )

    rounds = in_rounds()
    table = chip_table() if rounds else None
    split_up = (
        mixer_lookup_matrix, mixer_payload_matrix, mixer_accept_matrix,
        feedforward_lookup_matrix, feedforward_accept_matrix,
    )
    widths = (own_rows, own_rows, own_rows, hidden_rows, half)
    picks = jax.ShapeDtypeStruct((own_rows, 4 * half + hidden), BF16)
    if rounds:
        mine, other = whole_call(partial(pick_kernel, widths), (picks, picks), core, tuple(map(in_hbm, split_up)))
        other = swap(other)
        (mix_block,) = whole_call(
            partial(pack_mix_kernel, half), [jax.ShapeDtypeStruct(mix_views[2], BF16)],
            core, (mine, other, in_hbm(mixer_emit_matrix)),
        )
    else:
        halves = jnp.concatenate(
            [
                matrix.reshape(own_rows, -1, 2, width).transpose(2, 0, 1, 3).reshape(2, own_rows, -1)
                for matrix, width in zip(split_up, widths)
            ],
            axis=-1,
        )
        pair = both(mine_of(halves), swap(other_of(halves))).reshape(pair_rows, -1)
        pair_k = pair[:, 3 * half : 3 * half + hidden]
        pair_r = pair[:, 3 * half + hidden :]
        ffn_block = jnp.concatenate(
            [pair_k[:, i * breadth : (i + 1) * breadth] for i in range(spans)]
            + [feedforward_payload_matrix, jnp.concatenate([pair_r[:own_rows], pair_r[own_rows:]], axis=1)],
            axis=0,
        )
        emit = jnp.concatenate([mixer_emit_matrix[:, :half], mixer_emit_matrix[:, half:]], axis=0)
        mix_block = jnp.concatenate([pair[:, : 3 * half], emit], axis=1)
    Gather, Scatter = (GatherRounds, ScatterRounds) if rounds else (GatherRings, ScatterRings)
    mix_gather = Gather(table, mix_block, mix_views)
    mix_gather.step(0)
    mix_gather.place(-1)
    pieces = (
        norm1_scaling, norm1_offset, mixer_lookup_portion, mixer_payload_portion,
        mixer_accept_portion, norm2_scaling, norm2_offset, feedforward_lookup_portion,
        feedforward_accept_portion, temporal_fading_log, present_step_reward,
    )
    pieces = [piece.reshape(1, own_rows) for piece in pieces]
    vectors = run(
        stack_kernel,
        out_shape=jax.ShapeDtypeStruct((devices, len(pieces), own_rows), BF16),
        in_specs=[whole_block(piece.shape) for piece in pieces],
        out_specs=whole_block((devices, len(pieces), own_rows)),
    )(*pieces)
    mix_gather.step(1)
    if rounds:
        (ffn_block,) = whole_call(
            partial(pack_ffn_kernel, half, spans), [jax.ShapeDtypeStruct(ffn_views[2], BF16)],
            core, (mine, other, in_hbm(feedforward_payload_matrix)),
        )
    ffn_gather = Gather(table, ffn_block, ffn_views)
    ffn_gather.step(0)
    mix_gather.place(0)

    flat = lambda element: element.reshape(2 * rows, -1)
    (inputs,) = both_groups(core, (layer_incoming[0], swap(layer_incoming[0])))
    ends_of = lambda element: element.reshape(2, rows, -1)[:, rows - 1]

    vectors = lax.all_to_all(vectors, ALL, 0, 0, tiled=True)
    vectors = vectors.astype(F32).transpose(1, 0, 2)
    channel = lax.dynamic_index_in_dim(
        vectors[9:].reshape(2, chips, 2, own_rows), core, 2, keepdims=False
    ).reshape(2, 1, -1)
    vectors = vectors[:9].reshape(9, breadth)
    gain1, bias1, shares1, gain2, bias2, shares2 = (
        vectors[start:stop] for start, stop in ((0, 1), (1, 2), (2, 5), (5, 6), (6, 7), (7, 9))
    )
    rate, bonus = jnp.exp(channel[0]), jnp.exp(channel[1])

    begins = jnp.cumsum(series_extents[0]) - series_extents[0]
    starts = jnp.any(jnp.arange(parts)[:, None] * rows == begins[None, :], axis=1)
    joined = jnp.where(starts, 0.0, 1.0).astype(F32)
    joined = both(joined, swap(joined))
    keep = lax.dynamic_index_in_dim(joined, place, 1)[:, :, None]
    index = jnp.arange(parts)
    began = jnp.where((joined == 0.0) & (index[None] <= place), index[None], -1).max(axis=1)
    reach = ((index[None] < place) & (index[None] >= began[:, None])).astype(F32)
    begun = jnp.where((joined == 0.0) & (index[None] > place), index[None], parts).min(axis=1)
    reach_back = ((index[None] > place) & (index[None] < begun[:, None])).astype(F32)

    def entering(ends, reached, distance):
        fades = jnp.exp(-rate[None] * (float(rows) * jnp.maximum(distance, 0).astype(F32))[:, None, None])
        return jnp.sum(ends * (reached.T[:, None, :, None] * fades[:, :, None]), axis=0)

    def spread(ends):
        return lax.all_to_all(
            jnp.broadcast_to(ends[None], (parts,) + ends.shape), SEQ, 0, 0, tiled=True
        )

    def behind_of(normed):
        return along_seq(normed, 1) * keep[:, 0]

    mix_gather.step(2)
    mix_gather.place(1)
    behind1 = behind_of(norm_parts(ends_of(inputs).astype(F32))[0] * gain1 + bias1)
    zhat1, inverse1, mixed_k, mixed_v, mixed_r = norm_mix([inputs], behind1, gain1, bias1, shares1)
    mix_gather.step(3)
    mix_gather.place(2)
    mix_gather.step(4)
    mix_gather.place(3)
    ffn_gather.step(1)
    mix_gather.place(4)
    whole = lambda held: held.reshape(-1, held.shape[-1])
    weight_k, weight_v, weight_r, weight_o = map(whole, mix_gather.held)
    keys, values, recept, ends = keys_call(
        (mixed_k, mixed_v, mixed_r), (weight_k, weight_v, weight_r), rate
    )

    enter = entering(spread(ends), reach, place - 1 - index)
    ffn_gather.place(-1)
    ffn_gather.place(0)
    ffn_gather.step(2)
    ffn_gather.place(1)
    shape = lambda kind: jax.ShapeDtypeStruct((2 * rows, half), kind)
    attended, gated, prior_num, prior_den = wkv_call(
        wkv_kernel, 2,
        (jax.ShapeDtypeStruct((2 * rows, breadth), F32), shape(BF16), shape(F32), shape(F32)),
        (keys, values, recept, rate, bonus, enter[0], enter[1], weight_o),
    )
    swapped = swap(attended)
    ffn_gather.step(3)
    ffn_gather.place(2)
    (cotangent,) = both_groups(core, (emitted_adjoint[0], swap(emitted_adjoint[0])))
    ends2 = ends_of(inputs).astype(F32) + ends_of(attended) + ends_of(swapped)
    behind2 = behind_of(norm_parts(ends2)[0] * gain2 + bias2)
    middle, zhat2, inverse2, ffn_k, ffn_r = norm_mix(
        [inputs, attended, swapped], behind2, gain2, bias2, shares2
    )
    ffn_gather.step(4)
    ffn_gather.place(3)
    ffn_gather.place(4)
    weight_fk, weight_fv, weight_fr = map(whole, ffn_gather.held)
    gate_own = jax.nn.sigmoid(dot(ffn_r, weight_fr))
    gate_other = swap(gate_own)
    pre_hidden = jax.nn.relu(dot(ffn_k, weight_fk))
    hidden_act = jnp.square(pre_hidden).astype(BF16)
    value_part = dot(hidden_act, weight_fv)
    block_output, d_value_out, d_gate_pre = output(
        core, value_part, swap(value_part), gate_own, gate_other, cotangent, middle
    )
    block_output = mine_of(block_output.reshape(2, rows, breadth))

    grad_fv = outer(hidden_act, d_value_out).astype(BF16)
    d_hidden = dot_back(d_value_out, weight_fv)
    d_pre_hidden = (d_hidden * 2.0 * pre_hidden).astype(BF16)
    grad_fk = outer(ffn_k, d_pre_hidden).astype(BF16)
    grad_fr = outer(ffn_r, d_gate_pre).astype(BF16)
    per_chip = lambda grad: grad.reshape(chips, -1, grad.shape[-1])
    ffn_scatter = Scatter(table, [per_chip(grad) for grad in (grad_fk, grad_fv, grad_fr)], ffn_views)
    ffn_scatter.step(0)

    def came_back(first):
        first = first * keep[:, 0]
        pairs = [(2 * i + c, 2 * (i - 1) + 1 - c) for i in range(1, parts) for c in range(2)]
        return along_seq(first, -1) + lax.ppermute(first, SEQ + ("c",), pairs)

    part2, first2, share_grads2 = mix_back(
        core, (dot_back(d_pre_hidden, weight_fk), dot_back(d_gate_pre, weight_fr)),
        zhat2, behind2, gain2, bias2, shares2, False,
    )
    ffn_scatter.step(1)
    d_middle, d_attended, norm_grads2 = norm_back(
        core, (part2, swap(part2)), came_back(first2), zhat2, inverse2, gain2, cotangent, (F32, BF16), False
    )

    grad_o = outer(gated, d_attended).astype(BF16)
    d_gated = dot_back(d_attended, weight_o)
    d_weighted, d_recept_pre, begins_back = wkv_call(
        wkv_start_kernel, 2,
        (shape(BF16), shape(BF16), jax.ShapeDtypeStruct((2, 2, half), F32)),
        (d_gated, recept, keys, values, prior_num, prior_den, rate, bonus),
    )
    ffn_scatter.step(2)
    enter_back = entering(spread(begins_back), reach_back, index - place - 1)
    small = jax.ShapeDtypeStruct((TILE, half), F32)
    d_keys, d_values, decay_sum, first_sum = wkv_call(
        wkv_back_kernel, 2, (shape(BF16), shape(BF16), small, small),
        (keys, values, prior_num, prior_den, d_weighted, rate, bonus, enter_back[0], enter_back[1]),
    )
    grad_decay = -rate * jnp.exp(-rate) * decay_sum.sum(axis=0, keepdims=True)
    grad_first = first_sum.sum(axis=0, keepdims=True)

    ffn_scatter.step(3)
    grad_k = outer(mixed_k, d_keys).astype(BF16)
    grad_v = outer(mixed_v, d_values).astype(BF16)
    grad_r = outer(mixed_r, d_recept_pre).astype(BF16)
    own1, other1, first1, share_grads1 = mix_back(
        core,
        (dot_back(d_keys, weight_k), dot_back(d_values, weight_v), dot_back(d_recept_pre, weight_r)),
        zhat1, behind1, gain1, bias1, shares1, True,
    )
    ffn_scatter.step(4)
    mix_scatter = Scatter(
        table, [per_chip(grad) for grad in (grad_k, grad_v, grad_r, grad_o)], mix_views
    )
    mix_scatter.step(0)
    input_grad, norm_grads1 = norm_back(
        core, (own1, swap(other1)), mine_of(came_back(first1)[:, None]), zhat1, inverse1, gain1, d_middle,
        (F32,), True,
    )
    mix_scatter.step(1)

    def by_channel(grad):
        whole = jnp.zeros((chips, 2, own_rows), F32)
        return lax.dynamic_update_index_in_dim(
            whole, grad.reshape(chips, own_rows), core, 1
        ).reshape(1, breadth)

    grads = jnp.concatenate(
        [
            norm_grads1[0], share_grads1, by_channel(grad_decay), by_channel(grad_first),
            mine_of(norm_grads2), share_grads2,
        ],
        axis=0,
    )
    grads = grads.reshape(11, devices, own_rows).swapaxes(0, 1)
    grads = lax.all_to_all(grads, ALL, 0, 0, tiled=True).sum(axis=0)

    def joined_sums(block, split, widths):
        size = sum(size for _, _, size in split)
        piece = jax.ShapeDtypeStruct((own_rows, size), F32)
        if rounds:
            mine, other = whole_call(partial(split_kernel, own_rows, split), (piece, piece), core, (block,))
            other = swap(other)
            yield
            outs = [jax.ShapeDtypeStruct((own_rows, 2 * size), F32) for size, _ in widths]
            yield whole_call(partial(join_kernel, [width for _, width in widths]), outs, core, (mine, other))
            return
        pair = jnp.stack(
            [
                jnp.concatenate(
                    [block[at[0] : at[0] + own_rows, at[1] : at[1] + size] for at, size in pieces], axis=1
                )
                for pieces in ([(low, size) for low, _, size in split], [(high, size) for _, high, size in split])
            ]
        )
        mine, other = mine_of(pair), swap(other_of(pair))
        low, high = jnp.where(core == 0, mine, other), jnp.where(core == 0, other, mine)
        outs, at = [], 0
        yield
        for size, width in widths:
            pieces = [piece[:, at : at + size].reshape(own_rows, -1, 1, width) for piece in (low, high)]
            outs.append(jnp.concatenate(pieces, axis=2).reshape(own_rows, 2 * size))
            at += size
        yield outs

    ffn_sum = ffn_scatter.result()
    ffn_joined = joined_sums(
        ffn_sum,
        [((i * pair_rows, 0), (i * pair_rows + own_rows, 0), breadth) for i in range(spans)]
        + [((last + hidden_rows, 0), (last + hidden_rows, half), half)],
        [(hidden, hidden_rows), (half, half)],
    )
    next(ffn_joined)
    sum_fv = ffn_sum[last : last + hidden_rows]
    mix_scatter.step(2)
    sum_fk, sum_fr = next(ffn_joined)
    mix_scatter.step(3)
    mix_scatter.step(4)
    mix_sum = mix_scatter.result()
    mix_joined = joined_sums(mix_sum, [((0, 0), (own_rows, 0), 3 * half)], [(half, own_rows)] * 3)
    next(mix_joined)
    sum_k, sum_v, sum_r = next(mix_joined)
    emit_sum = mix_sum[:, 3 * half :]
    sum_o = jnp.concatenate([emit_sum[:own_rows], emit_sum[own_rows:]], axis=1)

    return (
        block_output[None],
        input_grad[None],
        *(grads[i] for i in range(7)),
        sum_k,
        sum_v,
        sum_r,
        sum_o,
        *(grads[i] for i in range(7, 11)),
        sum_fk,
        sum_fv,
        sum_fr,
    )


def solution(mesh):
    parts, groups = mesh.shape["seq"], mesh.shape["rep"]
    width = groups // 2
    fine = Mesh(mesh.devices.reshape(parts // width, width, width, 2), ALL)
    tokens = P(("y", "c"), SEQ, None)
    vector = P(ALL)
    matrix = P(ALL, None)
    return jax.shard_map(
        per_device,
        mesh=fine,
        in_specs=(
            (tokens, P(("y", "c"), None), tokens)
            + (vector,) * 7
            + (matrix,) * 4
            + (vector,) * 4
            + (matrix,) * 3
        ),
        out_specs=(
            (tokens, tokens) + (vector,) * 7 + (matrix,) * 4 + (vector,) * 4 + (matrix,) * 3
        ),
        check_vma=False,
    )
```

```python
from functools import partial

import jax
import jax.numpy as jnp
from jax import lax
from jax.experimental import pallas as pl
from jax.experimental.pallas import tpu as pltpu
from jax.sharding import Mesh, PartitionSpec as P

EPSILON = 1e-05
F32 = jnp.float32
BF16 = jnp.bfloat16
CHIPS = ("z", "x", "y")
SEQ = ("z", "x")
ALL = ("z", "x", "y", "c")
TILE = 16
FREE = pl.CostEstimate(flops=0, bytes_accessed=0, transcendentals=0)


def ring(count, step=1):
    return [(i, (i + step) % count) for i in range(count)]


def swap(block):
    return lax.ppermute(block, "c", ring(2))


def along_seq(block, step):
    count = lax.axis_size(SEQ)
    pairs = [(i, i + step) for i in range(count) if 0 <= i + step < count]
    return lax.ppermute(block, SEQ, pairs)


ROUNDS = (
    (("z", (0, 0, 0), (1, 0, 0)), ("y", (0, 0, 0), (0, 0, 1)), ("x", (0, 0, 0), (0, 1, 0))),
    (("z", (1, 0, 0), (2, 0, 0)), ("y", (1, 0, 0), (1, 0, 1)), ("x", (0, 0, 1), (0, 1, 1))),
    (("z", (2, 0, 0), (3, 0, 0)), ("y", (2, 0, 0), (2, 0, 1)), ("x", (1, 0, 0), (1, 1, 0))),
    (("z", (0, 1, 1), (1, 1, 1)), ("y", (3, 0, 0), (3, 0, 1)), ("x", (3, 0, 0), (3, 1, 0))),
    (("z", (1, 1, 1), (2, 1, 1)), ("y", (3, 1, 0), (3, 1, 1)), ("x", (2, 0, 0), (2, 1, 0))),
)


def in_rounds():
    return tuple(lax.axis_size(axis) for axis in CHIPS) == (4, 2, 2)


RELATIVES = tuple((z, x, y) for z in range(4) for x in range(2) for y in range(2))
ANYWHERE = pl.BlockSpec(memory_space=pl.ANY)


def chip_table():
    whole = jnp.asarray(RELATIVES, jnp.int32)
    total = jnp.zeros((len(RELATIVES),), jnp.int32)
    for i, axis in enumerate(CHIPS):
        count = lax.axis_size(axis)
        total = total * count + lax.rem(lax.axis_index(axis) + (count - whole[:, i]), count)
    return jnp.concatenate([total, lax.axis_index("c")[None]]).astype(jnp.int32)


def whole_block(shape):
    return pl.BlockSpec(shape, lambda *g: (0,) * len(shape))


def in_hbm(array):
    return pltpu.with_memory_space_constraint(array, pltpu.HBM)


LAST = []
HELD = []


def where_it_is(array):
    kinds = [kind for held, kind in HELD if held is array]
    return pltpu.with_memory_space_constraint(array, kinds[0]) if kinds else array


def run(
    kernel, *, out_shape, grid=(1,), in_specs=None, out_specs=None, grid_spec=None, hbm=(), vmem=(), **settings
):
    spec = grid_spec or dict(num_scalar_prefetch=0, grid=grid, in_specs=in_specs, out_specs=out_specs)
    spec.setdefault("scratch_shapes", settings.pop("scratch_shapes", ()))
    single = isinstance(out_shape, jax.ShapeDtypeStruct)
    shapes = [out_shape] if single else list(out_shape)
    kinds = [pltpu.HBM if i in hbm else pltpu.VMEM if i in vmem else None for i in range(len(shapes))]
    shapes = [out if kind is None else kind(out.shape, out.dtype) for out, kind in zip(shapes, kinds)]

    def call(*operands):
        marks = [mark for mark in LAST if not any(mark is operand for operand in operands)]
        count = len(operands)
        outputs = count + len(marks) + len(shapes)

        def body(*refs):
            refs[outputs][...] = jnp.zeros_like(refs[outputs])
            kernel(*refs[:count], *refs[count + len(marks) : outputs], *refs[outputs + 1 :])

        out_specs = [spec["out_specs"]] if single else list(spec["out_specs"])
        *outs, token = pl.pallas_call(
            body,
            grid_spec=pltpu.PrefetchScalarGridSpec(
                **{
                    **spec,
                    "in_specs": list(spec["in_specs"]) + [ANYWHERE] * len(marks),
                    "out_specs": out_specs + [whole_block((8, 128))],
                }
            ),
            out_shape=shapes + [pltpu.HBM((8, 128), F32)],
            cost_estimate=FREE,
            **settings,
        )(*map(where_it_is, operands), *map(where_it_is, marks))
        LAST[:] = [token]
        HELD.extend((out, kind) for out, kind in zip(outs + [token], kinds + [pltpu.HBM]) if kind is not None)
        return outs[0] if single else outs

    return call


def hold_kernel(*refs):
    pass


def hold(*arrays, kind=None):
    return run(
        hold_kernel,
        out_shape=[jax.ShapeDtypeStruct(array.shape, array.dtype) for array in arrays],
        vmem=range(len(arrays)) if kind else (),
        in_specs=[ANYWHERE] * len(arrays),
        out_specs=[ANYWHERE] * len(arrays),
        input_output_aliases={i: i for i in range(len(arrays))},
    )(*(pltpu.with_memory_space_constraint(array, kind) if kind else array for array in arrays))


def wait_for(*arrays):
    LAST.extend(arrays)
    run(hold_kernel, out_shape=[], in_specs=[], out_specs=[])()


def place_kernel(first, views, aliased, table_ref, *refs):
    blocks = refs[: len(first)]
    outs = refs[len(first) + aliased : -1]
    copies = []
    for i, block in enumerate(blocks):
        for number, (out, source, target) in enumerate(views[0]):
            copies.append(
                pltpu.make_async_copy(
                    block.at[source],
                    outs[out].at[(table_ref[first[i]],) + target],
                    refs[-1].at[i, number],
                )
            )
    for copy in copies:
        copy.start()
    for copy in copies:
        copy.wait()


def place_blocks(table, held, blocks, relatives, views):
    moves, shapes, _ = views
    chips = lax.axis_size(CHIPS)
    first = [RELATIVES.index(relative) for relative in relatives]
    operands = [table, *blocks]
    aliases = {}
    if held is not None:
        aliases = {len(operands) + i: i for i in range(len(shapes))}
        operands += held
    hbm = pl.BlockSpec(memory_space=pltpu.HBM)
    return run(
        partial(place_kernel, first, views, len(aliases)),
        grid=(1,),
        in_specs=[pl.BlockSpec(memory_space=pltpu.SMEM)]
        + [whole_block(block.shape) for block in blocks]
        + [hbm] * len(aliases),
        out_specs=[hbm] * len(shapes),
        out_shape=[jax.ShapeDtypeStruct((chips,) + shape, BF16) for shape in shapes],
        scratch_shapes=[pltpu.SemaphoreType.DMA((len(blocks), len(moves)))],
        input_output_aliases=aliases,
    )(*operands)


class GatherRounds:
    def __init__(self, table, block, views):
        self.table, self.views = table, views
        self.have = {(0, 0, 0): block}
        self.held, self.due = None, []

    def place(self, number):
        names = [(0, 0, 0)] if number < 0 else [received for _, _, received in ROUNDS[number]]
        blocks = [self.have[name] for name in names]
        self.held = place_blocks(self.table, self.held, blocks, names, self.views)

    def step(self, number):
        names = list({sent: None for _, sent, _ in ROUNDS[number]})
        LAST.extend(array for array in self.due if not any(array is self.have[name] for name in names))
        self.have.update(zip(names, hold(*(self.have[name] for name in names), kind=pltpu.VMEM)))
        for axis, sent, received in ROUNDS[number]:
            self.have[received] = lax.ppermute(self.have[sent], axis, ring(lax.axis_size(axis)))
        self.due = [self.have[received] for _, _, received in ROUNDS[number]]

    def last_blocks(self):
        names = [received for _, _, received in ROUNDS[-1]]
        return [RELATIVES.index(name) for name in names], [self.have[name] for name in names]


class GatherRings:
    def __init__(self, table, block, views):
        self.held = gather_rings(block, views)

    def place(self, number):
        pass

    def step(self, number):
        pass

    def last_blocks(self):
        return [], []


def gather_rings(block, views):
    have = []
    shape = block.shape
    for axis in CHIPS:
        count = lax.axis_size(axis)
        me = lax.axis_index(axis)
        have.append(axis)
        place = len(have) - 1
        whole = jnp.zeros(block.shape[:place] + (count,) + block.shape[place:], block.dtype)
        piece = block
        for step in range(count):
            if step:
                piece = lax.ppermute(piece, axis, ring(count))
            whole = lax.dynamic_update_index_in_dim(whole, piece, lax.rem(me - step + count, count), place)
        block = whole
    block = block.reshape((-1,) + shape)
    held = [jnp.zeros(block.shape[:1] + view, block.dtype) for view in views[1]]
    for out, source, target in views[0]:
        held[out] = held[out].at[(slice(None),) + target].set(block[(slice(None),) + source])
    return held


def sum_kernel(counts, views, table_ref, *refs):
    arrays = len(views[1])
    wanted = len(counts)
    grads = refs[: wanted * arrays]
    received = refs[wanted * arrays : wanted * arrays + sum(counts)]
    outs = refs[wanted * arrays + sum(counts) :]
    at = 0
    for i, count in enumerate(counts):
        for out, source, target in views[0]:
            total = grads[i * arrays + out][(0,) + target].astype(F32)
            for j in range(at, at + count):
                total += received[j][source].astype(F32)
            outs[i][source] = total.astype(outs[i].dtype)
        at += count


def sum_blocks(table, grads, relatives, received, views, kind=BF16):
    _, shapes, block_shape = views
    first = [RELATIVES.index(relative) for relative in relatives]
    counts = [len(blocks) for blocks in received]
    flat = [block for blocks in received for block in blocks]

    def pick(i, shape):
        zeros = (0,) * len(shape)
        return pl.BlockSpec((1,) + shape, lambda g, table: (table[first[i]],) + zeros)

    whole = whole_block(block_shape)
    return run(
        partial(sum_kernel, counts, views),
        grid_spec=dict(
            num_scalar_prefetch=1,
            grid=(1,),
            in_specs=[pick(i, shape) for i in range(len(relatives)) for shape in shapes] + [whole] * len(flat),
            out_specs=[whole] * len(relatives),
        ),
        out_shape=[jax.ShapeDtypeStruct(block_shape, kind) for _ in relatives],
        compiler_params=pltpu.CompilerParams(vmem_limit_bytes=16 << 20),
    )(table, *(list(grads) * len(relatives)), *flat)


def finish_kernel(views, count, pieces, wholes, table_ref, *refs):
    grads, received = refs[: len(views[1])], refs[len(views[1]) : len(views[1]) + count]
    mine, other, *outs, total_ref = refs[len(views[1]) + count :]
    for out, source, target in views[0]:
        total = grads[out][(0,) + target].astype(F32)
        for block in received:
            total += block[source].astype(F32)
        total_ref[source] = total
    core = table_ref[len(RELATIVES)]
    rows = mine.shape[0]
    at = 0
    for start, size in pieces:
        low, high = total_ref[:rows, start : start + size], total_ref[rows:, start : start + size]
        here = pl.ds(at, size)
        mine[:, here] = jnp.where(core == 0, low, high)
        other[:, here] = jnp.where(core == 0, high, low)
        at += size
    for out, (tall, parts) in zip(outs, wholes):
        at = 0
        for place in parts:
            size = place[0].size if tall else place[1].size
            out[(pl.ds(at, size), slice(None)) if tall else (slice(None), pl.ds(at, size))] = total_ref[place]
            at += size


class ScatterRounds:
    def __init__(self, table, grads, views):
        self.table, self.views = table, views
        self.grads = [in_hbm(grad) for grad in grads]
        self.arrived, self.made, self.due = {}, {}, []

    def make(self, *names):
        came = [self.arrived.pop(name, []) for name in names]
        self.made.update(zip(names, sum_blocks(self.table, self.grads, names, came, self.views)))

    def step(self, number, others=()):
        moves = ROUNDS[len(ROUNDS) - 1 - number]
        LAST.extend(self.due + list(others))
        self.make(*(sent for _, _, sent in moves))
        self.due = []
        for axis, target, sent in moves:
            self.due.append(lax.ppermute(self.made[sent], axis, ring(lax.axis_size(axis), -1)))
            self.arrived.setdefault(target, []).append(self.due[-1])

    def result(self):
        own = (0, 0, 0)
        return sum_blocks(self.table, self.grads, [own], [self.arrived.pop(own)], self.views, kind=F32)[0]

    def finish(self, core, pieces, wholes):
        own = (0, 0, 0)
        came = self.arrived.pop(own)
        rows = self.views[2][0] // 2
        shapes = [(rows, sum(size for _, size in pieces))] * 2 + [
            (sum(r.size for r, _ in parts), parts[0][1].size) if tall else (parts[0][0].size, sum(c.size for _, c in parts))
            for tall, parts in wholes
        ]
        blocks = [
            pl.BlockSpec((1,) + shape, lambda g, table: (table[0],) + (0,) * len(shape)) for shape in self.views[1]
        ]
        return run(
            partial(finish_kernel, self.views, len(came), pieces, wholes),
            grid_spec=dict(
                num_scalar_prefetch=1,
                grid=(1,),
                in_specs=blocks + [whole_block(block.shape) for block in came],
                out_specs=[whole_block(shape) for shape in shapes],
                scratch_shapes=[pltpu.VMEM(self.views[2], F32)],
            ),
            out_shape=[jax.ShapeDtypeStruct(shape, F32) for shape in shapes],
            compiler_params=pltpu.CompilerParams(vmem_limit_bytes=16 << 20),
        )(self.table, *self.grads, *came)


class ScatterRings:
    def __init__(self, table, grads, views):
        self.sums = scatter_rings(grads, views)
        self.views = views

    def make(self, *names):
        pass

    def step(self, number, others=()):
        pass

    def result(self):
        moves, _, block_shape = self.views
        block = jnp.zeros(block_shape, F32)
        for out, source, target in moves:
            block = block.at[source].set(self.sums[out][target])
        return block


def picked(width, core):
    source = lax.broadcasted_iota(jnp.int32, (256, 128), 0)
    target = lax.broadcasted_iota(jnp.int32, (256, 128), 1)
    wanted = (target // width) * (2 * width) + core * width + target % width
    return jnp.where(source == wanted, 1.0, 0.0).astype(BF16)


def pick_kernel(widths, core_ref, *refs):
    matrices, outs = refs[: len(widths)], refs[len(widths) :]
    core = core_ref[0]
    for out, wanted in zip(outs, (core, 1 - core)):
        at = 0
        for width, matrix in zip(widths, matrices):
            half = matrix.shape[1] // 2
            if width == half:
                out[:, at : at + half] = jnp.where(wanted == 0, matrix[:, :half], matrix[:, half:])
            else:
                choice = picked(width, wanted)
                for i in range(half // 128):
                    columns = dot(matrix[:, i * 256 : (i + 1) * 256], choice)
                    out[:, at + i * 128 : at + (i + 1) * 128] = columns.astype(BF16)
            at += half


def pack_kernel(half, core_ref, mine, other, emit, payload, block):
    rows, breadth = emit.shape
    core = core_ref[0]
    split = 3 * half
    last = half + mine.shape[1]
    for i, (own, its) in enumerate(((mine, other), (other, mine))):
        here = pl.ds(i * rows, rows)
        block[here, :split] = jnp.where(core == 0, own[:, :split], its[:, :split])
        block[here, split : split + half] = emit[:, i * half : (i + 1) * half]
        block[here, split + half : last] = jnp.where(core == 0, own[:, split:], its[:, split:])
    height = 2 * rows
    for i in range(payload.shape[0] // height):
        block[:, last + i * breadth : last + (i + 1) * breadth] = payload[i * height : (i + 1) * height, :]


def stack_kernel(*refs):
    for i, piece in enumerate(refs[:-1]):
        for device in range(refs[-1].shape[0]):
            refs[-1][device, i : i + 1, :] = piece[...]


def join_kernel(widths, core_ref, mine, other, *outs):
    core = core_ref[0]
    rows = mine.shape[0]
    at = 0
    for width, out in zip(widths, outs):
        half = out.shape[1] // 2
        low = jnp.where(core == 0, mine[:, at : at + half], other[:, at : at + half])
        high = jnp.where(core == 0, other[:, at : at + half], mine[:, at : at + half])
        if width == half:
            out[:, :half] = low
            out[:, half:] = high
        elif width == 128:
            for i in range(half // 128):
                out[:, i * 256 : i * 256 + 128] = low[:, i * 128 : (i + 1) * 128]
                out[:, i * 256 + 128 : (i + 1) * 256] = high[:, i * 128 : (i + 1) * 128]
        else:
            for i in range(half // 128):
                total = jnp.zeros((rows, 256), F32)
                for number, part in enumerate((low, high)):
                    rest = part[:, i * 128 : (i + 1) * 128]
                    for _ in range(3):
                        piece = rest.astype(BF16)
                        total += dot_back(piece, picked(width, number))
                        rest = rest - piece.astype(F32)
                out[:, i * 256 : (i + 1) * 256] = total
        at += half


def whole_call(kernel, shapes, scalar, operands, hbm=()):
    return run(
        kernel,
        grid=(1,),
        out_shape=shapes,
        in_specs=[pl.BlockSpec(memory_space=pltpu.SMEM)] + [whole_block(operand.shape) for operand in operands],
        out_specs=[whole_block(out.shape) for out in shapes],
        hbm=hbm,
        compiler_params=pltpu.CompilerParams(vmem_limit_bytes=16 << 20),
    )(scalar.astype(jnp.int32).reshape(1), *operands)


def sum_axis(block, axis, place):
    count = lax.axis_size(axis)
    me = lax.axis_index(axis)

    def part(step):
        return lax.dynamic_index_in_dim(block, lax.rem(me + step, count), place, keepdims=False)

    total = part(1)
    for step in range(2, count + 1):
        moved = lax.ppermute(total.astype(BF16), axis, ring(count, -1))
        total = moved.astype(F32) + part(step).astype(F32)
    return total


def sum_along_z(block):
    return lax.psum_scatter(block.astype(BF16), "z", scatter_dimension=0).astype(F32)


def scatter_rings(grads, views):
    sizes = tuple(lax.axis_size(axis) for axis in CHIPS)
    sums = []
    for grad in grads:
        block = grad.reshape(sizes + grad.shape[1:])
        sums.append(sum_along_z(sum_axis(sum_axis(block, "x", 1), "y", 1)))
    return sums


def dot(left, right):
    return jnp.dot(left, right, preferred_element_type=F32)


def dot_back(grad, weight):
    return lax.dot_general(grad, weight, (((1,), (1,)), ((), ())), preferred_element_type=F32)


def outer(left, right):
    return lax.dot_general(left, right, (((0,), (0,)), ((), ())), preferred_element_type=F32)


def norm_parts(rows):
    center = jnp.mean(rows, axis=-1, keepdims=True)
    deviation = rows - center
    variance = jnp.mean(deviation * deviation, axis=-1, keepdims=True)
    inverse = lax.rsqrt(variance + EPSILON)
    return deviation * inverse, inverse


def last_row(rows):
    return lax.broadcasted_iota(jnp.int32, rows.shape, 0) == rows.shape[0] - 1


def first_row(rows):
    return lax.broadcasted_iota(jnp.int32, rows.shape, 0) == 0


def both_kernel(core_ref, *refs):
    count = len(refs) // 3
    for i in range(count):
        refs[2 * count + i][...] = jnp.where(core_ref[0] == pl.program_id(0), refs[2 * i][...], refs[2 * i + 1][...])


def both_groups(core, *pairs):
    rows, breadth = pairs[0][0].shape
    return run(
        both_kernel,
        grid=(2,),
        in_specs=[pl.BlockSpec(memory_space=pltpu.SMEM)]
        + [pl.BlockSpec((rows, breadth), lambda g: (0, 0))] * (2 * len(pairs)),
        out_specs=[pl.BlockSpec((rows, breadth), lambda g: (g, 0))] * len(pairs),
        out_shape=[jax.ShapeDtypeStruct((2 * rows, breadth), pair[0].dtype) for pair in pairs],
        hbm=range(len(pairs)),
        compiler_params=pltpu.CompilerParams(vmem_limit_bytes=16 << 20),
    )(core.astype(jnp.int32).reshape(1), *(part for pair in pairs for part in pair))


def vectors_kernel(
    core_ref, norm1, shares1, decay, first, rate_ref, norm2, shares2, out
):
    core = core_ref[0]
    own_rows = out.shape[-1]
    devices = out.shape[0]
    rate = rate_ref[...]
    grad_decay = -rate * jnp.exp(-rate) * jnp.sum(decay[...], axis=0, keepdims=True)
    grad_first = jnp.sum(first[...], axis=0, keepdims=True)
    norms2 = jnp.where(core == 0, norm2[0], norm2[1])
    for device in range(devices):
        here = slice(device * own_rows, (device + 1) * own_rows)
        chip, owner = device // 2, device % 2
        out[device, 0:2, :] = norm1[0][:, here]
        out[device, 2:5, :] = shares1[:, here]
        channels = slice(chip * own_rows, (chip + 1) * own_rows)
        out[device, 5:6, :] = jnp.where(core == owner, grad_decay[:, channels], 0.0)
        out[device, 6:7, :] = jnp.where(core == owner, grad_first[:, channels], 0.0)
        out[device, 7:9, :] = norms2[:, here]
        out[device, 9:11, :] = shares2[:, here]


def vector_sums_kernel(parts, out):
    total = parts[0]
    for i in range(1, parts.shape[0]):
        total = total + parts[i]
    out[...] = total


def outer_kernel(left, right, out):
    out[...] = outer(left[...], right[...]).astype(BF16)


def outer_call(left, right):
    tokens, height = left.shape
    width = right.shape[1]
    block = min(512, width)
    return run(
        outer_kernel,
        grid=(width // block,),
        in_specs=[whole_block(left.shape), pl.BlockSpec((tokens, block), lambda i: (0, i))],
        out_specs=pl.BlockSpec((height, block), lambda i: (0, i)),
        out_shape=jax.ShapeDtypeStruct((height, width), BF16),
        hbm=(0,),
        compiler_params=pltpu.CompilerParams(vmem_limit_bytes=16 << 20),
    )(in_hbm(left), in_hbm(right))


def norm_mix_kernel(terms, behind, gain, bias, shares, *refs):
    rows = terms[0][...].astype(F32)
    for term in terms[1:]:
        rows = rows + term[...].astype(F32)
    outs = list(refs)
    if len(terms) > 1:
        outs.pop(0)[...] = rows
    zhat, inverse = norm_parts(rows)
    outs.pop(0)[...] = zhat
    outs.pop(0)[...] = inverse
    normed = zhat * gain[...] + bias[...]
    group = pl.program_id(0)
    before = jnp.where(group == 0, behind[:1, :], behind[1:, :])
    step = normed - jnp.where(first_row(normed), before, shift_rows(normed, 1))
    for i, out in enumerate(outs):
        out[...] = (normed - step * (1.0 - shares[i : i + 1, :])).astype(BF16)


def norm_mix(terms, behind, gain, bias, shares, hbm):
    rows, breadth = terms[0].shape
    block = pl.BlockSpec((rows // 2, breadth), lambda g: (g, 0))
    whole = lambda element: pl.BlockSpec(element.shape, lambda g: (0, 0))
    shape = lambda kind: jax.ShapeDtypeStruct((rows, breadth), kind)
    wide = [shape(F32)] * (2 if len(terms) > 1 else 1)

    def body(*refs):
        norm_mix_kernel(refs[: len(terms)], *refs[len(terms) :])

    return run(
        body,
        grid=(2,),
        in_specs=[block] * len(terms) + [whole(element) for element in (behind, gain, bias, shares)],
        out_specs=[block] * len(wide)
        + [pl.BlockSpec((rows // 2, 1), lambda g: (g, 0))]
        + [block] * shares.shape[0],
        out_shape=wide + [jax.ShapeDtypeStruct((rows, 1), F32)] + [shape(BF16)] * shares.shape[0],
        hbm=hbm,
        compiler_params=pltpu.CompilerParams(vmem_limit_bytes=18 << 20),
    )(*terms, behind, gain, bias, shares)


def norm_back_kernel(count, table, *refs):
    parts = refs[:count]
    came, zhat_ref, inverse_ref, gain, base = refs[count : count + 5]
    outs = refs[count + 5 :]
    grad = parts[0][...]
    for part in parts[1:]:
        grad = grad + part[...].astype(F32)
    group = pl.program_id(0)
    grad = grad + jnp.where(last_row(grad), jnp.where(group == 0, came[:1, :], came[-1:, :]), 0.0)
    zhat = zhat_ref[...]
    scaled = grad * gain[...]
    middle = jnp.mean(scaled, axis=-1, keepdims=True)
    slope = jnp.mean(scaled * zhat, axis=-1, keepdims=True)
    total = base[...].astype(F32) + inverse_ref[...] * (scaled - middle - zhat * slope)
    for out in outs[:-1]:
        out[...] = total.astype(out.dtype)
    outs[-1][0, :1, :] = jnp.sum(grad * zhat, axis=0, keepdims=True)
    outs[-1][0, 1:, :] = jnp.sum(grad, axis=0, keepdims=True)


def norm_back(core, parts, came, zhat, inverse, gain, base, kinds, own):
    breadth = zhat.shape[1]
    rows = zhat.shape[0] // 2
    groups = 1 if own else 2
    pick = lambda width: pl.BlockSpec((rows, width), lambda g, table: (table[0] if own else g, 0))
    block = pl.BlockSpec((rows, breadth), lambda g, table: (g, 0))
    whole = lambda element: pl.BlockSpec(element.shape, lambda g, table: (0, 0))
    return run(
        partial(norm_back_kernel, len(parts)),
        grid_spec=dict(
            num_scalar_prefetch=1,
            grid=(groups,),
            in_specs=[block] * len(parts)
            + [whole(came), pick(breadth), pick(1), whole(gain), pick(breadth)],
            out_specs=[block] * len(kinds) + [pl.BlockSpec((1, 2, breadth), lambda g, table: (g, 0, 0))],
        ),
        out_shape=[jax.ShapeDtypeStruct((groups * rows, breadth), kind) for kind in kinds]
        + [jax.ShapeDtypeStruct((groups, 2, breadth), F32)],
        hbm=() if own else (0,),
        compiler_params=pltpu.CompilerParams(vmem_limit_bytes=16 << 20),
    )(core.astype(jnp.int32).reshape(1), *parts, came, zhat, inverse, gain, base)


def output_kernel(core_ref, part, swapped, gate_own, gate_other, cot_ref, middle, out, d_value, d_gate):
    core = core_ref[0]
    half = gate_own.shape[1]
    value = part[...] + swapped[...].astype(F32)
    cot = cot_ref[...].astype(F32)
    own, other = gate_own[...], gate_other[...]
    for i in range(2):
        gate = jnp.where(core == i, own, other)
        here = pl.ds(i * half, half)
        out[:, here] = (middle[:, here] + gate * value[:, i * half : (i + 1) * half]).astype(BF16)
        d_value[:, here] = (cot[:, i * half : (i + 1) * half] * gate).astype(BF16)
    mine = lambda rows: jnp.where(core == 0, rows[:, :half], rows[:, half:])
    d_gate[...] = (mine(cot) * mine(value) * own * (1.0 - own)).astype(BF16)


def output(core, part, swapped, gate_own, gate_other, cot, middle):
    rows, breadth = part.shape
    block = lambda width: pl.BlockSpec((rows // 2, width), lambda g: (g, 0))
    half = breadth // 2
    return run(
        output_kernel,
        grid=(2,),
        in_specs=[pl.BlockSpec(memory_space=pltpu.SMEM)]
        + [block(width) for width in (breadth, breadth, half, half, breadth, breadth)],
        out_specs=[block(breadth), block(breadth), block(half)],
        out_shape=[jax.ShapeDtypeStruct((rows, width), BF16) for width in (breadth, breadth, half)],
        compiler_params=pltpu.CompilerParams(vmem_limit_bytes=16 << 20),
    )(core.astype(jnp.int32).reshape(1), part, swapped, gate_own, gate_other, cot, middle)


def shift_rows(rows, distance):
    return pltpu.roll(rows, distance % rows.shape[0], 0)


def fade_tables(rate, reverse):
    breadth = rate.shape[-1]
    place = lax.broadcasted_iota(jnp.int32, (TILE, breadth), 0)
    if reverse:
        place = TILE - 1 - place
    steps = []
    distance = 1
    while distance < TILE:
        factor = jnp.where(place >= distance, jnp.exp(-rate * float(distance)), 0.0)
        steps.append((distance, factor))
        distance *= 2
    passed = jnp.exp(-rate * place.astype(F32))
    before = (place >= 1).astype(F32)
    return steps, passed, before


def scan_tile(terms, steps, reverse):
    for distance, factor in steps:
        terms = terms + factor * shift_rows(terms, -distance if reverse else distance)
    return terms


def wkv_kernel(
    groups, key_ref, value_ref, recept_ref, key_old, value_old, recept_old, rate_ref, bonus_ref, num_ref, den_ref,
    emit_ref, attended_ref, sent_ref, old_ref, gated_ref, prior_num_ref, prior_den_ref,
):
    rows = key_ref.shape[0] // groups
    rate = rate_ref[...]
    bonus = bonus_ref[...]
    steps, passed, before = fade_tables(rate, False)
    tile_fade = jnp.exp(-rate * float(TILE))

    def body(index, carry):
        states = []
        for group in range(groups):
            num, den = carry[2 * group], carry[2 * group + 1]
            at = pl.ds(pl.multiple_of(group * rows + index * TILE, TILE), TILE)
            grown = jnp.exp(key_ref[at, :].astype(F32))
            product = grown * value_ref[at, :].astype(F32)
            inner_num = scan_tile(product, steps, False)
            inner_den = scan_tile(grown, steps, False)
            prior_num = shift_rows(inner_num, 1) * before + passed * num
            prior_den = shift_rows(inner_den, 1) * before + passed * den
            prior_num_ref[at, :] = prior_num
            prior_den_ref[at, :] = prior_den
            wkv = (prior_num + bonus * product) / (prior_den + bonus * grown)
            gated_ref[at, :] = (recept_ref[at, :] * wkv.astype(BF16).astype(F32)).astype(BF16)
            states.append(inner_num[TILE - 1 :, :] + tile_fade * num)
            states.append(inner_den[TILE - 1 :, :] + tile_fade * den)
        return tuple(states)

    start = []
    for group in range(groups):
        start += [num_ref[group : group + 1, :], den_ref[group : group + 1, :]]
    lax.fori_loop(0, rows // TILE, body, tuple(start))
    attended = dot(gated_ref[...], emit_ref[...])
    attended_ref[...] = attended
    sent_ref[: groups * rows, :] = attended.astype(BF16)
    pad = lambda ref: jnp.concatenate([ref[...], jnp.zeros((TILE - groups, rate.shape[-1]), F32)], axis=0)
    grown = jnp.exp(key_old[...].astype(F32))
    product = grown * value_old[...].astype(F32)
    unfade = jnp.exp(rate)
    num = (pad(num_ref) - product) * unfade + bonus * product
    den = (pad(den_ref) - grown) * unfade + bonus * grown
    old = (recept_old[...] * (num / den).astype(BF16).astype(F32)).astype(BF16)
    attended = dot(old, emit_ref[...])
    old_ref[...] = attended
    sent_ref[groups * rows :, :] = attended.astype(BF16)


def wkv_back_kernel(
    groups, key_ref, value_ref, prior_num_ref, prior_den_ref, weighted_ref, rate_ref, bonus_ref,
    num_ref, den_ref, dkey_ref, dvalue_ref, decay_ref, first_ref,
):
    rows = key_ref.shape[0] // groups
    rate = rate_ref[...]
    bonus = bonus_ref[...]
    steps, passed, before = fade_tables(rate, True)
    tile_fade = jnp.exp(-rate * float(TILE))
    decay_ref[...] = jnp.zeros_like(decay_ref)
    first_ref[...] = jnp.zeros_like(first_ref)

    def body(step, carry):
        index = rows // TILE - 1 - step
        states = []
        for group in range(groups):
            num, den = carry[2 * group], carry[2 * group + 1]
            at = pl.ds(pl.multiple_of(group * rows + index * TILE, TILE), TILE)
            grown = jnp.exp(key_ref[at, :].astype(F32))
            value = value_ref[at, :].astype(F32)
            prior_num = prior_num_ref[at, :]
            prior_den = prior_den_ref[at, :]
            wkv_den = prior_den + bonus * grown
            wkv = (prior_num + bonus * grown * value) / wkv_den
            grad = weighted_ref[at, :].astype(F32) / wkv_den
            inner_num = scan_tile(grad, steps, True)
            inner_den = scan_tile(-grad * wkv, steps, True)
            lam_num = shift_rows(inner_num, -1) * before + passed * num
            lam_den = shift_rows(inner_den, -1) * before + passed * den
            bonus_grad = bonus * grad
            dvalue_ref[at, :] = (grown * (bonus_grad + lam_num)).astype(BF16)
            direct = bonus_grad * (value - wkv)
            dkey_ref[at, :] = (grown * (direct + lam_num * value + lam_den)).astype(BF16)
            first_ref[...] += grown * direct
            decay_ref[...] += lam_num * prior_num + lam_den * prior_den
            states.append(inner_num[:1, :] + tile_fade * num)
            states.append(inner_den[:1, :] + tile_fade * den)
        return tuple(states)

    start = []
    for group in range(groups):
        start += [num_ref[group : group + 1, :], den_ref[group : group + 1, :]]
    lax.fori_loop(0, rows // TILE, body, tuple(start))


def wkv_start_kernel(
    groups, grad_ref, recept_ref, key_ref, value_ref, prior_num_ref, prior_den_ref, rate_ref, bonus_ref,
    weighted_ref, accept_ref, begin_ref,
):
    rows = key_ref.shape[0] // groups
    rate = rate_ref[...]
    bonus = bonus_ref[...]
    place = lax.broadcasted_iota(jnp.int32, (TILE, rate.shape[-1]), 0).astype(F32)
    tile_fade = jnp.exp(-rate * float(TILE))

    def body(index, carry):
        fade, sums = carry[0], []
        for group in range(groups):
            at = pl.ds(pl.multiple_of(group * rows + index * TILE, TILE), TILE)
            grown = bonus * jnp.exp(key_ref[at, :].astype(F32))
            wkv_den = prior_den_ref[at, :] + grown
            wkv = (prior_num_ref[at, :] + grown * value_ref[at, :].astype(F32)) / wkv_den
            recept = recept_ref[at, :]
            grad = grad_ref[at, :]
            kept = grad * recept
            weighted = kept.astype(BF16)
            weighted_ref[at, :] = weighted
            accept_ref[at, :] = (kept * wkv.astype(BF16).astype(F32) * (1.0 - recept)).astype(BF16)
            faded = fade * (weighted.astype(F32) / wkv_den)
            sums += [carry[1 + 2 * group] + faded, carry[2 + 2 * group] - faded * wkv]
        return (fade * tile_fade, *sums)

    zero = jnp.zeros((TILE, rate.shape[-1]), F32)
    _, *sums = lax.fori_loop(0, rows // TILE, body, (jnp.exp(-rate * place),) + (zero,) * (2 * groups))
    for group in range(groups):
        for i in range(2):
            begin_ref[i, group : group + 1, :] = jnp.sum(sums[2 * group + i], axis=0, keepdims=True)


def keys_kernel(groups, chips, blocks, table, *refs):
    mixes, befores, weights = refs[:3], refs[3:6], refs[6:9]
    late, rate = refs[9 : 9 + 3 * blocks], refs[9 + 3 * blocks]
    keys, values, recept, *before, ends, held = refs[10 + 3 * blocks :]
    kinds = (BF16, BF16, None)
    for i, (out, old, kind) in enumerate(zip((keys, values, recept), before, kinds)):
        held[...] = weights[i][...]
        for j in range(blocks):
            block = late[i * blocks + j]
            height = block.shape[0]
            held[pl.ds(pl.multiple_of(table[chips[j]] * height, height), height), :] = block[...]
        for target, mixed in ((out, mixes[i]), (old, befores[i])):
            product = dot(mixed[...], held[...])
            target[...] = jax.nn.sigmoid(product) if kind is None else product.astype(kind)
    rows = keys.shape[0] // groups
    left = (rows - 1 - lax.broadcasted_iota(jnp.int32, (rows, keys.shape[1]), 0)).astype(F32)
    fades = jnp.exp(-rate[...] * left)
    for group in range(groups):
        here = pl.ds(group * rows, rows)
        grown = jnp.exp(keys[here, :].astype(F32)) * fades
        ends[0, group : group + 1, :] = jnp.sum(grown * values[here, :].astype(F32), axis=0, keepdims=True)
        ends[1, group : group + 1, :] = jnp.sum(grown, axis=0, keepdims=True)


def keys_call(table, mixes, befores, weights, late, rate):
    rows, breadth = mixes[0].shape
    columns = weights[0].shape[1]
    block = min(256, columns)
    steps = columns // block
    chips, blocks = late
    wide = lambda height: pl.BlockSpec((height, block), lambda i, table: (0, i))
    part = lambda number: pl.BlockSpec(
        (blocks[0].shape[0], block), lambda i, table: (0, number * steps + i)
    )
    shape = lambda height, kind: jax.ShapeDtypeStruct((height, columns), kind)
    kinds = (BF16, BF16, F32)
    return run(
        partial(keys_kernel, 2, chips, len(blocks)),
        grid_spec=dict(
            num_scalar_prefetch=1,
            grid=(steps,),
            in_specs=[whole_block((rows, breadth))] * 3
            + [whole_block((TILE, breadth))] * 3
            + [wide(breadth)] * 3
            + [part(number) for number in range(3) for _ in blocks]
            + [wide(1)],
            out_specs=[wide(rows)] * 3 + [wide(TILE)] * 3 + [pl.BlockSpec((2, 2, block), lambda i, table: (0, 0, i))],
            scratch_shapes=[pltpu.VMEM((breadth, block), BF16)],
        ),
        out_shape=[shape(rows, kind) for kind in kinds]
        + [shape(TILE, kind) for kind in kinds]
        + [jax.ShapeDtypeStruct((2, 2, columns), F32)],
        hbm=(0, 1, 2),
        compiler_params=pltpu.CompilerParams(vmem_limit_bytes=20 << 20),
    )(table, *mixes, *befores, *map(in_hbm, weights), *(list(blocks) * 3), rate)


def wkv_call(kernel, groups, shapes, operands, hbm=(), vmem=()):
    return run(
        partial(kernel, groups),
        out_shape=shapes,
        in_specs=[whole_block(operand.shape) for operand in operands],
        out_specs=[whole_block(out.shape) for out in shapes],
        hbm=hbm,
        vmem=vmem,
        compiler_params=pltpu.CompilerParams(vmem_limit_bytes=14 << 20),
    )(*operands)


def mix_back_kernel(groups, count, core_ref, *refs):
    grads = refs[:count]
    zhat, behind, gain, bias, shares = refs[count : count + 5]
    *parts, first, sums = refs[count + 5 :]
    rows = zhat.shape[0] // groups
    totals = [0.0] * count
    for group in range(groups):
        here = pl.ds(group * rows, rows)
        normed = zhat[here, :] * gain[...] + bias[...]
        step = normed - jnp.where(first_row(normed), behind[group : group + 1, :], shift_rows(normed, 1))
        direct, shifted = 0.0, 0.0
        for i in range(count):
            grad = grads[i][here, :]
            moved = grad * (1.0 - shares[i : i + 1, :])
            direct += grad - moved
            shifted += moved
            totals[i] += jnp.sum(grad * step, axis=0, keepdims=True)
        first[group : group + 1, :] = shifted[:1, :]
        part = direct + jnp.where(last_row(shifted), 0.0, shift_rows(shifted, -1))
        if parts[0].shape == zhat.shape:
            parts[0][here, :] = part
            parts[1][here, :] = part.astype(BF16)
        else:
            for i in range(2):

                @pl.when((core_ref[0] == group) == (i == 0))
                def _():
                    parts[i][...] = part.astype(parts[i].dtype)
    for i in range(count):
        sums[i : i + 1, :] = totals[i]


def mix_back(core, grads, zhat, behind, gain, bias, shares, apart):
    rows, breadth = zhat.shape
    count = len(grads)
    block = min(256, breadth)
    column = lambda height: pl.BlockSpec((height, block), lambda i: (0, i))
    outs = [(rows // 2 if apart else rows, kind) for kind in (F32, BF16)] + [(2, F32), (count, F32)]
    return run(
        partial(mix_back_kernel, 2, count),
        grid=(breadth // block,),
        in_specs=[pl.BlockSpec(memory_space=pltpu.SMEM)]
        + [column(rows)] * (count + 1)
        + [column(2), column(1), column(1), column(count)],
        out_specs=[column(height) for height, _ in outs],
        out_shape=[jax.ShapeDtypeStruct((height, breadth), kind) for height, kind in outs],
        hbm=() if apart else (0,),
        compiler_params=pltpu.CompilerParams(vmem_limit_bytes=14 << 20),
    )(core.astype(jnp.int32).reshape(1), *grads, zhat, behind, gain, bias, shares)


def per_device(
    layer_incoming,
    series_extents,
    emitted_adjoint,
    norm1_scaling,
    norm1_offset,
    mixer_lookup_portion,
    mixer_payload_portion,
    mixer_accept_portion,
    temporal_fading_log,
    present_step_reward,
    mixer_lookup_matrix,
    mixer_payload_matrix,
    mixer_accept_matrix,
    mixer_emit_matrix,
    norm2_scaling,
    norm2_offset,
    feedforward_lookup_portion,
    feedforward_accept_portion,
    feedforward_lookup_matrix,
    feedforward_payload_matrix,
    feedforward_accept_matrix,
):
    LAST.clear()
    HELD.clear()
    devices = lax.axis_size(ALL)
    chips = lax.axis_size(CHIPS)
    parts = lax.axis_size(SEQ)
    core = lax.axis_index("c")
    place = lax.axis_index(SEQ)
    rows, breadth = layer_incoming.shape[1:]
    own_rows = mixer_lookup_matrix.shape[0]
    hidden_rows = feedforward_payload_matrix.shape[0]

    half = breadth // 2
    hidden = feedforward_lookup_matrix.shape[1] // 2
    both = lambda own, other: jnp.where(core == 0, jnp.stack([own, other]), jnp.stack([other, own]))
    mine_of = lambda pair: lax.dynamic_index_in_dim(pair, core, 0, keepdims=False)
    other_of = lambda pair: lax.dynamic_index_in_dim(pair, 1 - core, 0, keepdims=False)
    pair_rows = 2 * own_rows
    every = slice(None)
    mix_views = (
        tuple((i, (every, pl.ds(i * half, half)), (every, every)) for i in range(3))
        + tuple(
            (3, (pl.ds(i * own_rows, own_rows), pl.ds(3 * half, half)), (every, pl.ds(i * half, half)))
            for i in range(2)
        )
        + ((4, (every, pl.ds(4 * half, half)), (every, every)),),
        ((pair_rows, half),) * 3 + ((own_rows, breadth), (pair_rows, half)),
        (pair_rows, 5 * half),
    )
    stack = hidden_rows // pair_rows
    ffn_views = (
        ((0, (every, pl.ds(0, hidden)), (every, every)),)
        + tuple(
            (1, (every, pl.ds(hidden + i * breadth, breadth)), (pl.ds(i * pair_rows, pair_rows), every))
            for i in range(stack)
        ),
        ((pair_rows, hidden), (hidden_rows, breadth)),
        (pair_rows, hidden + stack * breadth),
    )
    gather_views = (
        mix_views[0]
        + tuple(
            (5 + out, (every, pl.ds(5 * half + source[1].start, source[1].size)), target)
            for out, source, target in ffn_views[0]
        ),
        mix_views[1] + ffn_views[1],
        (pair_rows, 5 * half + ffn_views[2][1]),
    )

    begins = jnp.cumsum(series_extents[0]) - series_extents[0]
    starts = jnp.any(jnp.arange(parts)[:, None] * rows == begins[None, :], axis=1)
    joined = jnp.where(starts, 0.0, 1.0).astype(F32)
    joined = both(joined, swap(joined))

    own_in, own_cot = in_hbm(layer_incoming[0]), in_hbm(emitted_adjoint[0])
    ends_of = lambda element: element.reshape(2, rows, -1)[:, rows - 2 :]

    rounds = in_rounds()
    table = chip_table() if rounds else jnp.zeros((1,), jnp.int32)
    split_up = (
        mixer_lookup_matrix, mixer_payload_matrix, mixer_accept_matrix,
        feedforward_accept_matrix, feedforward_lookup_matrix,
    )
    widths = (own_rows, own_rows, own_rows, half, hidden_rows)
    picks = jax.ShapeDtypeStruct((own_rows, 4 * half + hidden), BF16)
    both_inputs = lambda: both_groups(core, (own_in, swap(own_in)), (own_cot, swap(own_cot)))
    if rounds:
        mine, other = whole_call(partial(pick_kernel, widths), (picks, picks), core, tuple(map(in_hbm, split_up)))
        other = swap(other)
        inputs, cotangent = both_inputs()
        wait_for(joined)
        (block,) = whole_call(
            partial(pack_kernel, half), [jax.ShapeDtypeStruct(gather_views[2], BF16)],
            core, (mine, other, in_hbm(mixer_emit_matrix), in_hbm(feedforward_payload_matrix)),
        )
    else:
        halves = jnp.concatenate(
            [
                matrix.reshape(own_rows, -1, 2, width).transpose(2, 0, 1, 3).reshape(2, own_rows, -1)
                for matrix, width in zip(split_up, widths)
            ],
            axis=-1,
        )
        pair = both(mine_of(halves), swap(other_of(halves))).reshape(pair_rows, -1)
        emit = jnp.concatenate([mixer_emit_matrix[:, :half], mixer_emit_matrix[:, half:]], axis=0)
        inputs, cotangent = both_inputs()
        payload = [feedforward_payload_matrix[i * pair_rows : (i + 1) * pair_rows] for i in range(stack)]
        block = jnp.concatenate([pair[:, : 3 * half], emit, pair[:, 3 * half :], *payload], axis=1)
    Gather, Scatter = (GatherRounds, ScatterRounds) if rounds else (GatherRings, ScatterRings)
    weights = Gather(table, block, gather_views)
    weights.step(0)
    weights.place(-1)
    pieces = (
        norm1_scaling, norm1_offset, mixer_lookup_portion, mixer_payload_portion,
        mixer_accept_portion, norm2_scaling, norm2_offset, feedforward_lookup_portion,
        feedforward_accept_portion, temporal_fading_log, present_step_reward,
    )
    pieces = [piece.reshape(1, own_rows) for piece in pieces]
    vectors = run(
        stack_kernel,
        out_shape=jax.ShapeDtypeStruct((devices, len(pieces), own_rows), BF16),
        in_specs=[whole_block(piece.shape) for piece in pieces],
        out_specs=whole_block((devices, len(pieces), own_rows)),
    )(*pieces)
    vectors = lax.all_to_all(vectors, ALL, 0, 0, tiled=True)
    (edge,) = hold(ends_of(inputs))
    behind = along_seq(edge, 1)
    LAST.extend([behind, vectors])
    weights.step(1)
    weights.place(0)

    vectors = vectors.astype(F32).transpose(1, 0, 2)
    channel = lax.dynamic_index_in_dim(
        vectors[9:].reshape(2, chips, 2, own_rows), core, 2, keepdims=False
    ).reshape(2, 1, -1)
    vectors = vectors[:9].reshape(9, breadth)
    gain1, bias1, shares1, gain2, bias2, shares2 = (
        vectors[start:stop] for start, stop in ((0, 1), (1, 2), (2, 5), (5, 6), (6, 7), (7, 9))
    )
    rate, bonus = jnp.exp(channel[0]), jnp.exp(channel[1])

    keep = lax.dynamic_index_in_dim(joined, place, 1)[:, :, None]
    index = jnp.arange(parts)
    began = jnp.where((joined == 0.0) & (index[None] <= place), index[None], -1).max(axis=1)
    reach = ((index[None] < place) & (index[None] >= began[:, None])).astype(F32)
    begun = jnp.where((joined == 0.0) & (index[None] > place), index[None], parts).min(axis=1)
    reach_back = ((index[None] > place) & (index[None] < begun[:, None])).astype(F32)

    def entering(ends, reached, distance):
        fades = jnp.exp(-rate[None] * (float(rows) * jnp.maximum(distance, 0).astype(F32))[:, None, None])
        return jnp.sum(ends * (reached.T[:, None, :, None] * fades[:, :, None]), axis=0)

    def spread(ends):
        return lax.all_to_all(
            jnp.broadcast_to(ends[None], (parts,) + ends.shape), SEQ, 0, 0, tiled=True
        )

    weights.step(2)
    weights.place(1)
    behind = behind.astype(F32)
    normed_before = norm_parts(behind)[0] * gain1 + bias1
    step_before = normed_before[:, 1] - normed_before[:, 0]
    mixed_before = [
        jnp.pad(normed_before[:, 1] - step_before * (1.0 - shares1[i : i + 1]), ((0, TILE - 2), (0, 0))).astype(BF16)
        for i in range(3)
    ]
    behind1 = normed_before[:, 1] * keep[:, 0]
    zhat1, inverse1, mixed_k, mixed_v, mixed_r = norm_mix(
        [inputs], behind1, gain1, bias1, shares1, range(5)
    )
    weights.step(3)
    weights.place(2)
    weights.step(4)
    weights.place(3)
    whole = lambda held: held.reshape(-1, held.shape[-1])
    weight_k, weight_v, weight_r, *_ = map(whole, weights.held)
    keys, values, recept, *before, ends = keys_call(
        table, (mixed_k, mixed_v, mixed_r), mixed_before, (weight_k, weight_v, weight_r), weights.last_blocks(), rate
    )
    weights.place(4)
    weight_k, weight_v, weight_r, weight_o, weight_fr, weight_fk, weight_fv = map(whole, weights.held)

    enter = entering(spread(ends), reach, place - 1 - index)
    shape = lambda kind: jax.ShapeDtypeStruct((2 * rows, half), kind)
    attended, sent, old, gated, prior_num, prior_den = wkv_call(
        wkv_kernel, 2,
        (
            jax.ShapeDtypeStruct((2 * rows, breadth), F32), jax.ShapeDtypeStruct((2 * rows + TILE, breadth), BF16),
            jax.ShapeDtypeStruct((TILE, breadth), F32), shape(BF16), shape(F32), shape(F32),
        ),
        (keys, values, recept, *before, rate, bonus, enter[0], enter[1], in_hbm(weight_o)), (0, 3, 4, 5),
    )
    swapped = swap(sent)
    HELD.append((swapped, pltpu.HBM))
    before2 = behind[:, 1] + (old + swapped[2 * rows :].astype(F32))[:2]
    behind2 = (norm_parts(before2)[0] * gain2 + bias2) * keep[:, 0]
    middle, zhat2, inverse2, ffn_k, ffn_r = norm_mix(
        [inputs, attended, swapped], behind2, gain2, bias2, shares2, ()
    )
    gate_own = jax.nn.sigmoid(dot(ffn_r, weight_fr))
    gate_other = swap(gate_own)
    pre_hidden = jax.nn.relu(dot(ffn_k, weight_fk))
    hidden_act = jnp.square(pre_hidden).astype(BF16)
    value_part = dot(hidden_act, weight_fv)
    block_output, d_value_out, d_gate_pre = output(
        core, value_part, swap(value_part.astype(BF16)), gate_own, gate_other, cotangent, middle
    )
    block_output = mine_of(block_output.reshape(2, rows, breadth))

    d_hidden = dot_back(d_value_out, weight_fv)
    d_pre_hidden = (d_hidden * 2.0 * pre_hidden).astype(BF16)
    def came_back(first):
        first = first * keep[:, 0]
        pairs = [(2 * i + c, 2 * (i - 1) + 1 - c) for i in range(1, parts) for c in range(2)]
        return along_seq(first, -1) + lax.ppermute(first, SEQ + ("c",), pairs)

    part2, sent2, first2, share_grads2 = mix_back(
        core, (dot_back(d_pre_hidden, weight_fk), dot_back(d_gate_pre, weight_fr)),
        zhat2, behind2, gain2, bias2, shares2, False,
    )
    grad_fv = outer_call(hidden_act, d_value_out)
    swapped2 = swap(sent2)
    HELD.append((swapped2, pltpu.HBM))
    d_middle, d_attended, norm_grads2 = norm_back(
        core, (part2, swapped2), came_back(first2), zhat2, inverse2, gain2, cotangent,
        (F32, BF16), False,
    )

    grad_o = outer(gated, d_attended).astype(BF16)
    d_gated = dot_back(d_attended, weight_o)
    d_weighted, d_recept_pre, begins_back = wkv_call(
        wkv_start_kernel, 2,
        (shape(BF16), shape(BF16), jax.ShapeDtypeStruct((2, 2, half), F32)),
        (d_gated, recept, keys, values, prior_num, prior_den, rate, bonus),
    )
    grad_fk = outer_call(ffn_k, d_pre_hidden)
    enter_back = entering(spread(begins_back), reach_back, index - place - 1)
    small = jax.ShapeDtypeStruct((TILE, half), F32)
    d_keys, d_values, decay_sum, bonus_sum = wkv_call(
        wkv_back_kernel, 2, (shape(BF16), shape(BF16), small, small),
        (keys, values, prior_num, prior_den, d_weighted, rate, bonus, enter_back[0], enter_back[1]),
    )
    grad_fr = outer(ffn_r, d_gate_pre).astype(BF16)
    grad_k = outer(mixed_k, d_keys).astype(BF16)
    grad_v = outer(mixed_v, d_values).astype(BF16)
    grad_r = outer(mixed_r, d_recept_pre).astype(BF16)
    per_chip = lambda grad: grad.reshape(chips, -1, grad.shape[-1])
    scatter = Scatter(
        table,
        [per_chip(grad) for grad in (grad_k, grad_v, grad_r, grad_o, grad_fr, grad_fk, grad_fv)],
        gather_views,
    )
    scatter.step(0)
    own1, other1, first1, share_grads1 = mix_back(
        core,
        (dot_back(d_keys, weight_k), dot_back(d_values, weight_v), dot_back(d_recept_pre, weight_r)),
        zhat1, behind1, gain1, bias1, shares1, True,
    )
    swapped1 = swap(other1)
    first_sum = (first1 + swap(first1)) * keep[:, 0]
    scatter.step(1, [swapped1, first_sum])
    came1 = along_seq(first_sum, -1)
    scatter.step(2, [came1])
    input_grad, norm_grads1 = norm_back(
        core, (own1, swapped1), mine_of(came1[:, None]), zhat1, inverse1, gain1, d_middle, (F32,), True
    )
    pieces = (norm_grads1, share_grads1, decay_sum, bonus_sum, rate, norm_grads2, share_grads2)
    grads = run(
        vectors_kernel,
        out_shape=jax.ShapeDtypeStruct((devices, 11, own_rows), F32),
        in_specs=[pl.BlockSpec(memory_space=pltpu.SMEM)] + [whole_block(piece.shape) for piece in pieces],
        out_specs=whole_block((devices, 11, own_rows)),
    )(core.astype(jnp.int32).reshape(1), *pieces)
    grads = lax.all_to_all(grads, ALL, 0, 0, tiled=True)
    scatter.step(3)
    scatter.step(4, [grads])
    grads = run(
        vector_sums_kernel,
        out_shape=jax.ShapeDtypeStruct((11, own_rows), F32),
        in_specs=[whole_block(grads.shape)],
        out_specs=whole_block((11, own_rows)),
    )(grads)

    widths = [(half, own_rows)] * 3 + [(half, half), (hidden, hidden_rows)]
    emit_at = [(pl.ds(i * own_rows, own_rows), pl.ds(3 * half, half)) for i in range(2)]
    payload_at = [(pl.ds(0, pair_rows), pl.ds(5 * half + hidden + i * breadth, breadth)) for i in range(stack)]
    columns = [(0, 3 * half), (4 * half, half + hidden)]
    if rounds:
        mine, other, sum_o, sum_fv = scatter.finish(core, columns, [(False, emit_at), (True, payload_at)])
        outs = [jax.ShapeDtypeStruct((own_rows, 2 * size), F32) for size, _ in widths]
        sum_k, sum_v, sum_r, sum_fr, sum_fk = whole_call(
            partial(join_kernel, [width for _, width in widths]), outs, core, (mine, swap(other))
        )
    else:
        total = scatter.result()
        pair = jnp.concatenate([total[:, start : start + size] for start, size in columns], axis=1)
        pair = pair.reshape(2, own_rows, -1)
        mine, other = mine_of(pair), swap(other_of(pair))
        low, high = jnp.where(core == 0, mine, other), jnp.where(core == 0, other, mine)
        outs, at = [], 0
        for size, width in widths:
            pieces = [piece[:, at : at + size].reshape(own_rows, -1, 1, width) for piece in (low, high)]
            outs.append(jnp.concatenate(pieces, axis=2).reshape(own_rows, 2 * size))
            at += size
        sum_k, sum_v, sum_r, sum_fr, sum_fk = outs
        sum_o = jnp.concatenate([total[at] for at in emit_at], axis=1)
        sum_fv = jnp.concatenate([total[at] for at in payload_at], axis=0)

    return (
        block_output[None],
        input_grad[None],
        *(grads[i] for i in range(7)),
        sum_k,
        sum_v,
        sum_r,
        sum_o,
        *(grads[i] for i in range(7, 11)),
        sum_fk,
        sum_fv,
        sum_fr,
    )


def solution(mesh):
    parts, groups = mesh.shape["seq"], mesh.shape["rep"]
    width = groups // 2
    fine = Mesh(mesh.devices.reshape(parts // width, width, width, 2), ALL)
    tokens = P(("y", "c"), SEQ, None)
    vector = P(ALL)
    matrix = P(ALL, None)
    return jax.shard_map(
        per_device,
        mesh=fine,
        in_specs=(
            (tokens, P(("y", "c"), None), tokens)
            + (vector,) * 7
            + (matrix,) * 4
            + (vector,) * 4
            + (matrix,) * 3
        ),
        out_specs=(
            (tokens, tokens) + (vector,) * 7 + (matrix,) * 4 + (vector,) * 4 + (matrix,) * 3
        ),
        check_vma=False,
    )
```

```python
from functools import partial

import jax
import jax.numpy as jnp
from jax import lax
from jax.experimental import pallas as pl
from jax.experimental.pallas import tpu as pltpu
from jax.sharding import Mesh, PartitionSpec as P

EPSILON = 1e-05
F32 = jnp.float32
BF16 = jnp.bfloat16
CHIPS = ("z", "x", "y")
SEQ = ("z", "x")
ALL = ("z", "x", "y", "c")
TILE = 16
FREE = pl.CostEstimate(flops=0, bytes_accessed=0, transcendentals=0)


def ring(count, step=1):
    return [(i, (i + step) % count) for i in range(count)]


def swap(block):
    return lax.ppermute(block, "c", ring(2))


def along_seq(block, step):
    count = lax.axis_size(SEQ)
    pairs = [(i, i + step) for i in range(count) if 0 <= i + step < count]
    return lax.ppermute(block, SEQ, pairs)


ROUNDS = (
    (("z", (0, 0, 0), (1, 0, 0)), ("y", (0, 0, 0), (0, 0, 1)), ("x", (0, 0, 0), (0, 1, 0))),
    (("z", (1, 0, 0), (2, 0, 0)), ("y", (1, 0, 0), (1, 0, 1)), ("x", (0, 0, 1), (0, 1, 1))),
    (("z", (2, 0, 0), (3, 0, 0)), ("y", (2, 0, 0), (2, 0, 1)), ("x", (1, 0, 0), (1, 1, 0))),
    (("z", (0, 1, 1), (1, 1, 1)), ("y", (3, 0, 0), (3, 0, 1)), ("x", (3, 0, 0), (3, 1, 0))),
    (("z", (1, 1, 1), (2, 1, 1)), ("y", (3, 1, 0), (3, 1, 1)), ("x", (2, 0, 0), (2, 1, 0))),
)


def in_rounds():
    return tuple(lax.axis_size(axis) for axis in CHIPS) == (4, 2, 2)


RELATIVES = tuple((z, x, y) for z in range(4) for x in range(2) for y in range(2))
ANYWHERE = pl.BlockSpec(memory_space=pl.ANY)


def chip_table():
    whole = jnp.asarray(RELATIVES, jnp.int32)
    total = jnp.zeros((len(RELATIVES),), jnp.int32)
    for i, axis in enumerate(CHIPS):
        count = lax.axis_size(axis)
        total = total * count + lax.rem(lax.axis_index(axis) + (count - whole[:, i]), count)
    return jnp.concatenate([total, lax.axis_index("c")[None]]).astype(jnp.int32)


def whole_block(shape):
    return pl.BlockSpec(shape, lambda *g: (0,) * len(shape))


def in_hbm(array):
    return pltpu.with_memory_space_constraint(array, pltpu.HBM)


LAST = []
HELD = []


def where_it_is(array):
    kinds = [kind for held, kind in HELD if held is array]
    return pltpu.with_memory_space_constraint(array, kinds[0]) if kinds else array


def run(
    kernel, *, out_shape, grid=(1,), in_specs=None, out_specs=None, grid_spec=None, hbm=(), vmem=(), **settings
):
    spec = grid_spec or dict(num_scalar_prefetch=0, grid=grid, in_specs=in_specs, out_specs=out_specs)
    spec.setdefault("scratch_shapes", settings.pop("scratch_shapes", ()))
    direct = not spec["grid"]
    single = isinstance(out_shape, jax.ShapeDtypeStruct)
    shapes = [out_shape] if single else list(out_shape)
    kinds = [pltpu.HBM if i in hbm else pltpu.VMEM if i in vmem else None for i in range(len(shapes))]
    shapes = [out if kind is None else kind(out.shape, out.dtype) for out, kind in zip(shapes, kinds)]

    def call(*operands):
        marks = [mark for mark in LAST if not any(mark is operand for operand in operands)]
        count = len(operands)
        outputs = count + len(marks) + len(shapes)

        def body(*refs):
            refs[outputs][...] = jnp.zeros_like(refs[outputs])
            kernel(*refs[:count], *refs[count + len(marks) : outputs], *refs[outputs + 1 :])

        out_specs = [spec["out_specs"]] if single else list(spec["out_specs"])
        *outs, token = pl.pallas_call(
            body,
            grid_spec=pltpu.PrefetchScalarGridSpec(
                **{
                    **spec,
                    "in_specs": list(spec["in_specs"]) + [ANYWHERE] * len(marks),
                    "out_specs": out_specs + [pl.BlockSpec(memory_space=pltpu.VMEM) if direct else whole_block((8, 128))],
                }
            ),
            out_shape=shapes + [jax.ShapeDtypeStruct((8, 128), F32) if direct else pltpu.HBM((8, 128), F32)],
            cost_estimate=FREE,
            **settings,
        )(*map(where_it_is, operands), *map(where_it_is, marks))
        LAST[:] = [token]
        HELD.extend((out, kind) for out, kind in zip(outs + [token], kinds + [None if direct else pltpu.HBM]) if kind is not None)
        return outs[0] if single else outs

    return call


def hold_kernel(*refs):
    pass


def hold(*arrays, kind=None):
    return run(
        hold_kernel,
        out_shape=[jax.ShapeDtypeStruct(array.shape, array.dtype) for array in arrays],
        vmem=range(len(arrays)) if kind else (),
        in_specs=[ANYWHERE] * len(arrays),
        out_specs=[ANYWHERE] * len(arrays),
        input_output_aliases={i: i for i in range(len(arrays))},
    )(*(pltpu.with_memory_space_constraint(array, kind) if kind else array for array in arrays))


def wait_for(*arrays):
    LAST.extend(arrays)
    run(hold_kernel, out_shape=[], in_specs=[], out_specs=[])()


def place_kernel(first, views, aliased, table_ref, *refs):
    blocks = refs[: len(first)]
    outs = refs[len(first) + aliased : -1]
    copies = []
    for i, block in enumerate(blocks):
        for number, (out, source, target) in enumerate(views[0]):
            copies.append(
                pltpu.make_async_copy(
                    block.at[source],
                    outs[out].at[(table_ref[first[i]],) + target],
                    refs[-1].at[i, number],
                )
            )
    for copy in copies:
        copy.start()
    for copy in copies:
        copy.wait()


def place_blocks(table, held, blocks, relatives, views):
    moves, shapes, _ = views
    chips = lax.axis_size(CHIPS)
    first = [RELATIVES.index(relative) for relative in relatives]
    operands = [table, *blocks]
    aliases = {}
    if held is not None:
        aliases = {len(operands) + i: i for i in range(len(shapes))}
        operands += held
    hbm = pl.BlockSpec(memory_space=pltpu.HBM)
    return run(
        partial(place_kernel, first, views, len(aliases)),
        grid=(1,),
        in_specs=[pl.BlockSpec(memory_space=pltpu.SMEM)]
        + [whole_block(block.shape) for block in blocks]
        + [hbm] * len(aliases),
        out_specs=[hbm] * len(shapes),
        out_shape=[jax.ShapeDtypeStruct((chips,) + shape, BF16) for shape in shapes],
        scratch_shapes=[pltpu.SemaphoreType.DMA((len(blocks), len(moves)))],
        input_output_aliases=aliases,
    )(*operands)


class GatherRounds:
    def __init__(self, table, block, views):
        self.table, self.views = table, views
        self.have = {(0, 0, 0): block}
        self.held, self.due = None, []

    def place(self, number):
        names = [(0, 0, 0)] if number < 0 else [received for _, _, received in ROUNDS[number]]
        blocks = [self.have[name] for name in names]
        self.held = place_blocks(self.table, self.held, blocks, names, self.views)

    def step(self, number):
        names = list({sent: None for _, sent, _ in ROUNDS[number]})
        LAST.extend(array for array in self.due if not any(array is self.have[name] for name in names))
        self.have.update(zip(names, hold(*(self.have[name] for name in names), kind=pltpu.VMEM)))
        for axis, sent, received in ROUNDS[number]:
            self.have[received] = lax.ppermute(self.have[sent], axis, ring(lax.axis_size(axis)))
        self.due = [self.have[received] for _, _, received in ROUNDS[number]]

    def last_blocks(self):
        names = [received for _, _, received in ROUNDS[-1]]
        return [RELATIVES.index(name) for name in names], [self.have[name] for name in names]


class GatherRings:
    def __init__(self, table, block, views):
        self.held = gather_rings(block, views)

    def place(self, number):
        pass

    def step(self, number):
        pass

    def last_blocks(self):
        return [], []


def gather_rings(block, views):
    have = []
    shape = block.shape
    for axis in CHIPS:
        count = lax.axis_size(axis)
        me = lax.axis_index(axis)
        have.append(axis)
        place = len(have) - 1
        whole = jnp.zeros(block.shape[:place] + (count,) + block.shape[place:], block.dtype)
        piece = block
        for step in range(count):
            if step:
                piece = lax.ppermute(piece, axis, ring(count))
            whole = lax.dynamic_update_index_in_dim(whole, piece, lax.rem(me - step + count, count), place)
        block = whole
    block = block.reshape((-1,) + shape)
    held = [jnp.zeros(block.shape[:1] + view, block.dtype) for view in views[1]]
    for out, source, target in views[0]:
        held[out] = held[out].at[(slice(None),) + target].set(block[(slice(None),) + source])
    return held


def sum_kernel(first, counts, views, passing, table_ref, *refs):
    arrays, wanted = len(views[1]), len(counts)
    inputs = arrays + sum(counts) + passing
    grads = refs[:arrays]
    received = refs[arrays : arrays + sum(counts)]
    outs = refs[inputs : inputs + wanted]
    *own, sems = refs[inputs + wanted + passing :]
    copies = [
        [
            pltpu.make_async_copy(grads[a].at[table_ref[chip]], own[a].at[i], sems.at[i, a])
            for a in range(arrays)
            if chip is not None
        ]
        for i, chip in enumerate(first)
    ]
    for copy in sum(copies, []):
        copy.start()
    at = 0
    for i, count in enumerate(counts):
        for copy in copies[i]:
            copy.wait()
        for out, source, target in pieces_of(views):
            terms = [] if first[i] is None else [own[out][(i,) + target].astype(F32)]
            terms += [received[j][source].astype(F32) for j in range(at, at + count)]
            outs[i][source] = sum(terms[1:], terms[0]).astype(outs[i].dtype)
        at += count


def pieces_of(views):
    moves, shapes, block_shape = views
    spans = lambda place, size: (place.start, place.size) if isinstance(place, pl.Slice) else (0, size)
    for out, source, target in moves:
        starts = [spans(place, size) for place, size in zip(source + target, block_shape + shapes[out])]
        (top, rows), (left, columns), (low, _), (first, _) = starts
        for i in range(0, rows, 32):
            for j in range(0, columns, 512):
                size = (min(32, rows - i), min(512, columns - j))
                place = lambda row, column: (pl.ds(row + i, size[0]), pl.ds(column + j, size[1]))
                yield out, place(top, left), place(low, first)


def sum_blocks(table, grads, relatives, received, views, passing=()):
    _, shapes, block_shape = views
    first = [None if relative is None else RELATIVES.index(relative) for relative in relatives]
    counts = [len(blocks) for blocks in received]
    flat = [block for blocks in received for block in blocks]
    vmem = pl.BlockSpec(memory_space=pltpu.VMEM)
    count = 1 + len(grads) + len(flat)
    return run(
        partial(sum_kernel, first, counts, views, len(passing)),
        grid=(),
        in_specs=[pl.BlockSpec(memory_space=pltpu.SMEM)]
        + [pl.BlockSpec(memory_space=pltpu.HBM)] * len(grads)
        + [vmem] * len(flat)
        + [ANYWHERE] * len(passing),
        out_specs=[vmem] * len(relatives) + [ANYWHERE] * len(passing),
        out_shape=[jax.ShapeDtypeStruct(block_shape, BF16)] * (len(relatives) + len(passing)),
        input_output_aliases={count + i: len(relatives) + i for i in range(len(passing))},
        scratch_shapes=[pltpu.VMEM((len(relatives),) + shape, BF16) for shape in shapes]
        + [pltpu.SemaphoreType.DMA((len(relatives), len(shapes)))],
        compiler_params=pltpu.CompilerParams(vmem_limit_bytes=8 << 20),
    )(table, *grads, *flat, *passing)


def finish_kernel(views, count, pieces, wholes, table_ref, *refs):
    grads, received = refs[: len(views[1])], refs[len(views[1]) : len(views[1]) + count]
    mine, other, *outs, total_ref = refs[len(views[1]) + count :]
    for out, source, target in pieces_of(views):
        total = grads[out][(0,) + target].astype(F32)
        for block in received:
            total += block[source].astype(F32)
        total_ref[source] = total
    core = table_ref[len(RELATIVES)]
    rows = mine.shape[0]
    at = 0
    for start, size in pieces:
        low, high = total_ref[:rows, start : start + size], total_ref[rows:, start : start + size]
        here = pl.ds(at, size)
        mine[:, here] = jnp.where(core == 0, low, high)
        other[:, here] = jnp.where(core == 0, high, low)
        at += size
    for out, (tall, parts) in zip(outs, wholes):
        at = 0
        for place in parts:
            size = place[0].size if tall else place[1].size
            out[(pl.ds(at, size), slice(None)) if tall else (slice(None), pl.ds(at, size))] = total_ref[place]
            at += size


class ScatterRounds:
    def __init__(self, table, grads, views):
        self.table, self.views = table, views
        self.grads = [in_hbm(grad) for grad in grads]
        self.arrived, self.made, self.due = {}, {}, []

    def ahead(self, *names, most=2):
        came = [self.arrived.pop(name, []) for name in names]
        self.arrived.update((name, blocks[most:]) for name, blocks in zip(names, came) if blocks[most:])
        came = [blocks[:most] for blocks in came]
        self.made.update(zip(names, sum_blocks(self.table, self.grads, names, came, self.views)))

    def step(self, number, others=()):
        moves = ROUNDS[len(ROUNDS) - 1 - number]
        names = [sent for _, _, sent in moves]
        ready = [name for name in names if name in self.made and name not in self.arrived]
        missing = [name for name in names if name not in ready]
        came = [[self.made[name]] if name in self.made else [] for name in missing]
        came = [blocks + self.arrived.pop(name, []) for blocks, name in zip(came, missing)]
        own = [None if name in self.made else name for name in missing]
        LAST.extend(self.due + list(others))
        blocks = sum_blocks(
            self.table, self.grads, own, came, self.views, [self.made[name] for name in ready]
        )
        self.made.update(zip(missing + ready, blocks))
        self.due = []
        for axis, target, sent in moves:
            self.due.append(lax.ppermute(self.made[sent], axis, ring(lax.axis_size(axis), -1)))
            self.arrived.setdefault(target, []).append(self.due[-1])

    def finish(self, core, pieces, wholes):
        own = (0, 0, 0)
        came = self.arrived.pop(own)
        rows = self.views[2][0] // 2
        shapes = [(rows, sum(size for _, size in pieces))] * 2 + [
            (sum(r.size for r, _ in parts), parts[0][1].size) if tall else (parts[0][0].size, sum(c.size for _, c in parts))
            for tall, parts in wholes
        ]
        blocks = [
            pl.BlockSpec((1,) + shape, lambda g, table: (table[0],) + (0,) * len(shape)) for shape in self.views[1]
        ]
        return run(
            partial(finish_kernel, self.views, len(came), pieces, wholes),
            grid_spec=dict(
                num_scalar_prefetch=1,
                grid=(1,),
                in_specs=blocks + [whole_block(block.shape) for block in came],
                out_specs=[whole_block(shape) for shape in shapes],
                scratch_shapes=[pltpu.VMEM(self.views[2], F32)],
            ),
            out_shape=[jax.ShapeDtypeStruct(shape, F32) for shape in shapes],
            compiler_params=pltpu.CompilerParams(vmem_limit_bytes=16 << 20),
        )(self.table, *self.grads, *came)


class ScatterRings:
    def __init__(self, table, grads, views):
        self.sums = scatter_rings(grads, views)
        self.views = views

    def ahead(self, *names, most=2):
        pass

    def step(self, number, others=()):
        pass

    def result(self):
        moves, _, block_shape = self.views
        block = jnp.zeros(block_shape, F32)
        for out, source, target in moves:
            block = block.at[source].set(self.sums[out][target])
        return block


def picked(width, core):
    source = lax.broadcasted_iota(jnp.int32, (256, 128), 0)
    target = lax.broadcasted_iota(jnp.int32, (256, 128), 1)
    wanted = (target // width) * (2 * width) + core * width + target % width
    return jnp.where(source == wanted, 1.0, 0.0).astype(BF16)


def pick_kernel(widths, core_ref, *refs):
    matrices, outs = refs[: len(widths)], refs[len(widths) :]
    core = core_ref[0]
    for out, wanted in zip(outs, (core, 1 - core)):
        at = 0
        for width, matrix in zip(widths, matrices):
            half = matrix.shape[1] // 2
            if width == half:
                out[:, at : at + half] = jnp.where(wanted == 0, matrix[:, :half], matrix[:, half:])
            else:
                choice = picked(width, wanted)
                for i in range(half // 128):
                    columns = dot(matrix[:, i * 256 : (i + 1) * 256], choice)
                    out[:, at + i * 128 : at + (i + 1) * 128] = columns.astype(BF16)
            at += half


def pack_kernel(half, core_ref, mine, other, emit, payload, block):
    rows, breadth = emit.shape
    core = core_ref[0]
    split = 3 * half
    last = half + mine.shape[1]
    for i, (own, its) in enumerate(((mine, other), (other, mine))):
        here = pl.ds(i * rows, rows)
        block[here, :split] = jnp.where(core == 0, own[:, :split], its[:, :split])
        block[here, split : split + half] = emit[:, i * half : (i + 1) * half]
        block[here, split + half : last] = jnp.where(core == 0, own[:, split:], its[:, split:])
    height = 2 * rows
    for i in range(payload.shape[0] // height):
        block[:, last + i * breadth : last + (i + 1) * breadth] = payload[i * height : (i + 1) * height, :]


def stack_kernel(*refs):
    for i, piece in enumerate(refs[:-1]):
        for device in range(refs[-1].shape[0]):
            refs[-1][device, i : i + 1, :] = piece[...]


def join_kernel(widths, core_ref, mine, other, *outs):
    core = core_ref[0]
    rows = mine.shape[0]
    at = 0
    for width, out in zip(widths, outs):
        half = out.shape[1] // 2
        low = jnp.where(core == 0, mine[:, at : at + half], other[:, at : at + half])
        high = jnp.where(core == 0, other[:, at : at + half], mine[:, at : at + half])
        if width == half:
            out[:, :half] = low
            out[:, half:] = high
        elif width == 128:
            for i in range(half // 128):
                out[:, i * 256 : i * 256 + 128] = low[:, i * 128 : (i + 1) * 128]
                out[:, i * 256 + 128 : (i + 1) * 256] = high[:, i * 128 : (i + 1) * 128]
        else:
            for i in range(half // 128):
                total = jnp.zeros((rows, 256), F32)
                for number, part in enumerate((low, high)):
                    rest = part[:, i * 128 : (i + 1) * 128]
                    for _ in range(3):
                        piece = rest.astype(BF16)
                        total += dot_back(piece, picked(width, number))
                        rest = rest - piece.astype(F32)
                out[:, i * 256 : (i + 1) * 256] = total
        at += half


def whole_call(kernel, shapes, scalar, operands, hbm=()):
    return run(
        kernel,
        grid=(1,),
        out_shape=shapes,
        in_specs=[pl.BlockSpec(memory_space=pltpu.SMEM)] + [whole_block(operand.shape) for operand in operands],
        out_specs=[whole_block(out.shape) for out in shapes],
        hbm=hbm,
        compiler_params=pltpu.CompilerParams(vmem_limit_bytes=16 << 20),
    )(scalar.astype(jnp.int32).reshape(1), *operands)


def sum_axis(block, axis, place):
    count = lax.axis_size(axis)
    me = lax.axis_index(axis)

    def part(step):
        return lax.dynamic_index_in_dim(block, lax.rem(me + step, count), place, keepdims=False)

    total = part(1)
    for step in range(2, count + 1):
        moved = lax.ppermute(total.astype(BF16), axis, ring(count, -1))
        total = moved.astype(F32) + part(step).astype(F32)
    return total


def sum_along_z(block):
    return lax.psum_scatter(block.astype(BF16), "z", scatter_dimension=0).astype(F32)


def scatter_rings(grads, views):
    sizes = tuple(lax.axis_size(axis) for axis in CHIPS)
    sums = []
    for grad in grads:
        block = grad.reshape(sizes + grad.shape[1:])
        sums.append(sum_along_z(sum_axis(sum_axis(block, "x", 1), "y", 1)))
    return sums


def dot(left, right):
    return jnp.dot(left, right, preferred_element_type=F32)


def dot_back(grad, weight):
    return lax.dot_general(grad, weight, (((1,), (1,)), ((), ())), preferred_element_type=F32)


def outer(left, right):
    return lax.dot_general(left, right, (((0,), (0,)), ((), ())), preferred_element_type=F32)


def norm_parts(rows):
    center = jnp.mean(rows, axis=-1, keepdims=True)
    deviation = rows - center
    variance = jnp.mean(deviation * deviation, axis=-1, keepdims=True)
    inverse = lax.rsqrt(variance + EPSILON)
    return deviation * inverse, inverse


def last_row(rows):
    return lax.broadcasted_iota(jnp.int32, rows.shape, 0) == rows.shape[0] - 1


def first_row(rows):
    return lax.broadcasted_iota(jnp.int32, rows.shape, 0) == 0


def both_kernel(core_ref, *refs):
    count = len(refs) // 3
    for i in range(count):
        refs[2 * count + i][...] = jnp.where(core_ref[0] == pl.program_id(0), refs[2 * i][...], refs[2 * i + 1][...])


def both_groups(core, *pairs):
    rows, breadth = pairs[0][0].shape
    return run(
        both_kernel,
        grid=(2,),
        in_specs=[pl.BlockSpec(memory_space=pltpu.SMEM)]
        + [pl.BlockSpec((rows, breadth), lambda g: (0, 0))] * (2 * len(pairs)),
        out_specs=[pl.BlockSpec((rows, breadth), lambda g: (g, 0))] * len(pairs),
        out_shape=[jax.ShapeDtypeStruct((2 * rows, breadth), pair[0].dtype) for pair in pairs],
        hbm=range(len(pairs)),
        compiler_params=pltpu.CompilerParams(vmem_limit_bytes=16 << 20),
    )(core.astype(jnp.int32).reshape(1), *(part for pair in pairs for part in pair))


def vectors_kernel(
    core_ref, norm1, shares1, decay, first, rate_ref, norm2, shares2, out
):
    core = core_ref[0]
    own_rows = out.shape[-1]
    devices = out.shape[0]
    rate = rate_ref[...]
    grad_decay = -rate * jnp.exp(-rate) * jnp.sum(decay[...], axis=0, keepdims=True)
    grad_first = jnp.sum(first[...], axis=0, keepdims=True)
    norms2 = jnp.where(core == 0, norm2[0], norm2[1])
    for device in range(devices):
        here = slice(device * own_rows, (device + 1) * own_rows)
        chip, owner = device // 2, device % 2
        out[device, 0:2, :] = norm1[0][:, here]
        out[device, 2:5, :] = shares1[:, here]
        channels = slice(chip * own_rows, (chip + 1) * own_rows)
        out[device, 5:6, :] = jnp.where(core == owner, grad_decay[:, channels], 0.0)
        out[device, 6:7, :] = jnp.where(core == owner, grad_first[:, channels], 0.0)
        out[device, 7:9, :] = norms2[:, here]
        out[device, 9:11, :] = shares2[:, here]


def vector_sums_kernel(parts, out):
    total = parts[0]
    for i in range(1, parts.shape[0]):
        total = total + parts[i]
    out[...] = total


def outer_kernel(left, right, out):
    out[...] = outer(left[...], right[...]).astype(BF16)


def outer_call(left, right):
    tokens, height = left.shape
    width = right.shape[1]
    block = min(512, width)
    return run(
        outer_kernel,
        grid=(width // block,),
        in_specs=[whole_block(left.shape), pl.BlockSpec((tokens, block), lambda i: (0, i))],
        out_specs=pl.BlockSpec((height, block), lambda i: (0, i)),
        out_shape=jax.ShapeDtypeStruct((height, width), BF16),
        hbm=(0,),
        compiler_params=pltpu.CompilerParams(vmem_limit_bytes=16 << 20),
    )(in_hbm(left), in_hbm(right))


def norm_mix_kernel(terms, behind, gain, bias, shares, *refs):
    rows = terms[0][...].astype(F32)
    for term in terms[1:]:
        rows = rows + term[...].astype(F32)
    outs = list(refs)
    if len(terms) > 1:
        outs.pop(0)[...] = rows
    zhat, inverse = norm_parts(rows)
    outs.pop(0)[...] = zhat.astype(BF16)
    outs.pop(0)[...] = inverse
    normed = zhat * gain[...] + bias[...]
    group = pl.program_id(0)
    before = jnp.where(group == 0, behind[:1, :], behind[1:, :])
    step = normed - jnp.where(first_row(normed), before, shift_rows(normed, 1))
    for i, out in enumerate(outs):
        out[...] = (normed - step * (1.0 - shares[i : i + 1, :])).astype(BF16)


def norm_mix(terms, behind, gain, bias, shares, hbm):
    rows, breadth = terms[0].shape
    block = pl.BlockSpec((rows // 2, breadth), lambda g: (g, 0))
    whole = lambda element: pl.BlockSpec(element.shape, lambda g: (0, 0))
    shape = lambda kind: jax.ShapeDtypeStruct((rows, breadth), kind)
    wide = [shape(F32)] * (len(terms) > 1) + [shape(BF16)]

    def body(*refs):
        norm_mix_kernel(refs[: len(terms)], *refs[len(terms) :])

    return run(
        body,
        grid=(2,),
        in_specs=[block] * len(terms) + [whole(element) for element in (behind, gain, bias, shares)],
        out_specs=[block] * len(wide)
        + [pl.BlockSpec((rows // 2, 1), lambda g: (g, 0))]
        + [block] * shares.shape[0],
        out_shape=wide + [jax.ShapeDtypeStruct((rows, 1), F32)] + [shape(BF16)] * shares.shape[0],
        hbm=hbm,
        compiler_params=pltpu.CompilerParams(vmem_limit_bytes=18 << 20),
    )(*terms, behind, gain, bias, shares)


def norm_back_kernel(count, table, *refs):
    parts = refs[:count]
    came, zhat_ref, inverse_ref, gain, base = refs[count : count + 5]
    outs = refs[count + 5 :]
    grad = parts[0][...].astype(F32)
    for part in parts[1:]:
        grad = grad + part[...].astype(F32)
    group = pl.program_id(0)
    grad = grad + jnp.where(last_row(grad), jnp.where(group == 0, came[:1, :], came[-1:, :]), 0.0)
    zhat = zhat_ref[...].astype(F32)
    scaled = grad * gain[...]
    middle = jnp.mean(scaled, axis=-1, keepdims=True)
    slope = jnp.mean(scaled * zhat, axis=-1, keepdims=True)
    total = base[...].astype(F32) + inverse_ref[...] * (scaled - middle - zhat * slope)
    for out in outs[:-1]:
        out[...] = total.astype(out.dtype)
    outs[-1][0, :1, :] = jnp.sum(grad * zhat, axis=0, keepdims=True)
    outs[-1][0, 1:, :] = jnp.sum(grad, axis=0, keepdims=True)


def norm_back(core, parts, came, zhat, inverse, gain, base, kinds, own):
    breadth = zhat.shape[1]
    rows = zhat.shape[0] // 2
    groups = 1 if own else 2
    pick = lambda width: pl.BlockSpec((rows, width), lambda g, table: (table[0] if own else g, 0))
    block = pl.BlockSpec((rows, breadth), lambda g, table: (g, 0))
    whole = lambda element: pl.BlockSpec(element.shape, lambda g, table: (0, 0))
    return run(
        partial(norm_back_kernel, len(parts)),
        grid_spec=dict(
            num_scalar_prefetch=1,
            grid=(groups,),
            in_specs=[block] * len(parts)
            + [whole(came), pick(breadth), pick(1), whole(gain), pick(breadth)],
            out_specs=[block] * len(kinds) + [pl.BlockSpec((1, 2, breadth), lambda g, table: (g, 0, 0))],
        ),
        out_shape=[jax.ShapeDtypeStruct((groups * rows, breadth), kind) for kind in kinds]
        + [jax.ShapeDtypeStruct((groups, 2, breadth), F32)],
        hbm=() if own else (0,),
        compiler_params=pltpu.CompilerParams(vmem_limit_bytes=16 << 20),
    )(core.astype(jnp.int32).reshape(1), *parts, came, zhat, inverse, gain, base)


def output_kernel(core_ref, part, swapped, gate_own, gate_other, cot_ref, middle, out, d_value, d_gate):
    core = core_ref[0]
    half = gate_own.shape[1]
    value = part[...].astype(F32) + swapped[...].astype(F32)
    cot = cot_ref[...].astype(F32)
    own, other = gate_own[...], gate_other[...]
    for i in range(2):
        gate = jnp.where(core == i, own, other)
        here = pl.ds(i * half, half)
        out[:, here] = (middle[:, here] + gate * value[:, i * half : (i + 1) * half]).astype(BF16)
        d_value[:, here] = (cot[:, i * half : (i + 1) * half] * gate).astype(BF16)
    mine = lambda rows: jnp.where(core == 0, rows[:, :half], rows[:, half:])
    d_gate[...] = (mine(cot) * mine(value) * own * (1.0 - own)).astype(BF16)


def output(core, part, swapped, gate_own, gate_other, cot, middle):
    rows, breadth = part.shape
    block = lambda width: pl.BlockSpec((rows // 2, width), lambda g: (g, 0))
    half = breadth // 2
    return run(
        output_kernel,
        grid=(2,),
        in_specs=[pl.BlockSpec(memory_space=pltpu.SMEM)]
        + [block(width) for width in (breadth, breadth, half, half, breadth, breadth)],
        out_specs=[block(breadth), block(breadth), block(half)],
        out_shape=[jax.ShapeDtypeStruct((rows, width), BF16) for width in (breadth, breadth, half)],
        compiler_params=pltpu.CompilerParams(vmem_limit_bytes=16 << 20),
    )(core.astype(jnp.int32).reshape(1), part, swapped, gate_own, gate_other, cot, middle)


def shift_rows(rows, distance):
    return pltpu.roll(rows, distance % rows.shape[0], 0)


def fade_tables(rate, reverse):
    breadth = rate.shape[-1]
    place = lax.broadcasted_iota(jnp.int32, (TILE, breadth), 0)
    if reverse:
        place = TILE - 1 - place
    steps = []
    distance = 1
    while distance < TILE:
        factor = jnp.where(place >= distance, jnp.exp(-rate * float(distance)), 0.0)
        steps.append((distance, factor))
        distance *= 2
    passed = jnp.exp(-rate * place.astype(F32))
    before = (place >= 1).astype(F32)
    return steps, passed, before


def scan_tile(terms, steps, reverse):
    for distance, factor in steps:
        terms = terms + factor * shift_rows(terms, -distance if reverse else distance)
    return terms


def wkv_kernel(
    groups, key_ref, value_ref, recept_ref, key_old, value_old, recept_old, rate_ref, bonus_ref, num_ref, den_ref,
    emit_ref, sent_ref, gated_ref, prior_num_ref, prior_den_ref,
):
    rows = key_ref.shape[0] // groups
    rate = rate_ref[...]
    bonus = bonus_ref[...]
    steps, passed, before = fade_tables(rate, False)
    tile_fade = jnp.exp(-rate * float(TILE))

    def body(index, carry):
        states = []
        for group in range(groups):
            num, den = carry[2 * group], carry[2 * group + 1]
            at = pl.ds(pl.multiple_of(group * rows + index * TILE, TILE), TILE)
            grown = jnp.exp(key_ref[at, :].astype(F32))
            product = grown * value_ref[at, :].astype(F32)
            inner_num = scan_tile(product, steps, False)
            inner_den = scan_tile(grown, steps, False)
            prior_num = shift_rows(inner_num, 1) * before + passed * num
            prior_den = shift_rows(inner_den, 1) * before + passed * den
            prior_num_ref[at, :] = prior_num
            prior_den_ref[at, :] = prior_den
            wkv = (prior_num + bonus * product) / (prior_den + bonus * grown)
            gated_ref[at, :] = (recept_ref[at, :] * wkv.astype(BF16).astype(F32)).astype(BF16)
            states.append(inner_num[TILE - 1 :, :] + tile_fade * num)
            states.append(inner_den[TILE - 1 :, :] + tile_fade * den)
        return tuple(states)

    start = []
    for group in range(groups):
        start += [num_ref[group : group + 1, :], den_ref[group : group + 1, :]]
    lax.fori_loop(0, rows // TILE, body, tuple(start))
    attended = dot(gated_ref[...], emit_ref[...])
    sent_ref[: groups * rows, :] = attended.astype(BF16)
    pad = lambda ref: jnp.concatenate([ref[...], jnp.zeros((TILE - groups, rate.shape[-1]), F32)], axis=0)
    grown = jnp.exp(key_old[...].astype(F32))
    product = grown * value_old[...].astype(F32)
    unfade = jnp.exp(rate)
    num = (pad(num_ref) - product) * unfade + bonus * product
    den = (pad(den_ref) - grown) * unfade + bonus * grown
    old = (recept_old[...] * (num / den).astype(BF16).astype(F32)).astype(BF16)
    attended = dot(old, emit_ref[...])
    sent_ref[groups * rows :, :] = attended.astype(BF16)


def wkv_back_kernel(
    groups, key_ref, value_ref, prior_num_ref, prior_den_ref, weighted_ref, rate_ref, bonus_ref,
    num_ref, den_ref, dkey_ref, dvalue_ref, decay_ref, first_ref,
):
    rows = key_ref.shape[0] // groups
    rate = rate_ref[...]
    bonus = bonus_ref[...]
    steps, passed, before = fade_tables(rate, True)
    tile_fade = jnp.exp(-rate * float(TILE))
    decay_ref[...] = jnp.zeros_like(decay_ref)
    first_ref[...] = jnp.zeros_like(first_ref)

    def body(step, carry):
        index = rows // TILE - 1 - step
        states = []
        for group in range(groups):
            num, den = carry[2 * group], carry[2 * group + 1]
            at = pl.ds(pl.multiple_of(group * rows + index * TILE, TILE), TILE)
            grown = jnp.exp(key_ref[at, :].astype(F32))
            value = value_ref[at, :].astype(F32)
            prior_num = prior_num_ref[at, :]
            prior_den = prior_den_ref[at, :]
            wkv_den = prior_den + bonus * grown
            wkv = (prior_num + bonus * grown * value) / wkv_den
            grad = weighted_ref[at, :].astype(F32) / wkv_den
            inner_num = scan_tile(grad, steps, True)
            inner_den = scan_tile(-grad * wkv, steps, True)
            lam_num = shift_rows(inner_num, -1) * before + passed * num
            lam_den = shift_rows(inner_den, -1) * before + passed * den
            bonus_grad = bonus * grad
            dvalue_ref[at, :] = (grown * (bonus_grad + lam_num)).astype(BF16)
            direct = bonus_grad * (value - wkv)
            dkey_ref[at, :] = (grown * (direct + lam_num * value + lam_den)).astype(BF16)
            first_ref[...] += grown * direct
            decay_ref[...] += lam_num * prior_num + lam_den * prior_den
            states.append(inner_num[:1, :] + tile_fade * num)
            states.append(inner_den[:1, :] + tile_fade * den)
        return tuple(states)

    start = []
    for group in range(groups):
        start += [num_ref[group : group + 1, :], den_ref[group : group + 1, :]]
    lax.fori_loop(0, rows // TILE, body, tuple(start))


def wkv_start_kernel(
    groups, grad_ref, recept_ref, key_ref, value_ref, prior_num_ref, prior_den_ref, rate_ref, bonus_ref,
    weighted_ref, accept_ref, begin_ref,
):
    rows = key_ref.shape[0] // groups
    rate = rate_ref[...]
    bonus = bonus_ref[...]
    place = lax.broadcasted_iota(jnp.int32, (TILE, rate.shape[-1]), 0).astype(F32)
    tile_fade = jnp.exp(-rate * float(TILE))

    def body(index, carry):
        fade, sums = carry[0], []
        for group in range(groups):
            at = pl.ds(pl.multiple_of(group * rows + index * TILE, TILE), TILE)
            grown = bonus * jnp.exp(key_ref[at, :].astype(F32))
            wkv_den = prior_den_ref[at, :] + grown
            wkv = (prior_num_ref[at, :] + grown * value_ref[at, :].astype(F32)) / wkv_den
            recept = recept_ref[at, :]
            grad = grad_ref[at, :]
            kept = grad * recept
            weighted = kept.astype(BF16)
            weighted_ref[at, :] = weighted
            accept_ref[at, :] = (kept * wkv.astype(BF16).astype(F32) * (1.0 - recept)).astype(BF16)
            faded = fade * (weighted.astype(F32) / wkv_den)
            sums += [carry[1 + 2 * group] + faded, carry[2 + 2 * group] - faded * wkv]
        return (fade * tile_fade, *sums)

    zero = jnp.zeros((TILE, rate.shape[-1]), F32)
    _, *sums = lax.fori_loop(0, rows // TILE, body, (jnp.exp(-rate * place),) + (zero,) * (2 * groups))
    for group in range(groups):
        for i in range(2):
            begin_ref[i, group : group + 1, :] = jnp.sum(sums[2 * group + i], axis=0, keepdims=True)


def keys_start_kernel(chips, table, *refs):
    mixes, befores, weights = refs[:3], refs[3:6], refs[6:9]
    parts, lates, held = refs[9:12], refs[12:15], refs[15]
    height = lates[0].shape[1] // max(len(chips), 1)
    breadth = held.shape[0]
    tokens = mixes[0].shape[0]
    for i in range(3):
        held[...] = weights[i][...]
        for chip in chips:
            here = pl.ds(pl.multiple_of(table[chip] * height, height), height)
            held[here, :] = jnp.zeros((height, held.shape[1]), BF16)
        for rows, mixed in ((pl.ds(0, tokens), mixes[i]), (pl.ds(tokens, TILE), befores[i])):
            parts[i][rows, :] = dot(mixed[...], held[...])

    @pl.when(pl.program_id(0) == 0)
    def _():
        row = lax.broadcasted_iota(jnp.int32, (breadth, lates[0].shape[1]), 0)
        column = lax.broadcasted_iota(jnp.int32, (breadth, lates[0].shape[1]), 1)
        start = jnp.zeros_like(column)
        for j, chip in enumerate(chips):
            start = jnp.where(column // height == j, table[chip] * height, start)
        chosen = jnp.where(row == start + column % height, 1.0, 0.0).astype(BF16)
        for i in range(3):
            for rows, mixed in ((pl.ds(0, tokens), mixes[i]), (pl.ds(tokens, TILE), befores[i])):
                lates[i][rows, :] = dot(mixed[...], chosen).astype(BF16)


def keys_end_kernel(groups, blocks, *refs):
    parts, lates, late = refs[:3], refs[3:6], refs[6 : 6 + 3 * blocks]
    rate = refs[6 + 3 * blocks]
    *outs, ends = refs[7 + 3 * blocks :]
    tokens = outs[0].shape[0]
    for i in range(3):
        product = parts[i][...]
        if blocks:
            rows = jnp.concatenate([block[...] for block in late[i * blocks : (i + 1) * blocks]], axis=0)
            product = product + dot(lates[i][...], rows)
        if i == 2:
            product = jax.nn.sigmoid(product)
        outs[i][...] = product[:tokens].astype(outs[i].dtype)
        outs[3 + i][...] = product[tokens:].astype(outs[i].dtype)
    keys, values = outs[:2]
    rows = tokens // groups
    left = (rows - 1 - lax.broadcasted_iota(jnp.int32, (rows, keys.shape[1]), 0)).astype(F32)
    fades = jnp.exp(-rate[...] * left)
    for group in range(groups):
        here = pl.ds(group * rows, rows)
        grown = jnp.exp(keys[here, :].astype(F32)) * fades
        ends[0, group : group + 1, :] = jnp.sum(grown * values[here, :].astype(F32), axis=0, keepdims=True)
        ends[1, group : group + 1, :] = jnp.sum(grown, axis=0, keepdims=True)


def keys_start(table, mixes, befores, weights, chips):
    rows, breadth = mixes[0].shape
    columns = weights[0].shape[1]
    block = min(256, columns)
    late = max(len(chips), 1) * (breadth // lax.axis_size(CHIPS))
    wide = lambda height: pl.BlockSpec((height, block), lambda i, table: (0, i))
    return run(
        partial(keys_start_kernel, chips),
        grid_spec=dict(
            num_scalar_prefetch=1,
            grid=(columns // block,),
            in_specs=[whole_block((rows, breadth))] * 3 + [whole_block((TILE, breadth))] * 3 + [wide(breadth)] * 3,
            out_specs=[wide(rows + TILE)] * 3 + [whole_block((rows + TILE, late))] * 3,
            scratch_shapes=[pltpu.VMEM((breadth, block), BF16)],
        ),
        out_shape=[jax.ShapeDtypeStruct((rows + TILE, columns), F32)] * 3
        + [jax.ShapeDtypeStruct((rows + TILE, late), BF16)] * 3,
        hbm=range(6),
        compiler_params=pltpu.CompilerParams(vmem_limit_bytes=24 << 20),
    )(table, *mixes, *befores, *map(in_hbm, weights))


def keys_end(started, blocks, rate):
    rows, columns = started[0].shape
    block = min(256, columns)
    steps = columns // block
    wide = lambda height: pl.BlockSpec((height, block), lambda i: (0, i))
    part = lambda number: pl.BlockSpec((blocks[0].shape[0], block), lambda i: (0, number * steps + i))
    shape = lambda height, kind: jax.ShapeDtypeStruct((height, columns), kind)
    kinds = (BF16, BF16, F32)
    return run(
        partial(keys_end_kernel, 2, len(blocks)),
        grid=(steps,),
        in_specs=[wide(rows)] * 3
        + [whole_block(started[3].shape)] * 3
        + [part(number) for number in range(3) for _ in blocks]
        + [wide(1)],
        out_specs=[wide(rows - TILE)] * 3 + [wide(TILE)] * 3 + [pl.BlockSpec((2, 2, block), lambda i: (0, 0, i))],
        out_shape=[shape(rows - TILE, kind) for kind in kinds]
        + [shape(TILE, kind) for kind in kinds]
        + [jax.ShapeDtypeStruct((2, 2, columns), F32)],
        hbm=(0, 1, 2),
        compiler_params=pltpu.CompilerParams(vmem_limit_bytes=24 << 20),
    )(*started, *(list(blocks) * 3), rate)


def wkv_call(kernel, groups, shapes, operands, hbm=(), vmem=()):
    return run(
        partial(kernel, groups),
        out_shape=shapes,
        in_specs=[whole_block(operand.shape) for operand in operands],
        out_specs=[whole_block(out.shape) for out in shapes],
        hbm=hbm,
        vmem=vmem,
        compiler_params=pltpu.CompilerParams(vmem_limit_bytes=14 << 20),
    )(*operands)


def mix_back_kernel(groups, count, core_ref, *refs):
    grads = refs[:count]
    zhat, behind, gain, bias, shares = refs[count : count + 5]
    *parts, first, sums = refs[count + 5 :]
    rows = zhat.shape[0] // groups
    totals = [0.0] * count
    for group in range(groups):
        here = pl.ds(group * rows, rows)
        normed = zhat[here, :].astype(F32) * gain[...] + bias[...]
        step = normed - jnp.where(first_row(normed), behind[group : group + 1, :], shift_rows(normed, 1))
        direct, shifted = 0.0, 0.0
        for i in range(count):
            grad = grads[i][here, :].astype(F32)
            moved = grad * (1.0 - shares[i : i + 1, :])
            direct += grad - moved
            shifted += moved
            totals[i] += jnp.sum(grad * step, axis=0, keepdims=True)
        first[group : group + 1, :] = shifted[:1, :]
        part = direct + jnp.where(last_row(shifted), 0.0, shift_rows(shifted, -1))
        if parts[0].shape == zhat.shape:
            parts[0][here, :] = part.astype(BF16)
        else:
            for i in range(2):

                @pl.when((core_ref[0] == group) == (i == 0))
                def _():
                    parts[i][...] = part.astype(parts[i].dtype)
    for i in range(count):
        sums[i : i + 1, :] = totals[i]


def mix_back(core, grads, zhat, behind, gain, bias, shares, apart):
    rows, breadth = zhat.shape
    count = len(grads)
    block = min(256, breadth)
    column = lambda height: pl.BlockSpec((height, block), lambda i: (0, i))
    outs = [(rows // 2, BF16)] * 2 if apart else [(rows, BF16)]
    outs += [(2, F32), (count, F32)]
    return run(
        partial(mix_back_kernel, 2, count),
        grid=(breadth // block,),
        in_specs=[pl.BlockSpec(memory_space=pltpu.SMEM)]
        + [column(rows)] * (count + 1)
        + [column(2), column(1), column(1), column(count)],
        out_specs=[column(height) for height, _ in outs],
        out_shape=[jax.ShapeDtypeStruct((height, breadth), kind) for height, kind in outs],
        compiler_params=pltpu.CompilerParams(vmem_limit_bytes=14 << 20),
    )(core.astype(jnp.int32).reshape(1), *grads, zhat, behind, gain, bias, shares)


def per_device(
    layer_incoming,
    series_extents,
    emitted_adjoint,
    norm1_scaling,
    norm1_offset,
    mixer_lookup_portion,
    mixer_payload_portion,
    mixer_accept_portion,
    temporal_fading_log,
    present_step_reward,
    mixer_lookup_matrix,
    mixer_payload_matrix,
    mixer_accept_matrix,
    mixer_emit_matrix,
    norm2_scaling,
    norm2_offset,
    feedforward_lookup_portion,
    feedforward_accept_portion,
    feedforward_lookup_matrix,
    feedforward_payload_matrix,
    feedforward_accept_matrix,
):
    LAST.clear()
    HELD.clear()
    devices = lax.axis_size(ALL)
    chips = lax.axis_size(CHIPS)
    parts = lax.axis_size(SEQ)
    core = lax.axis_index("c")
    place = lax.axis_index(SEQ)
    rows, breadth = layer_incoming.shape[1:]
    own_rows = mixer_lookup_matrix.shape[0]
    hidden_rows = feedforward_payload_matrix.shape[0]

    half = breadth // 2
    hidden = feedforward_lookup_matrix.shape[1] // 2
    both = lambda own, other: jnp.where(core == 0, jnp.stack([own, other]), jnp.stack([other, own]))
    mine_of = lambda pair: lax.dynamic_index_in_dim(pair, core, 0, keepdims=False)
    other_of = lambda pair: lax.dynamic_index_in_dim(pair, 1 - core, 0, keepdims=False)
    pair_rows = 2 * own_rows
    every = slice(None)
    mix_views = (
        tuple((i, (every, pl.ds(i * half, half)), (every, every)) for i in range(3))
        + tuple(
            (3, (pl.ds(i * own_rows, own_rows), pl.ds(3 * half, half)), (every, pl.ds(i * half, half)))
            for i in range(2)
        )
        + ((4, (every, pl.ds(4 * half, half)), (every, every)),),
        ((pair_rows, half),) * 3 + ((own_rows, breadth), (pair_rows, half)),
        (pair_rows, 5 * half),
    )
    stack = hidden_rows // pair_rows
    ffn_views = (
        ((0, (every, pl.ds(0, hidden)), (every, every)),)
        + tuple(
            (1, (every, pl.ds(hidden + i * breadth, breadth)), (pl.ds(i * pair_rows, pair_rows), every))
            for i in range(stack)
        ),
        ((pair_rows, hidden), (hidden_rows, breadth)),
        (pair_rows, hidden + stack * breadth),
    )
    gather_views = (
        mix_views[0]
        + tuple(
            (5 + out, (every, pl.ds(5 * half + source[1].start, source[1].size)), target)
            for out, source, target in ffn_views[0]
        ),
        mix_views[1] + ffn_views[1],
        (pair_rows, 5 * half + ffn_views[2][1]),
    )

    begins = jnp.cumsum(series_extents[0]) - series_extents[0]
    starts = jnp.any(jnp.arange(parts)[:, None] * rows == begins[None, :], axis=1)
    joined = jnp.where(starts, 0.0, 1.0).astype(F32)
    joined = both(joined, swap(joined))

    own_in, own_cot = in_hbm(layer_incoming[0]), in_hbm(emitted_adjoint[0])
    ends_of = lambda element: element.reshape(2, rows, -1)[:, rows - 2 :]

    rounds = in_rounds()
    table = chip_table() if rounds else jnp.zeros((1,), jnp.int32)
    split_up = (
        mixer_lookup_matrix, mixer_payload_matrix, mixer_accept_matrix,
        feedforward_accept_matrix, feedforward_lookup_matrix,
    )
    widths = (own_rows, own_rows, own_rows, half, hidden_rows)
    picks = jax.ShapeDtypeStruct((own_rows, 4 * half + hidden), BF16)
    both_inputs = lambda: both_groups(core, (own_in, swap(own_in)), (own_cot, swap(own_cot)))
    if rounds:
        mine, other = whole_call(partial(pick_kernel, widths), (picks, picks), core, tuple(map(in_hbm, split_up)))
        other = swap(other)
        (block,) = whole_call(
            partial(pack_kernel, half), [jax.ShapeDtypeStruct(gather_views[2], BF16)],
            core, (mine, other, in_hbm(mixer_emit_matrix), in_hbm(feedforward_payload_matrix)),
        )
    else:
        halves = jnp.concatenate(
            [
                matrix.reshape(own_rows, -1, 2, width).transpose(2, 0, 1, 3).reshape(2, own_rows, -1)
                for matrix, width in zip(split_up, widths)
            ],
            axis=-1,
        )
        pair = both(mine_of(halves), swap(other_of(halves))).reshape(pair_rows, -1)
        emit = jnp.concatenate([mixer_emit_matrix[:, :half], mixer_emit_matrix[:, half:]], axis=0)
        payload = [feedforward_payload_matrix[i * pair_rows : (i + 1) * pair_rows] for i in range(stack)]
        block = jnp.concatenate([pair[:, : 3 * half], emit, pair[:, 3 * half :], *payload], axis=1)
    Gather, Scatter = (GatherRounds, ScatterRounds) if rounds else (GatherRings, ScatterRings)
    weights = Gather(table, block, gather_views)
    weights.step(0)
    inputs, cotangent = both_inputs()
    weights.place(-1)
    pieces = (
        norm1_scaling, norm1_offset, mixer_lookup_portion, mixer_payload_portion,
        mixer_accept_portion, norm2_scaling, norm2_offset, feedforward_lookup_portion,
        feedforward_accept_portion, temporal_fading_log, present_step_reward,
    )
    pieces = [piece.reshape(1, own_rows) for piece in pieces]
    vectors = run(
        stack_kernel,
        out_shape=jax.ShapeDtypeStruct((devices, len(pieces), own_rows), BF16),
        in_specs=[whole_block(piece.shape) for piece in pieces],
        out_specs=whole_block((devices, len(pieces), own_rows)),
    )(*pieces)
    vectors = lax.all_to_all(vectors, ALL, 0, 0, tiled=True)
    (edge,) = hold(ends_of(inputs))
    behind = along_seq(edge, 1)
    LAST.append(joined)
    weights.step(1)
    LAST.extend([behind, vectors])
    weights.step(2)
    weights.place(0)

    vectors = vectors.astype(F32).transpose(1, 0, 2)
    channel = lax.dynamic_index_in_dim(
        vectors[9:].reshape(2, chips, 2, own_rows), core, 2, keepdims=False
    ).reshape(2, 1, -1)
    vectors = vectors[:9].reshape(9, breadth)
    gain1, bias1, shares1, gain2, bias2, shares2 = (
        vectors[start:stop] for start, stop in ((0, 1), (1, 2), (2, 5), (5, 6), (6, 7), (7, 9))
    )
    rate, bonus = jnp.exp(channel[0]), jnp.exp(channel[1])

    keep = lax.dynamic_index_in_dim(joined, place, 1)[:, :, None]
    index = jnp.arange(parts)
    began = jnp.where((joined == 0.0) & (index[None] <= place), index[None], -1).max(axis=1)
    reach = ((index[None] < place) & (index[None] >= began[:, None])).astype(F32)
    begun = jnp.where((joined == 0.0) & (index[None] > place), index[None], parts).min(axis=1)
    reach_back = ((index[None] > place) & (index[None] < begun[:, None])).astype(F32)

    def entering(ends, reached, distance):
        fades = jnp.exp(-rate[None] * (float(rows) * jnp.maximum(distance, 0).astype(F32))[:, None, None])
        return jnp.sum(ends * (reached.T[:, None, :, None] * fades[:, :, None]), axis=0)

    def spread(ends):
        return lax.all_to_all(
            jnp.broadcast_to(ends[None], (parts,) + ends.shape), SEQ, 0, 0, tiled=True
        )

    weights.place(1)
    behind = behind.astype(F32)
    normed_before = norm_parts(behind)[0] * gain1 + bias1
    step_before = normed_before[:, 1] - normed_before[:, 0]
    mixed_before = [
        jnp.pad(normed_before[:, 1] - step_before * (1.0 - shares1[i : i + 1]), ((0, TILE - 2), (0, 0))).astype(BF16)
        for i in range(3)
    ]
    behind1 = normed_before[:, 1] * keep[:, 0]
    zhat1, inverse1, mixed_k, mixed_v, mixed_r = norm_mix(
        [inputs], behind1, gain1, bias1, shares1, range(5)
    )
    weights.step(3)
    weights.place(2)
    weights.step(4)
    weights.place(3)
    whole = lambda held: held.reshape(-1, held.shape[-1])
    weight_k, weight_v, weight_r, *_ = map(whole, weights.held)
    chips_late, blocks_late = weights.last_blocks()
    started = keys_start(
        table, (mixed_k, mixed_v, mixed_r), mixed_before, (weight_k, weight_v, weight_r), chips_late
    )
    keys, values, recept, *before, ends = keys_end(started, blocks_late, rate)
    weights.place(4)
    weight_k, weight_v, weight_r, weight_o, weight_fr, weight_fk, weight_fv = map(whole, weights.held)

    enter = entering(spread(ends), reach, place - 1 - index)
    shape = lambda kind: jax.ShapeDtypeStruct((2 * rows, half), kind)
    sent, gated, prior_num, prior_den = wkv_call(
        wkv_kernel, 2,
        (
            jax.ShapeDtypeStruct((2 * rows + TILE, breadth), BF16),
            shape(BF16), shape(F32), shape(F32),
        ),
        (keys, values, recept, *before, rate, bonus, enter[0], enter[1], in_hbm(weight_o)), (1, 2, 3),
    )
    swapped = swap(sent)
    HELD.append((swapped, pltpu.HBM))
    before2 = behind[:, 1] + (sent[2 * rows :].astype(F32) + swapped[2 * rows :].astype(F32))[:2]
    behind2 = (norm_parts(before2)[0] * gain2 + bias2) * keep[:, 0]
    middle, zhat2, inverse2, ffn_k, ffn_r = norm_mix(
        [inputs, sent, swapped], behind2, gain2, bias2, shares2, ()
    )
    gate_own = jax.nn.sigmoid(dot(ffn_r, weight_fr))
    gate_other = swap(gate_own)
    pre_hidden = jax.nn.relu(dot(ffn_k, weight_fk))
    hidden_act = jnp.square(pre_hidden).astype(BF16)
    value_part = dot(hidden_act, weight_fv).astype(BF16)
    block_output, d_value_out, d_gate_pre = output(
        core, value_part, swap(value_part), gate_own, gate_other, cotangent, middle
    )
    block_output = mine_of(block_output.reshape(2, rows, breadth))

    d_hidden = dot_back(d_value_out, weight_fv)
    d_pre_hidden = (d_hidden * 2.0 * pre_hidden).astype(BF16)
    low_back = lambda grad, weight: dot_back(grad, weight).astype(BF16)

    def came_back(first):
        return along_seq((first + swap(first)) * keep[:, 0], -1)

    part2, first2, share_grads2 = mix_back(
        core, (low_back(d_pre_hidden, weight_fk), low_back(d_gate_pre, weight_fr)),
        zhat2, behind2, gain2, bias2, shares2, False,
    )
    grad_fr = outer(ffn_r, d_gate_pre).astype(BF16)
    grad_fv = outer_call(hidden_act, d_value_out)
    swapped2 = swap(part2)
    HELD.append((swapped2, pltpu.HBM))
    d_middle, d_attended, norm_grads2 = norm_back(
        core, (part2, swapped2), came_back(first2), zhat2, inverse2, gain2, cotangent,
        (F32, BF16), False,
    )

    grad_o = outer(gated, d_attended).astype(BF16)
    d_gated = dot_back(d_attended, weight_o)
    d_weighted, d_recept_pre, begins_back = wkv_call(
        wkv_start_kernel, 2,
        (shape(BF16), shape(BF16), jax.ShapeDtypeStruct((2, 2, half), F32)),
        (d_gated, recept, keys, values, prior_num, prior_den, rate, bonus),
    )
    grad_fk = outer_call(ffn_k, d_pre_hidden)
    enter_back = entering(spread(begins_back), reach_back, index - place - 1)
    small = jax.ShapeDtypeStruct((TILE, half), F32)
    d_keys, d_values, decay_sum, bonus_sum = wkv_call(
        wkv_back_kernel, 2, (shape(BF16), shape(BF16), small, small),
        (keys, values, prior_num, prior_den, d_weighted, rate, bonus, enter_back[0], enter_back[1]),
    )
    grad_k = outer(mixed_k, d_keys).astype(BF16)
    grad_v = outer(mixed_v, d_values).astype(BF16)
    grad_r = outer(mixed_r, d_recept_pre).astype(BF16)
    per_chip = lambda grad: grad.reshape(chips, -1, grad.shape[-1])
    scatter = Scatter(
        table,
        [per_chip(grad) for grad in (grad_k, grad_v, grad_r, grad_o, grad_fr, grad_fk, grad_fv)],
        gather_views,
    )
    scatter.step(0)
    scatter.ahead((3, 0, 1), (2, 0, 1), (1, 1, 0))
    own1, other1, first1, share_grads1 = mix_back(
        core,
        (low_back(d_keys, weight_k), low_back(d_values, weight_v), low_back(d_recept_pre, weight_r)),
        zhat1, behind1, gain1, bias1, shares1, True,
    )
    swapped1 = swap(other1)
    first_sum = (first1 + swap(first1)) * keep[:, 0]
    scatter.step(1, [swapped1, first_sum])
    scatter.ahead((2, 0, 0), (1, 0, 1), (0, 1, 0))
    came1 = along_seq(first_sum, -1)
    scatter.step(2, [came1])
    scatter.ahead((0, 1, 1))
    input_grad, norm_grads1 = norm_back(
        core, (own1, swapped1), mine_of(came1[:, None]), zhat1, inverse1, gain1, d_middle, (F32,), True
    )
    pieces = (norm_grads1, share_grads1, decay_sum, bonus_sum, rate, norm_grads2, share_grads2)
    grads = run(
        vectors_kernel,
        out_shape=jax.ShapeDtypeStruct((devices, 11, own_rows), F32),
        in_specs=[pl.BlockSpec(memory_space=pltpu.SMEM)] + [whole_block(piece.shape) for piece in pieces],
        out_specs=whole_block((devices, 11, own_rows)),
    )(core.astype(jnp.int32).reshape(1), *pieces)
    scatter.step(3)
    scatter.ahead((1, 0, 0), most=1)
    scatter.step(4)
    (grads,) = hold(grads)
    grads = lax.all_to_all(grads, ALL, 0, 0, tiled=True)
    grads = run(
        vector_sums_kernel,
        out_shape=jax.ShapeDtypeStruct((11, own_rows), F32),
        in_specs=[whole_block(grads.shape)],
        out_specs=whole_block((11, own_rows)),
    )(grads)

    widths = [(half, own_rows)] * 3 + [(half, half), (hidden, hidden_rows)]
    emit_at = [(pl.ds(i * own_rows, own_rows), pl.ds(3 * half, half)) for i in range(2)]
    payload_at = [(pl.ds(0, pair_rows), pl.ds(5 * half + hidden + i * breadth, breadth)) for i in range(stack)]
    columns = [(0, 3 * half), (4 * half, half + hidden)]
    if rounds:
        mine, other, sum_o, sum_fv = scatter.finish(core, columns, [(False, emit_at), (True, payload_at)])
        other = swap(other)
        outs = [jax.ShapeDtypeStruct((own_rows, 2 * size), F32) for size, _ in widths]
        sum_k, sum_v, sum_r, sum_fr, sum_fk = whole_call(
            partial(join_kernel, [width for _, width in widths]), outs, core, (mine, other)
        )
    else:
        total = scatter.result()
        pair = jnp.concatenate([total[:, start : start + size] for start, size in columns], axis=1)
        pair = pair.reshape(2, own_rows, -1)
        mine, other = mine_of(pair), swap(other_of(pair))
        low, high = jnp.where(core == 0, mine, other), jnp.where(core == 0, other, mine)
        outs, at = [], 0
        for size, width in widths:
            pieces = [piece[:, at : at + size].reshape(own_rows, -1, 1, width) for piece in (low, high)]
            outs.append(jnp.concatenate(pieces, axis=2).reshape(own_rows, 2 * size))
            at += size
        sum_k, sum_v, sum_r, sum_fr, sum_fk = outs
        sum_o = jnp.concatenate([total[at] for at in emit_at], axis=1)
        sum_fv = jnp.concatenate([total[at] for at in payload_at], axis=0)

    return (
        block_output[None],
        input_grad[None],
        *(grads[i] for i in range(7)),
        sum_k,
        sum_v,
        sum_r,
        sum_o,
        *(grads[i] for i in range(7, 11)),
        sum_fk,
        sum_fv,
        sum_fr,
    )


def solution(mesh):
    parts, groups = mesh.shape["seq"], mesh.shape["rep"]
    width = groups // 2
    fine = Mesh(mesh.devices.reshape(parts // width, width, width, 2), ALL)
    tokens = P(("y", "c"), SEQ, None)
    vector = P(ALL)
    matrix = P(ALL, None)
    return jax.shard_map(
        per_device,
        mesh=fine,
        in_specs=(
            (tokens, P(("y", "c"), None), tokens)
            + (vector,) * 7
            + (matrix,) * 4
            + (vector,) * 4
            + (matrix,) * 3
        ),
        out_specs=(
            (tokens, tokens) + (vector,) * 7 + (matrix,) * 4 + (vector,) * 4 + (matrix,) * 3
        ),
        check_vma=False,
    )
```

```python
from functools import partial

import jax
import jax.numpy as jnp
from jax import lax
from jax.experimental import pallas as pl
from jax.experimental.pallas import tpu as pltpu
from jax.sharding import Mesh, PartitionSpec as P

EPSILON = 1e-05
F32 = jnp.float32
BF16 = jnp.bfloat16
CHIPS = ("z", "x", "y")
SEQ = ("z", "x")
ALL = ("z", "x", "y", "c")
TILE = 16
FREE = pl.CostEstimate(flops=0, bytes_accessed=0, transcendentals=0)


def ring(count, step=1):
    return [(i, (i + step) % count) for i in range(count)]


def swap(block):
    return lax.ppermute(block, "c", ring(2))


def along_seq(block, step):
    count = lax.axis_size(SEQ)
    pairs = [(i, i + step) for i in range(count) if 0 <= i + step < count]
    return lax.ppermute(block, SEQ, pairs)


ROUNDS = (
    (("z", (0, 0, 0), (1, 0, 0)), ("y", (0, 0, 0), (0, 0, 1)), ("x", (0, 0, 0), (0, 1, 0))),
    (("z", (1, 0, 0), (2, 0, 0)), ("y", (1, 0, 0), (1, 0, 1)), ("x", (0, 0, 1), (0, 1, 1))),
    (("z", (2, 0, 0), (3, 0, 0)), ("y", (2, 0, 0), (2, 0, 1)), ("x", (1, 0, 0), (1, 1, 0))),
    (("z", (0, 1, 1), (1, 1, 1)), ("y", (3, 0, 0), (3, 0, 1)), ("x", (3, 0, 0), (3, 1, 0))),
    (("z", (1, 1, 1), (2, 1, 1)), ("y", (3, 1, 0), (3, 1, 1)), ("x", (2, 0, 0), (2, 1, 0))),
)


def in_rounds():
    return tuple(lax.axis_size(axis) for axis in CHIPS) == (4, 2, 2)


RELATIVES = tuple((z, x, y) for z in range(4) for x in range(2) for y in range(2))
ANYWHERE = pl.BlockSpec(memory_space=pl.ANY)


def chip_table():
    whole = jnp.asarray(RELATIVES, jnp.int32)
    total = jnp.zeros((len(RELATIVES),), jnp.int32)
    for i, axis in enumerate(CHIPS):
        count = lax.axis_size(axis)
        total = total * count + lax.rem(lax.axis_index(axis) + (count - whole[:, i]), count)
    return jnp.concatenate([total, lax.axis_index("c")[None]]).astype(jnp.int32)


def whole_block(shape):
    return pl.BlockSpec(shape, lambda *g: (0,) * len(shape))


def in_hbm(array):
    return pltpu.with_memory_space_constraint(array, pltpu.HBM)


LAST = []
HELD = []


def where_it_is(array):
    kinds = [kind for held, kind in HELD if held is array]
    return pltpu.with_memory_space_constraint(array, kinds[0]) if kinds else array


def run(
    kernel, *, out_shape, grid=(1,), in_specs=None, out_specs=None, grid_spec=None, hbm=(), vmem=(), **settings
):
    spec = grid_spec or dict(num_scalar_prefetch=0, grid=grid, in_specs=in_specs, out_specs=out_specs)
    spec.setdefault("scratch_shapes", settings.pop("scratch_shapes", ()))
    direct = not spec["grid"]
    single = isinstance(out_shape, jax.ShapeDtypeStruct)
    shapes = [out_shape] if single else list(out_shape)
    kinds = [pltpu.HBM if i in hbm else pltpu.VMEM if i in vmem else None for i in range(len(shapes))]
    shapes = [out if kind is None else kind(out.shape, out.dtype) for out, kind in zip(shapes, kinds)]

    def call(*operands):
        marks = [mark for mark in LAST if not any(mark is operand for operand in operands)]
        count = len(operands)
        outputs = count + len(marks) + len(shapes)

        def body(*refs):
            refs[outputs][...] = jnp.zeros_like(refs[outputs])
            kernel(*refs[:count], *refs[count + len(marks) : outputs], *refs[outputs + 1 :])

        out_specs = [spec["out_specs"]] if single else list(spec["out_specs"])
        *outs, token = pl.pallas_call(
            body,
            grid_spec=pltpu.PrefetchScalarGridSpec(
                **{
                    **spec,
                    "in_specs": list(spec["in_specs"]) + [ANYWHERE] * len(marks),
                    "out_specs": out_specs + [pl.BlockSpec(memory_space=pltpu.VMEM) if direct else whole_block((8, 128))],
                }
            ),
            out_shape=shapes + [jax.ShapeDtypeStruct((8, 128), F32) if direct else pltpu.HBM((8, 128), F32)],
            cost_estimate=FREE,
            **settings,
        )(*map(where_it_is, operands), *map(where_it_is, marks))
        LAST[:] = [token]
        HELD.extend((out, kind) for out, kind in zip(outs + [token], kinds + [None if direct else pltpu.HBM]) if kind is not None)
        return outs[0] if single else outs

    return call


def hold_kernel(*refs):
    pass


def hold(*arrays, kind=None):
    return run(
        hold_kernel,
        out_shape=[jax.ShapeDtypeStruct(array.shape, array.dtype) for array in arrays],
        vmem=range(len(arrays)) if kind else (),
        in_specs=[ANYWHERE] * len(arrays),
        out_specs=[ANYWHERE] * len(arrays),
        input_output_aliases={i: i for i in range(len(arrays))},
    )(*(pltpu.with_memory_space_constraint(array, kind) if kind else array for array in arrays))


def wait_for(*arrays):
    LAST.extend(arrays)
    run(hold_kernel, out_shape=[], in_specs=[], out_specs=[])()


def place_kernel(first, views, aliased, table_ref, *refs):
    blocks = refs[: len(first)]
    outs = refs[len(first) + aliased : -1]
    copies = []
    for i, block in enumerate(blocks):
        for number, (out, source, target) in enumerate(views[0]):
            copies.append(
                pltpu.make_async_copy(
                    block.at[source],
                    outs[out].at[(table_ref[first[i]],) + target],
                    refs[-1].at[i, number],
                )
            )
    for copy in copies:
        copy.start()
    for copy in copies:
        copy.wait()


def place_blocks(table, held, blocks, relatives, views):
    moves, shapes, _ = views
    chips = lax.axis_size(CHIPS)
    first = [RELATIVES.index(relative) for relative in relatives]
    operands = [table, *blocks]
    aliases = {}
    if held is not None:
        aliases = {len(operands) + i: i for i in range(len(shapes))}
        operands += held
    hbm = pl.BlockSpec(memory_space=pltpu.HBM)
    return run(
        partial(place_kernel, first, views, len(aliases)),
        grid=(1,),
        in_specs=[pl.BlockSpec(memory_space=pltpu.SMEM)]
        + [whole_block(block.shape) for block in blocks]
        + [hbm] * len(aliases),
        out_specs=[hbm] * len(shapes),
        out_shape=[jax.ShapeDtypeStruct((chips,) + shape, BF16) for shape in shapes],
        scratch_shapes=[pltpu.SemaphoreType.DMA((len(blocks), len(moves)))],
        input_output_aliases=aliases,
    )(*operands)


class GatherRounds:
    def __init__(self, table, block, views):
        self.table, self.views = table, views
        self.have = {(0, 0, 0): block}
        self.held, self.due = None, []

    def place(self, number):
        names = [(0, 0, 0)] if number < 0 else [received for _, _, received in ROUNDS[number]]
        blocks = [self.have[name] for name in names]
        self.held = place_blocks(self.table, self.held, blocks, names, self.views)

    def step(self, number):
        names = list({sent: None for _, sent, _ in ROUNDS[number]}) if number else []
        LAST.extend(array for array in self.due if not any(array is self.have[name] for name in names))
        if names:
            self.have.update(zip(names, hold(*(self.have[name] for name in names), kind=pltpu.VMEM)))
        for axis, sent, received in ROUNDS[number]:
            self.have[received] = lax.ppermute(self.have[sent], axis, ring(lax.axis_size(axis)))
        self.due = [self.have[received] for _, _, received in ROUNDS[number]]

    def last_blocks(self):
        names = [received for _, _, received in ROUNDS[-1]]
        return [RELATIVES.index(name) for name in names], [self.have[name] for name in names]


class GatherRings:
    def __init__(self, table, block, views):
        self.held = gather_rings(block, views)

    def place(self, number):
        pass

    def step(self, number):
        pass

    def last_blocks(self):
        return [], []


def gather_rings(block, views):
    have = []
    shape = block.shape
    for axis in CHIPS:
        count = lax.axis_size(axis)
        me = lax.axis_index(axis)
        have.append(axis)
        place = len(have) - 1
        whole = jnp.zeros(block.shape[:place] + (count,) + block.shape[place:], block.dtype)
        piece = block
        for step in range(count):
            if step:
                piece = lax.ppermute(piece, axis, ring(count))
            whole = lax.dynamic_update_index_in_dim(whole, piece, lax.rem(me - step + count, count), place)
        block = whole
    block = block.reshape((-1,) + shape)
    held = [jnp.zeros(block.shape[:1] + view, block.dtype) for view in views[1]]
    for out, source, target in views[0]:
        held[out] = held[out].at[(slice(None),) + target].set(block[(slice(None),) + source])
    return held


def sum_kernel(first, counts, views, passing, table_ref, *refs):
    arrays, wanted = len(views[1]), len(counts)
    inputs = arrays + sum(counts) + passing
    grads = refs[:arrays]
    received = refs[arrays : arrays + sum(counts)]
    outs = refs[inputs : inputs + wanted]
    *own, sems = refs[inputs + wanted + passing :]
    copies = [
        [
            pltpu.make_async_copy(grads[a].at[table_ref[chip]], own[a].at[i], sems.at[i, a])
            for a in range(arrays)
            if chip is not None
        ]
        for i, chip in enumerate(first)
    ]
    for copy in sum(copies, []):
        copy.start()
    at = 0
    for i, count in enumerate(counts):
        for copy in copies[i]:
            copy.wait()
        for out, source, target in pieces_of(views):
            terms = [] if first[i] is None else [own[out][(i,) + target].astype(F32)]
            terms += [received[j][source].astype(F32) for j in range(at, at + count)]
            outs[i][source] = sum(terms[1:], terms[0]).astype(outs[i].dtype)
        at += count


def pieces_of(views):
    moves, shapes, block_shape = views
    spans = lambda place, size: (place.start, place.size) if isinstance(place, pl.Slice) else (0, size)
    for out, source, target in moves:
        starts = [spans(place, size) for place, size in zip(source + target, block_shape + shapes[out])]
        (top, rows), (left, columns), (low, _), (first, _) = starts
        for i in range(0, rows, 32):
            for j in range(0, columns, 512):
                size = (min(32, rows - i), min(512, columns - j))
                place = lambda row, column: (pl.ds(row + i, size[0]), pl.ds(column + j, size[1]))
                yield out, place(top, left), place(low, first)


def sum_blocks(table, grads, relatives, received, views, passing=()):
    _, shapes, block_shape = views
    first = [None if relative is None else RELATIVES.index(relative) for relative in relatives]
    counts = [len(blocks) for blocks in received]
    flat = [block for blocks in received for block in blocks]
    vmem = pl.BlockSpec(memory_space=pltpu.VMEM)
    count = 1 + len(grads) + len(flat)
    return run(
        partial(sum_kernel, first, counts, views, len(passing)),
        grid=(),
        in_specs=[pl.BlockSpec(memory_space=pltpu.SMEM)]
        + [pl.BlockSpec(memory_space=pltpu.HBM)] * len(grads)
        + [vmem] * len(flat)
        + [ANYWHERE] * len(passing),
        out_specs=[vmem] * len(relatives) + [ANYWHERE] * len(passing),
        out_shape=[jax.ShapeDtypeStruct(block_shape, BF16)] * (len(relatives) + len(passing)),
        input_output_aliases={count + i: len(relatives) + i for i in range(len(passing))},
        scratch_shapes=[pltpu.VMEM((len(relatives),) + shape, BF16) for shape in shapes]
        + [pltpu.SemaphoreType.DMA((len(relatives), len(shapes)))],
        compiler_params=pltpu.CompilerParams(vmem_limit_bytes=8 << 20),
    )(table, *grads, *flat, *passing)


def finish_kernel(views, count, pieces, wholes, table_ref, *refs):
    grads, received = refs[: len(views[1])], refs[len(views[1]) : len(views[1]) + count]
    mine, other, *outs, total_ref = refs[len(views[1]) + count :]
    for out, source, target in pieces_of(views):
        total = grads[out][(0,) + target].astype(F32)
        for block in received:
            total += block[source].astype(F32)
        total_ref[source] = total
    core = table_ref[len(RELATIVES)]
    rows = mine.shape[0]
    at = 0
    for start, size in pieces:
        low, high = total_ref[:rows, start : start + size], total_ref[rows:, start : start + size]
        here = pl.ds(at, size)
        mine[:, here] = jnp.where(core == 0, low, high)
        other[:, here] = jnp.where(core == 0, high, low)
        at += size
    for out, (tall, parts) in zip(outs, wholes):
        at = 0
        for place in parts:
            size = place[0].size if tall else place[1].size
            out[(pl.ds(at, size), slice(None)) if tall else (slice(None), pl.ds(at, size))] = total_ref[place]
            at += size


class ScatterRounds:
    def __init__(self, table, grads, views):
        self.table, self.views = table, views
        self.grads = [in_hbm(grad) for grad in grads]
        self.arrived, self.made, self.due = {}, {}, []

    def ahead(self, *names, most=2):
        came = [self.arrived.pop(name, []) for name in names]
        self.arrived.update((name, blocks[most:]) for name, blocks in zip(names, came) if blocks[most:])
        came = [blocks[:most] for blocks in came]
        self.made.update(zip(names, sum_blocks(self.table, self.grads, names, came, self.views)))

    def step(self, number, others=()):
        moves = ROUNDS[len(ROUNDS) - 1 - number]
        names = [sent for _, _, sent in moves]
        ready = [name for name in names if name in self.made and name not in self.arrived]
        missing = [name for name in names if name not in ready]
        came = [[self.made[name]] if name in self.made else [] for name in missing]
        came = [blocks + self.arrived.pop(name, []) for blocks, name in zip(came, missing)]
        own = [None if name in self.made else name for name in missing]
        LAST.extend(self.due + list(others))
        blocks = sum_blocks(
            self.table, self.grads, own, came, self.views, [self.made[name] for name in ready]
        )
        self.made.update(zip(missing + ready, blocks))
        self.due = []
        for axis, target, sent in moves:
            self.due.append(lax.ppermute(self.made[sent], axis, ring(lax.axis_size(axis), -1)))
            self.arrived.setdefault(target, []).append(self.due[-1])

    def finish(self, core, pieces, wholes):
        own = (0, 0, 0)
        came = self.arrived.pop(own)
        rows = self.views[2][0] // 2
        shapes = [(rows, sum(size for _, size in pieces))] * 2 + [
            (sum(r.size for r, _ in parts), parts[0][1].size) if tall else (parts[0][0].size, sum(c.size for _, c in parts))
            for tall, parts in wholes
        ]
        blocks = [
            pl.BlockSpec((1,) + shape, lambda g, table: (table[0],) + (0,) * len(shape)) for shape in self.views[1]
        ]
        return run(
            partial(finish_kernel, self.views, len(came), pieces, wholes),
            grid_spec=dict(
                num_scalar_prefetch=1,
                grid=(1,),
                in_specs=blocks + [whole_block(block.shape) for block in came],
                out_specs=[whole_block(shape) for shape in shapes],
                scratch_shapes=[pltpu.VMEM(self.views[2], F32)],
            ),
            out_shape=[jax.ShapeDtypeStruct(shape, F32) for shape in shapes],
            compiler_params=pltpu.CompilerParams(vmem_limit_bytes=16 << 20),
        )(self.table, *self.grads, *came)


class ScatterRings:
    def __init__(self, table, grads, views):
        self.sums = scatter_rings(grads, views)
        self.views = views

    def ahead(self, *names, most=2):
        pass

    def step(self, number, others=()):
        pass

    def result(self):
        moves, _, block_shape = self.views
        block = jnp.zeros(block_shape, F32)
        for out, source, target in moves:
            block = block.at[source].set(self.sums[out][target])
        return block


def picked(width, core):
    source = lax.broadcasted_iota(jnp.int32, (256, 128), 0)
    target = lax.broadcasted_iota(jnp.int32, (256, 128), 1)
    wanted = (target // width) * (2 * width) + core * width + target % width
    return jnp.where(source == wanted, 1.0, 0.0).astype(BF16)


def pick_kernel(widths, core_ref, *refs):
    matrices, outs = refs[: len(widths)], refs[len(widths) :]
    core = core_ref[0]
    for out, wanted in zip(outs, (core, 1 - core)):
        at = 0
        for width, matrix in zip(widths, matrices):
            half = matrix.shape[1] // 2
            if width == half:
                out[:, at : at + half] = jnp.where(wanted == 0, matrix[:, :half], matrix[:, half:])
            else:
                choice = picked(width, wanted)
                for i in range(half // 128):
                    columns = dot(matrix[:, i * 256 : (i + 1) * 256], choice)
                    out[:, at + i * 128 : at + (i + 1) * 128] = columns.astype(BF16)
            at += half


def pack_kernel(half, core_ref, mine, other, emit, payload, block):
    rows, breadth = emit.shape
    core = core_ref[0]
    split = 3 * half
    last = half + mine.shape[1]
    for i, (own, its) in enumerate(((mine, other), (other, mine))):
        here = pl.ds(i * rows, rows)
        block[here, :split] = jnp.where(core == 0, own[:, :split], its[:, :split])
        block[here, split : split + half] = emit[:, i * half : (i + 1) * half]
        block[here, split + half : last] = jnp.where(core == 0, own[:, split:], its[:, split:])
    height = 2 * rows
    for i in range(payload.shape[0] // height):
        block[:, last + i * breadth : last + (i + 1) * breadth] = payload[i * height : (i + 1) * height, :]


def stack_kernel(*refs):
    for i, piece in enumerate(refs[:-1]):
        for device in range(refs[-1].shape[0]):
            refs[-1][device, i : i + 1, :] = piece[...]


def join_kernel(widths, core_ref, mine, other, *outs):
    core = core_ref[0]
    rows = mine.shape[0]
    at = 0
    for width, out in zip(widths, outs):
        half = out.shape[1] // 2
        low = jnp.where(core == 0, mine[:, at : at + half], other[:, at : at + half])
        high = jnp.where(core == 0, other[:, at : at + half], mine[:, at : at + half])
        if width == half:
            out[:, :half] = low
            out[:, half:] = high
        elif width == 128:
            for i in range(half // 128):
                out[:, i * 256 : i * 256 + 128] = low[:, i * 128 : (i + 1) * 128]
                out[:, i * 256 + 128 : (i + 1) * 256] = high[:, i * 128 : (i + 1) * 128]
        else:
            for i in range(half // 128):
                total = jnp.zeros((rows, 256), F32)
                for number, part in enumerate((low, high)):
                    rest = part[:, i * 128 : (i + 1) * 128]
                    for _ in range(3):
                        piece = rest.astype(BF16)
                        total += dot_back(piece, picked(width, number))
                        rest = rest - piece.astype(F32)
                out[:, i * 256 : (i + 1) * 256] = total
        at += half


def whole_call(kernel, shapes, scalar, operands, hbm=()):
    return run(
        kernel,
        grid=(1,),
        out_shape=shapes,
        in_specs=[pl.BlockSpec(memory_space=pltpu.SMEM)] + [whole_block(operand.shape) for operand in operands],
        out_specs=[whole_block(out.shape) for out in shapes],
        hbm=hbm,
        compiler_params=pltpu.CompilerParams(vmem_limit_bytes=16 << 20),
    )(scalar.astype(jnp.int32).reshape(1), *operands)


def sum_axis(block, axis, place):
    count = lax.axis_size(axis)
    me = lax.axis_index(axis)

    def part(step):
        return lax.dynamic_index_in_dim(block, lax.rem(me + step, count), place, keepdims=False)

    total = part(1)
    for step in range(2, count + 1):
        moved = lax.ppermute(total.astype(BF16), axis, ring(count, -1))
        total = moved.astype(F32) + part(step).astype(F32)
    return total


def sum_along_z(block):
    return lax.psum_scatter(block.astype(BF16), "z", scatter_dimension=0).astype(F32)


def scatter_rings(grads, views):
    sizes = tuple(lax.axis_size(axis) for axis in CHIPS)
    sums = []
    for grad in grads:
        block = grad.reshape(sizes + grad.shape[1:])
        sums.append(sum_along_z(sum_axis(sum_axis(block, "x", 1), "y", 1)))
    return sums


def dot(left, right):
    return jnp.dot(left, right, preferred_element_type=F32)


def dot_back(grad, weight):
    return lax.dot_general(grad, weight, (((1,), (1,)), ((), ())), preferred_element_type=F32)


def outer(left, right):
    return lax.dot_general(left, right, (((0,), (0,)), ((), ())), preferred_element_type=F32)


def norm_parts(rows):
    center = jnp.mean(rows, axis=-1, keepdims=True)
    deviation = rows - center
    variance = jnp.mean(deviation * deviation, axis=-1, keepdims=True)
    inverse = lax.rsqrt(variance + EPSILON)
    return deviation * inverse, inverse


def last_row(rows):
    return lax.broadcasted_iota(jnp.int32, rows.shape, 0) == rows.shape[0] - 1


def first_row(rows):
    return lax.broadcasted_iota(jnp.int32, rows.shape, 0) == 0


def both_kernel(core_ref, *refs):
    count = len(refs) // 3
    for i in range(count):
        refs[2 * count + i][...] = jnp.where(core_ref[0] == pl.program_id(0), refs[2 * i][...], refs[2 * i + 1][...])


def both_groups(core, *pairs):
    rows, breadth = pairs[0][0].shape
    return run(
        both_kernel,
        grid=(2,),
        in_specs=[pl.BlockSpec(memory_space=pltpu.SMEM)]
        + [pl.BlockSpec((rows, breadth), lambda g: (0, 0))] * (2 * len(pairs)),
        out_specs=[pl.BlockSpec((rows, breadth), lambda g: (g, 0))] * len(pairs),
        out_shape=[jax.ShapeDtypeStruct((2 * rows, breadth), pair[0].dtype) for pair in pairs],
        hbm=range(len(pairs)),
        compiler_params=pltpu.CompilerParams(vmem_limit_bytes=16 << 20),
    )(core.astype(jnp.int32).reshape(1), *(part for pair in pairs for part in pair))


def parameters_kernel(
    core_ref, got, behind, keep, gain1, bias1, shares1, gain2, bias2, shares2, rate, bonus, behind1, *befores
):
    core = core_ref[0]
    own_rows = got.shape[-1]
    targets = ((gain1, 0, 1), (bias1, 1, 2), (shares1, 2, 5), (gain2, 5, 6), (bias2, 6, 7), (shares2, 7, 9))
    for chip in range(got.shape[0] // 2):
        pieces = [got[2 * chip + i].astype(F32) for i in range(2)]
        for i, piece in enumerate(pieces):
            for out, start, stop in targets:
                out[:, (2 * chip + i) * own_rows : (2 * chip + i + 1) * own_rows] = piece[start:stop]
        piece = jnp.exp(jnp.where(core == 0, pieces[0][9:], pieces[1][9:]))
        for i, out in enumerate((rate, bonus)):
            out[:, chip * own_rows : (chip + 1) * own_rows] = piece[i : i + 1]
    rows = [[] for _ in befores]
    for group in range(2):
        normed = norm_parts(behind[group].astype(F32))[0] * gain1[...] + bias1[...]
        behind1[group : group + 1, :] = normed[1:] * keep[group : group + 1, :]
        for i in range(len(befores)):
            rows[i].append(normed[1:] - (normed[1:] - normed[:1]) * (1.0 - shares1[i : i + 1, :]))
    for before, pair in zip(befores, rows):
        zeros = jnp.zeros((before.shape[0] - 2, before.shape[1]), F32)
        before[...] = jnp.concatenate(pair + [zeros], axis=0).astype(BF16)


def vectors_kernel(
    core_ref, norm1, shares1, decay, first, rate_ref, norm2, shares2, out
):
    core = core_ref[0]
    own_rows = out.shape[-1]
    devices = out.shape[0]
    rate = rate_ref[...]
    grad_decay = -rate * jnp.exp(-rate) * jnp.sum(decay[...], axis=0, keepdims=True)
    grad_first = jnp.sum(first[...], axis=0, keepdims=True)
    norms2 = jnp.where(core == 0, norm2[0], norm2[1])
    for device in range(devices):
        here = slice(device * own_rows, (device + 1) * own_rows)
        chip, owner = device // 2, device % 2
        out[device, 0:2, :] = norm1[0][:, here]
        out[device, 2:5, :] = shares1[:, here]
        channels = slice(chip * own_rows, (chip + 1) * own_rows)
        out[device, 5:6, :] = jnp.where(core == owner, grad_decay[:, channels], 0.0)
        out[device, 6:7, :] = jnp.where(core == owner, grad_first[:, channels], 0.0)
        out[device, 7:9, :] = norms2[:, here]
        out[device, 9:11, :] = shares2[:, here]


def vector_sums_kernel(parts, out):
    total = parts[0]
    for i in range(1, parts.shape[0]):
        total = total + parts[i]
    out[...] = total


def outer_kernel(left, right, out):
    out[...] = outer(left[...], right[...]).astype(BF16)


def outer_call(left, right, pin):
    tokens, height = left.shape
    width = right.shape[1]
    block = min(512, width)
    return run(
        outer_kernel,
        grid=(width // block,),
        in_specs=[whole_block(left.shape), pl.BlockSpec((tokens, block), lambda i: (0, i))],
        out_specs=pl.BlockSpec((height, block), lambda i: (0, i)),
        out_shape=jax.ShapeDtypeStruct((height, width), BF16),
        hbm=(0,),
        compiler_params=pltpu.CompilerParams(vmem_limit_bytes=16 << 20),
    )(*(in_hbm(array) if pin else array for array in (left, right)))


def norm_mix_kernel(terms, behind, gain, bias, shares, *refs):
    rows = terms[0][...].astype(F32)
    for term in terms[1:]:
        rows = rows + term[...].astype(F32)
    outs = list(refs)
    if len(terms) > 1:
        outs.pop(0)[...] = rows
    zhat, inverse = norm_parts(rows)
    outs.pop(0)[...] = zhat.astype(BF16)
    outs.pop(0)[...] = inverse
    normed = zhat * gain[...] + bias[...]
    group = pl.program_id(0)
    before = jnp.where(group == 0, behind[:1, :], behind[1:, :])
    step = normed - jnp.where(first_row(normed), before, shift_rows(normed, 1))
    for i, out in enumerate(outs):
        out[...] = (normed - step * (1.0 - shares[i : i + 1, :])).astype(BF16)


def norm_mix(terms, behind, gain, bias, shares, hbm):
    rows, breadth = terms[0].shape
    block = pl.BlockSpec((rows // 2, breadth), lambda g: (g, 0))
    whole = lambda element: pl.BlockSpec(element.shape, lambda g: (0, 0))
    shape = lambda kind: jax.ShapeDtypeStruct((rows, breadth), kind)
    wide = [shape(F32)] * (len(terms) > 1) + [shape(BF16)]

    def body(*refs):
        norm_mix_kernel(refs[: len(terms)], *refs[len(terms) :])

    return run(
        body,
        grid=(2,),
        in_specs=[block] * len(terms) + [whole(element) for element in (behind, gain, bias, shares)],
        out_specs=[block] * len(wide)
        + [pl.BlockSpec((rows // 2, 1), lambda g: (g, 0))]
        + [block] * shares.shape[0],
        out_shape=wide + [jax.ShapeDtypeStruct((rows, 1), F32)] + [shape(BF16)] * shares.shape[0],
        hbm=hbm,
        compiler_params=pltpu.CompilerParams(vmem_limit_bytes=18 << 20),
    )(*terms, behind, gain, bias, shares)


def norm_back_kernel(count, table, *refs):
    parts = refs[:count]
    came, zhat_ref, inverse_ref, gain, base = refs[count : count + 5]
    outs = refs[count + 5 :]
    grad = parts[0][...].astype(F32)
    for part in parts[1:]:
        grad = grad + part[...].astype(F32)
    group = pl.program_id(0)
    grad = grad + jnp.where(last_row(grad), jnp.where(group == 0, came[:1, :], came[-1:, :]), 0.0)
    zhat = zhat_ref[...].astype(F32)
    scaled = grad * gain[...]
    middle = jnp.mean(scaled, axis=-1, keepdims=True)
    slope = jnp.mean(scaled * zhat, axis=-1, keepdims=True)
    total = base[...].astype(F32) + inverse_ref[...] * (scaled - middle - zhat * slope)
    for out in outs[:-1]:
        out[...] = total.astype(out.dtype)
    outs[-1][0, :1, :] = jnp.sum(grad * zhat, axis=0, keepdims=True)
    outs[-1][0, 1:, :] = jnp.sum(grad, axis=0, keepdims=True)


def norm_back(core, parts, came, zhat, inverse, gain, base, kinds, own):
    breadth = zhat.shape[1]
    rows = zhat.shape[0] // 2
    groups = 1 if own else 2
    pick = lambda width: pl.BlockSpec((rows, width), lambda g, table: (table[0] if own else g, 0))
    block = pl.BlockSpec((rows, breadth), lambda g, table: (g, 0))
    whole = lambda element: pl.BlockSpec(element.shape, lambda g, table: (0, 0))
    return run(
        partial(norm_back_kernel, len(parts)),
        grid_spec=dict(
            num_scalar_prefetch=1,
            grid=(groups,),
            in_specs=[block] * len(parts)
            + [whole(came), pick(breadth), pick(1), whole(gain), pick(breadth)],
            out_specs=[block] * len(kinds) + [pl.BlockSpec((1, 2, breadth), lambda g, table: (g, 0, 0))],
        ),
        out_shape=[jax.ShapeDtypeStruct((groups * rows, breadth), kind) for kind in kinds]
        + [jax.ShapeDtypeStruct((groups, 2, breadth), F32)],
        hbm=() if own else (0,),
        compiler_params=pltpu.CompilerParams(vmem_limit_bytes=16 << 20),
    )(core.astype(jnp.int32).reshape(1), *parts, came, zhat, inverse, gain, base)


def output_kernel(core_ref, part, swapped, gate_own, gate_other, cot_ref, middle, out, d_value, d_gate):
    core = core_ref[0]
    half = gate_own.shape[1]
    value = part[...].astype(F32) + swapped[...].astype(F32)
    cot = cot_ref[...].astype(F32)
    own, other = gate_own[...], gate_other[...]
    for i in range(2):
        gate = jnp.where(core == i, own, other)
        here = pl.ds(i * half, half)
        out[:, here] = (middle[:, here] + gate * value[:, i * half : (i + 1) * half]).astype(BF16)
        d_value[:, here] = (cot[:, i * half : (i + 1) * half] * gate).astype(BF16)
    mine = lambda rows: jnp.where(core == 0, rows[:, :half], rows[:, half:])
    d_gate[...] = (mine(cot) * mine(value) * own * (1.0 - own)).astype(BF16)


def output(core, part, swapped, gate_own, gate_other, cot, middle):
    rows, breadth = part.shape
    block = lambda width: pl.BlockSpec((rows // 2, width), lambda g: (g, 0))
    half = breadth // 2
    return run(
        output_kernel,
        grid=(2,),
        in_specs=[pl.BlockSpec(memory_space=pltpu.SMEM)]
        + [block(width) for width in (breadth, breadth, half, half, breadth, breadth)],
        out_specs=[block(breadth), block(breadth), block(half)],
        out_shape=[jax.ShapeDtypeStruct((rows, width), BF16) for width in (breadth, breadth, half)],
        compiler_params=pltpu.CompilerParams(vmem_limit_bytes=16 << 20),
    )(core.astype(jnp.int32).reshape(1), part, swapped, gate_own, gate_other, cot, middle)


def shift_rows(rows, distance):
    return pltpu.roll(rows, distance % rows.shape[0], 0)


def fade_tables(rate, reverse):
    breadth = rate.shape[-1]
    place = lax.broadcasted_iota(jnp.int32, (TILE, breadth), 0)
    if reverse:
        place = TILE - 1 - place
    steps = []
    distance = 1
    while distance < TILE:
        factor = jnp.where(place >= distance, jnp.exp(-rate * float(distance)), 0.0)
        steps.append((distance, factor))
        distance *= 2
    passed = jnp.exp(-rate * place.astype(F32))
    before = (place >= 1).astype(F32)
    return steps, passed, before


def scan_tile(terms, steps, reverse):
    for distance, factor in steps:
        terms = terms + factor * shift_rows(terms, -distance if reverse else distance)
    return terms


def entering(reach, distance, ends, rate, rows, groups):
    totals = [[0.0, 0.0] for _ in range(groups)]
    for device in range(ends.shape[0]):
        fade = jnp.exp(-rate * (float(rows) * distance[device]))
        for group in range(groups):
            for i in range(2):
                term = ends[device, i, group : group + 1, :] * fade
                totals[group][i] += jnp.where(reach[group, device] > 0.5, term, 0.0)
    return [total for pair in totals for total in pair]


def wkv_kernel(
    groups, reach, distance, key_ref, value_ref, recept_ref, key_old, value_old, recept_old, rate_ref, bonus_ref,
    ends_ref, emit_ref, sent_ref, gated_ref, prior_num_ref, prior_den_ref,
):
    rows = key_ref.shape[0] // groups
    rate = rate_ref[...]
    bonus = bonus_ref[...]
    steps, passed, before = fade_tables(rate, False)
    tile_fade = jnp.exp(-rate * float(TILE))

    def body(index, carry):
        states = []
        for group in range(groups):
            num, den = carry[2 * group], carry[2 * group + 1]
            at = pl.ds(pl.multiple_of(group * rows + index * TILE, TILE), TILE)
            grown = jnp.exp(key_ref[at, :].astype(F32))
            product = grown * value_ref[at, :].astype(F32)
            inner_num = scan_tile(product, steps, False)
            inner_den = scan_tile(grown, steps, False)
            prior_num = shift_rows(inner_num, 1) * before + passed * num
            prior_den = shift_rows(inner_den, 1) * before + passed * den
            prior_num_ref[at, :] = prior_num
            prior_den_ref[at, :] = prior_den
            wkv = (prior_num + bonus * product) / (prior_den + bonus * grown)
            gated_ref[at, :] = (recept_ref[at, :] * wkv.astype(BF16).astype(F32)).astype(BF16)
            states.append(inner_num[TILE - 1 :, :] + tile_fade * num)
            states.append(inner_den[TILE - 1 :, :] + tile_fade * den)
        return tuple(states)

    start = entering(reach, distance, ends_ref, rate, rows, groups)
    lax.fori_loop(0, rows // TILE, body, tuple(start))
    attended = dot(gated_ref[...], emit_ref[...])
    sent_ref[: groups * rows, :] = attended.astype(BF16)
    pad = lambda rows: jnp.concatenate(rows + [jnp.zeros((TILE - groups, rate.shape[-1]), F32)], axis=0)
    grown = jnp.exp(key_old[...].astype(F32))
    product = grown * value_old[...].astype(F32)
    unfade = jnp.exp(rate)
    num = (pad(start[::2]) - product) * unfade + bonus * product
    den = (pad(start[1::2]) - grown) * unfade + bonus * grown
    old = (recept_old[...] * (num / den).astype(BF16).astype(F32)).astype(BF16)
    attended = dot(old, emit_ref[...])
    sent_ref[groups * rows :, :] = attended.astype(BF16)


def wkv_back_kernel(
    groups, reach, distance, key_ref, value_ref, prior_num_ref, prior_den_ref, weighted_ref, rate_ref, bonus_ref,
    ends_ref, dkey_ref, dvalue_ref, decay_ref, first_ref,
):
    rows = key_ref.shape[0] // groups
    rate = rate_ref[...]
    bonus = bonus_ref[...]
    steps, passed, before = fade_tables(rate, True)
    tile_fade = jnp.exp(-rate * float(TILE))
    decay_ref[...] = jnp.zeros_like(decay_ref)
    first_ref[...] = jnp.zeros_like(first_ref)

    def body(step, carry):
        index = rows // TILE - 1 - step
        states = []
        for group in range(groups):
            num, den = carry[2 * group], carry[2 * group + 1]
            at = pl.ds(pl.multiple_of(group * rows + index * TILE, TILE), TILE)
            grown = jnp.exp(key_ref[at, :].astype(F32))
            value = value_ref[at, :].astype(F32)
            prior_num = prior_num_ref[at, :]
            prior_den = prior_den_ref[at, :]
            wkv_den = prior_den + bonus * grown
            wkv = (prior_num + bonus * grown * value) / wkv_den
            grad = weighted_ref[at, :].astype(F32) / wkv_den
            inner_num = scan_tile(grad, steps, True)
            inner_den = scan_tile(-grad * wkv, steps, True)
            lam_num = shift_rows(inner_num, -1) * before + passed * num
            lam_den = shift_rows(inner_den, -1) * before + passed * den
            bonus_grad = bonus * grad
            dvalue_ref[at, :] = (grown * (bonus_grad + lam_num)).astype(BF16)
            direct = bonus_grad * (value - wkv)
            dkey_ref[at, :] = (grown * (direct + lam_num * value + lam_den)).astype(BF16)
            first_ref[...] += grown * direct
            decay_ref[...] += lam_num * prior_num + lam_den * prior_den
            states.append(inner_num[:1, :] + tile_fade * num)
            states.append(inner_den[:1, :] + tile_fade * den)
        return tuple(states)

    start = entering(reach, distance, ends_ref, rate, rows, groups)
    lax.fori_loop(0, rows // TILE, body, tuple(start))


def wkv_start_kernel(
    groups, grad_ref, recept_ref, key_ref, value_ref, prior_num_ref, prior_den_ref, rate_ref, bonus_ref,
    weighted_ref, accept_ref, begin_ref,
):
    rows = key_ref.shape[0] // groups
    rate = rate_ref[...]
    bonus = bonus_ref[...]
    place = lax.broadcasted_iota(jnp.int32, (TILE, rate.shape[-1]), 0).astype(F32)
    tile_fade = jnp.exp(-rate * float(TILE))

    def body(index, carry):
        fade, sums = carry[0], []
        for group in range(groups):
            at = pl.ds(pl.multiple_of(group * rows + index * TILE, TILE), TILE)
            grown = bonus * jnp.exp(key_ref[at, :].astype(F32))
            wkv_den = prior_den_ref[at, :] + grown
            wkv = (prior_num_ref[at, :] + grown * value_ref[at, :].astype(F32)) / wkv_den
            recept = recept_ref[at, :]
            grad = grad_ref[at, :]
            kept = grad * recept
            weighted = kept.astype(BF16)
            weighted_ref[at, :] = weighted
            accept_ref[at, :] = (kept * wkv.astype(BF16).astype(F32) * (1.0 - recept)).astype(BF16)
            faded = fade * (weighted.astype(F32) / wkv_den)
            sums += [carry[1 + 2 * group] + faded, carry[2 + 2 * group] - faded * wkv]
        return (fade * tile_fade, *sums)

    zero = jnp.zeros((TILE, rate.shape[-1]), F32)
    _, *sums = lax.fori_loop(0, rows // TILE, body, (jnp.exp(-rate * place),) + (zero,) * (2 * groups))
    for group in range(groups):
        for i in range(2):
            total = jnp.sum(sums[2 * group + i], axis=0, keepdims=True)
            for device in range(begin_ref.shape[0]):
                begin_ref[device, i, group : group + 1, :] = total


def keys_start_kernel(chips, table, *refs):
    mixes, befores, weights = refs[:3], refs[3:6], refs[6:9]
    parts, lates, held = refs[9:12], refs[12:15], refs[15]
    height = lates[0].shape[1] // max(len(chips), 1)
    breadth = held.shape[0]
    tokens = mixes[0].shape[0]
    for i in range(3):
        held[...] = weights[i][...]
        for chip in chips:
            here = pl.ds(pl.multiple_of(table[chip] * height, height), height)
            held[here, :] = jnp.zeros((height, held.shape[1]), BF16)
        for rows, mixed in ((pl.ds(0, tokens), mixes[i]), (pl.ds(tokens, TILE), befores[i])):
            parts[i][rows, :] = dot(mixed[...], held[...])

    @pl.when(pl.program_id(0) == 0)
    def _():
        row = lax.broadcasted_iota(jnp.int32, (breadth, lates[0].shape[1]), 0)
        column = lax.broadcasted_iota(jnp.int32, (breadth, lates[0].shape[1]), 1)
        start = jnp.zeros_like(column)
        for j, chip in enumerate(chips):
            start = jnp.where(column // height == j, table[chip] * height, start)
        chosen = jnp.where(row == start + column % height, 1.0, 0.0).astype(BF16)
        for i in range(3):
            for rows, mixed in ((pl.ds(0, tokens), mixes[i]), (pl.ds(tokens, TILE), befores[i])):
                lates[i][rows, :] = dot(mixed[...], chosen).astype(BF16)


def keys_end_kernel(groups, blocks, *refs):
    parts, lates, late = refs[:3], refs[3:6], refs[6 : 6 + 3 * blocks]
    rate = refs[6 + 3 * blocks]
    *outs, ends = refs[7 + 3 * blocks :]
    tokens = outs[0].shape[0]
    for i in range(3):
        product = parts[i][...]
        if blocks:
            rows = jnp.concatenate([block[...] for block in late[i * blocks : (i + 1) * blocks]], axis=0)
            product = product + dot(lates[i][...], rows)
        if i == 2:
            product = jax.nn.sigmoid(product)
        outs[i][...] = product[:tokens].astype(outs[i].dtype)
        outs[3 + i][...] = product[tokens:].astype(outs[i].dtype)
    keys, values = outs[:2]
    rows = tokens // groups
    left = (rows - 1 - lax.broadcasted_iota(jnp.int32, (rows, keys.shape[1]), 0)).astype(F32)
    fades = jnp.exp(-rate[...] * left)
    for group in range(groups):
        here = pl.ds(group * rows, rows)
        grown = jnp.exp(keys[here, :].astype(F32)) * fades
        num = jnp.sum(grown * values[here, :].astype(F32), axis=0, keepdims=True)
        den = jnp.sum(grown, axis=0, keepdims=True)
        for device in range(ends.shape[0]):
            ends[device, 0, group : group + 1, :] = num
            ends[device, 1, group : group + 1, :] = den


def keys_start(table, mixes, befores, weights, chips):
    rows, breadth = mixes[0].shape
    columns = weights[0].shape[1]
    block = min(256, columns)
    late = max(len(chips), 1) * (breadth // lax.axis_size(CHIPS))
    wide = lambda height: pl.BlockSpec((height, block), lambda i, table: (0, i))
    return run(
        partial(keys_start_kernel, chips),
        grid_spec=dict(
            num_scalar_prefetch=1,
            grid=(columns // block,),
            in_specs=[whole_block((rows, breadth))] * 3 + [whole_block((TILE, breadth))] * 3 + [wide(breadth)] * 3,
            out_specs=[wide(rows + TILE)] * 3 + [whole_block((rows + TILE, late))] * 3,
            scratch_shapes=[pltpu.VMEM((breadth, block), BF16)],
        ),
        out_shape=[jax.ShapeDtypeStruct((rows + TILE, columns), F32)] * 3
        + [jax.ShapeDtypeStruct((rows + TILE, late), BF16)] * 3,
        hbm=range(6),
        compiler_params=pltpu.CompilerParams(vmem_limit_bytes=24 << 20),
    )(table, *mixes, *befores, *map(in_hbm, weights))


def keys_end(started, blocks, rate, parts):
    rows, columns = started[0].shape
    block = min(256, columns)
    steps = columns // block
    wide = lambda height: pl.BlockSpec((height, block), lambda i: (0, i))
    part = lambda number: pl.BlockSpec((blocks[0].shape[0], block), lambda i: (0, number * steps + i))
    shape = lambda height, kind: jax.ShapeDtypeStruct((height, columns), kind)
    kinds = (BF16, BF16, F32)
    return run(
        partial(keys_end_kernel, 2, len(blocks)),
        grid=(steps,),
        in_specs=[wide(rows)] * 3
        + [whole_block(started[3].shape)] * 3
        + [part(number) for number in range(3) for _ in blocks]
        + [wide(1)],
        out_specs=[wide(rows - TILE)] * 3 + [wide(TILE)] * 3 + [pl.BlockSpec((parts, 2, 2, block), lambda i: (0, 0, 0, i))],
        out_shape=[shape(rows - TILE, kind) for kind in kinds]
        + [shape(TILE, kind) for kind in kinds]
        + [jax.ShapeDtypeStruct((parts, 2, 2, columns), F32)],
        hbm=(0, 1, 2),
        compiler_params=pltpu.CompilerParams(vmem_limit_bytes=24 << 20),
    )(*started, *(list(blocks) * 3), rate)


def wkv_call(kernel, groups, shapes, operands, hbm=(), columns=1, scalars=()):
    def block(array):
        shape = array.shape[:-1] + (array.shape[-1] // columns,)
        return pl.BlockSpec(shape, lambda i: (0,) * (len(shape) - 1) + (i,))

    return run(
        partial(kernel, groups),
        grid=(columns,),
        out_shape=shapes,
        in_specs=[pl.BlockSpec(memory_space=pltpu.SMEM)] * len(scalars) + [block(operand) for operand in operands],
        out_specs=[block(out) for out in shapes],
        hbm=hbm,
        compiler_params=pltpu.CompilerParams(vmem_limit_bytes=14 << 20),
    )(*scalars, *operands)


def mix_back_kernel(groups, count, core_ref, *refs):
    grads = refs[:count]
    zhat, behind, gain, bias, shares = refs[count : count + 5]
    *parts, first, sums = refs[count + 5 :]
    rows = zhat.shape[0] // groups
    totals = [0.0] * count
    for group in range(groups):
        here = pl.ds(group * rows, rows)
        normed = zhat[here, :].astype(F32) * gain[...] + bias[...]
        step = normed - jnp.where(first_row(normed), behind[group : group + 1, :], shift_rows(normed, 1))
        direct, shifted = 0.0, 0.0
        for i in range(count):
            grad = grads[i][here, :].astype(F32)
            moved = grad * (1.0 - shares[i : i + 1, :])
            direct += grad - moved
            shifted += moved
            totals[i] += jnp.sum(grad * step, axis=0, keepdims=True)
        first[group : group + 1, :] = shifted[:1, :]
        part = direct + jnp.where(last_row(shifted), 0.0, shift_rows(shifted, -1))
        if parts[0].shape == zhat.shape:
            parts[0][here, :] = part.astype(BF16)
        else:
            for i in range(2):

                @pl.when((core_ref[0] == group) == (i == 0))
                def _():
                    parts[i][...] = part.astype(parts[i].dtype)
    for i in range(count):
        sums[i : i + 1, :] = totals[i]


def mix_back(core, grads, zhat, behind, gain, bias, shares, apart):
    rows, breadth = zhat.shape
    count = len(grads)
    block = min(256, breadth)
    column = lambda height: pl.BlockSpec((height, block), lambda i: (0, i))
    outs = [(rows // 2, BF16)] * 2 if apart else [(rows, BF16)]
    outs += [(2, F32), (count, F32)]
    return run(
        partial(mix_back_kernel, 2, count),
        grid=(breadth // block,),
        in_specs=[pl.BlockSpec(memory_space=pltpu.SMEM)]
        + [column(rows)] * (count + 1)
        + [column(2), column(1), column(1), column(count)],
        out_specs=[column(height) for height, _ in outs],
        out_shape=[jax.ShapeDtypeStruct((height, breadth), kind) for height, kind in outs],
        compiler_params=pltpu.CompilerParams(vmem_limit_bytes=14 << 20),
    )(core.astype(jnp.int32).reshape(1), *grads, zhat, behind, gain, bias, shares)


def per_device(
    layer_incoming,
    series_extents,
    emitted_adjoint,
    norm1_scaling,
    norm1_offset,
    mixer_lookup_portion,
    mixer_payload_portion,
    mixer_accept_portion,
    temporal_fading_log,
    present_step_reward,
    mixer_lookup_matrix,
    mixer_payload_matrix,
    mixer_accept_matrix,
    mixer_emit_matrix,
    norm2_scaling,
    norm2_offset,
    feedforward_lookup_portion,
    feedforward_accept_portion,
    feedforward_lookup_matrix,
    feedforward_payload_matrix,
    feedforward_accept_matrix,
):
    LAST.clear()
    HELD.clear()
    devices = lax.axis_size(ALL)
    chips = lax.axis_size(CHIPS)
    parts = lax.axis_size(SEQ)
    core = lax.axis_index("c")
    place = lax.axis_index(SEQ)
    rows, breadth = layer_incoming.shape[1:]
    own_rows = mixer_lookup_matrix.shape[0]
    hidden_rows = feedforward_payload_matrix.shape[0]

    half = breadth // 2
    blocks = max(half // 256, 1)
    hidden = feedforward_lookup_matrix.shape[1] // 2
    both = lambda own, other: jnp.where(core == 0, jnp.stack([own, other]), jnp.stack([other, own]))
    mine_of = lambda pair: lax.dynamic_index_in_dim(pair, core, 0, keepdims=False)
    other_of = lambda pair: lax.dynamic_index_in_dim(pair, 1 - core, 0, keepdims=False)
    pair_rows = 2 * own_rows
    every = slice(None)
    mix_views = (
        tuple((i, (every, pl.ds(i * half, half)), (every, every)) for i in range(3))
        + tuple(
            (3, (pl.ds(i * own_rows, own_rows), pl.ds(3 * half, half)), (every, pl.ds(i * half, half)))
            for i in range(2)
        )
        + ((4, (every, pl.ds(4 * half, half)), (every, every)),),
        ((pair_rows, half),) * 3 + ((own_rows, breadth), (pair_rows, half)),
        (pair_rows, 5 * half),
    )
    stack = hidden_rows // pair_rows
    ffn_views = (
        ((0, (every, pl.ds(0, hidden)), (every, every)),)
        + tuple(
            (1, (every, pl.ds(hidden + i * breadth, breadth)), (pl.ds(i * pair_rows, pair_rows), every))
            for i in range(stack)
        ),
        ((pair_rows, hidden), (hidden_rows, breadth)),
        (pair_rows, hidden + stack * breadth),
    )
    gather_views = (
        mix_views[0]
        + tuple(
            (5 + out, (every, pl.ds(5 * half + source[1].start, source[1].size)), target)
            for out, source, target in ffn_views[0]
        ),
        mix_views[1] + ffn_views[1],
        (pair_rows, 5 * half + ffn_views[2][1]),
    )

    begins = jnp.cumsum(series_extents[0]) - series_extents[0]
    starts = jnp.any(jnp.arange(parts)[:, None] * rows == begins[None, :], axis=1)
    joined = jnp.where(starts, 0.0, 1.0).astype(F32)
    joined = both(joined, swap(joined))

    own_in, own_cot = in_hbm(layer_incoming[0]), in_hbm(emitted_adjoint[0])
    ends_of = lambda element: element.reshape(2, rows, -1)[:, rows - 2 :]

    rounds = in_rounds()
    table = chip_table() if rounds else jnp.zeros((1,), jnp.int32)
    split_up = (
        mixer_lookup_matrix, mixer_payload_matrix, mixer_accept_matrix,
        feedforward_accept_matrix, feedforward_lookup_matrix,
    )
    widths = (own_rows, own_rows, own_rows, half, hidden_rows)
    picks = jax.ShapeDtypeStruct((own_rows, 4 * half + hidden), BF16)
    both_inputs = lambda: both_groups(core, (own_in, swap(own_in)), (own_cot, swap(own_cot)))
    if rounds:
        mine, other = whole_call(partial(pick_kernel, widths), (picks, picks), core, tuple(map(in_hbm, split_up)))
        other = swap(other)
        (block,) = whole_call(
            partial(pack_kernel, half), [jax.ShapeDtypeStruct(gather_views[2], BF16)],
            core, (mine, other, in_hbm(mixer_emit_matrix), in_hbm(feedforward_payload_matrix)),
        )
    else:
        halves = jnp.concatenate(
            [
                matrix.reshape(own_rows, -1, 2, width).transpose(2, 0, 1, 3).reshape(2, own_rows, -1)
                for matrix, width in zip(split_up, widths)
            ],
            axis=-1,
        )
        pair = both(mine_of(halves), swap(other_of(halves))).reshape(pair_rows, -1)
        emit = jnp.concatenate([mixer_emit_matrix[:, :half], mixer_emit_matrix[:, half:]], axis=0)
        payload = [feedforward_payload_matrix[i * pair_rows : (i + 1) * pair_rows] for i in range(stack)]
        block = jnp.concatenate([pair[:, : 3 * half], emit, pair[:, 3 * half :], *payload], axis=1)
    Gather, Scatter = (GatherRounds, ScatterRounds) if rounds else (GatherRings, ScatterRings)
    weights = Gather(table, block, gather_views)
    weights.step(0)
    inputs, cotangent = both_inputs()
    weights.place(-1)
    pieces = (
        norm1_scaling, norm1_offset, mixer_lookup_portion, mixer_payload_portion,
        mixer_accept_portion, norm2_scaling, norm2_offset, feedforward_lookup_portion,
        feedforward_accept_portion, temporal_fading_log, present_step_reward,
    )
    pieces = [piece.reshape(1, own_rows) for piece in pieces]
    vectors = run(
        stack_kernel,
        out_shape=jax.ShapeDtypeStruct((devices, len(pieces), own_rows), BF16),
        in_specs=[whole_block(piece.shape) for piece in pieces],
        out_specs=whole_block((devices, len(pieces), own_rows)),
    )(*pieces)
    vectors = lax.all_to_all(vectors, ALL, 0, 0, tiled=True)
    (edge,) = hold(ends_of(inputs))
    behind = along_seq(edge, 1)
    LAST.append(joined)
    weights.step(1)
    LAST.extend([behind, vectors])
    weights.step(2)
    weights.place(0)

    keep = lax.dynamic_index_in_dim(joined, place, 1)[:, :, None]
    index = jnp.arange(parts)
    began = jnp.where((joined == 0.0) & (index[None] <= place), index[None], -1).max(axis=1)
    reach = ((index[None] < place) & (index[None] >= began[:, None])).astype(F32)
    begun = jnp.where((joined == 0.0) & (index[None] > place), index[None], parts).min(axis=1)
    reach_back = ((index[None] > place) & (index[None] < begun[:, None])).astype(F32)

    def spread(ends):
        return lax.all_to_all(ends, SEQ, 0, 0, tiled=True)

    distances = lambda places: jnp.maximum(places, 0).astype(F32)
    heights = [(height, breadth) for height in (1, 1, 3, 1, 1, 2)] + [(1, half), (1, half), (2, breadth)]
    shapes = [jax.ShapeDtypeStruct(shape, F32) for shape in heights] + [jax.ShapeDtypeStruct((TILE, breadth), BF16)] * 3
    gain1, bias1, shares1, gain2, bias2, shares2, rate, bonus, behind1, *mixed_before = run(
        parameters_kernel,
        out_shape=shapes,
        in_specs=[pl.BlockSpec(memory_space=pltpu.SMEM)]
        + [whole_block(array.shape) for array in (vectors, behind, keep[:, 0])],
        out_specs=[whole_block(shape.shape) for shape in shapes],
    )(core.astype(jnp.int32).reshape(1), vectors, behind, keep[:, 0])
    weights.place(1)
    zhat1, inverse1, mixed_k, mixed_v, mixed_r = norm_mix(
        [inputs], behind1, gain1, bias1, shares1, range(5)
    )
    weights.step(3)
    weights.place(2)
    weights.step(4)
    weights.place(3)
    whole = lambda held: held.reshape(-1, held.shape[-1])
    weight_k, weight_v, weight_r, *_ = map(whole, weights.held)
    chips_late, blocks_late = weights.last_blocks()
    started = keys_start(
        table, (mixed_k, mixed_v, mixed_r), mixed_before, (weight_k, weight_v, weight_r), chips_late
    )
    keys, values, recept, *before, ends = keys_end(started, blocks_late, rate, parts)
    weights.place(4)
    weight_k, weight_v, weight_r, weight_o, weight_fr, weight_fk, weight_fv = map(whole, weights.held)

    shape = lambda kind: jax.ShapeDtypeStruct((2 * rows, half), kind)
    sent, gated, prior_num, prior_den = wkv_call(
        wkv_kernel, 2,
        (
            jax.ShapeDtypeStruct((2 * rows + TILE, breadth), BF16),
            shape(BF16), shape(F32), shape(F32),
        ),
        (keys, values, recept, *before, rate, bonus, spread(ends), in_hbm(weight_o)), (1, 2, 3),
        scalars=(reach, distances(place - 1 - index)),
    )
    swapped = swap(sent)
    HELD.append((swapped, pltpu.HBM))
    before2 = behind[:, 1].astype(F32) + (sent[2 * rows :].astype(F32) + swapped[2 * rows :].astype(F32))[:2]
    behind2 = jnp.where(keep[:, 0] > 0.5, norm_parts(before2)[0] * gain2 + bias2, 0.0)
    middle, zhat2, inverse2, ffn_k, ffn_r = norm_mix(
        [inputs, sent, swapped], behind2, gain2, bias2, shares2, ()
    )
    gate_own = jax.nn.sigmoid(dot(ffn_r, weight_fr))
    gate_other = swap(gate_own)
    pre_hidden = jax.nn.relu(dot(ffn_k, weight_fk))
    hidden_act = jnp.square(pre_hidden).astype(BF16)
    value_part = dot(hidden_act, weight_fv).astype(BF16)
    block_output, d_value_out, d_gate_pre = output(
        core, value_part, swap(value_part), gate_own, gate_other, cotangent, middle
    )
    block_output = mine_of(block_output.reshape(2, rows, breadth))

    d_hidden = dot_back(d_value_out, weight_fv)
    d_pre_hidden = (d_hidden * 2.0 * pre_hidden).astype(BF16)
    low_back = lambda grad, weight: dot_back(grad, weight).astype(BF16)

    def came_back(first):
        return along_seq((first + swap(first)) * keep[:, 0], -1)

    part2, first2, share_grads2 = mix_back(
        core, (low_back(d_pre_hidden, weight_fk), low_back(d_gate_pre, weight_fr)),
        zhat2, behind2, gain2, bias2, shares2, False,
    )
    grad_fr = outer(ffn_r, d_gate_pre).astype(BF16)
    grad_fv = outer_call(hidden_act, d_value_out, False)
    swapped2 = swap(part2)
    HELD.append((swapped2, pltpu.HBM))
    d_middle, d_attended, norm_grads2 = norm_back(
        core, (part2, swapped2), came_back(first2), zhat2, inverse2, gain2, cotangent,
        (F32, BF16), False,
    )

    grad_o = outer(gated, d_attended).astype(BF16)
    d_gated = dot_back(d_attended, weight_o)
    d_weighted, d_recept_pre, begins_back = wkv_call(
        wkv_start_kernel, 2,
        (shape(BF16), shape(BF16), jax.ShapeDtypeStruct((parts, 2, 2, half), F32)),
        (d_gated, recept, keys, values, prior_num, prior_den, rate, bonus), columns=blocks,
    )
    grad_fk = outer_call(ffn_k, d_pre_hidden, True)
    begins_back = spread(begins_back)
    small = jax.ShapeDtypeStruct((TILE, half), F32)
    d_keys, d_values, decay_sum, bonus_sum = wkv_call(
        wkv_back_kernel, 2, (shape(BF16), shape(BF16), small, small),
        (keys, values, prior_num, prior_den, d_weighted, rate, bonus, begins_back),
        columns=blocks, scalars=(reach_back, distances(index - place - 1)),
    )
    grad_k = outer(mixed_k, d_keys).astype(BF16)
    grad_v = outer(mixed_v, d_values).astype(BF16)
    grad_r = outer(mixed_r, d_recept_pre).astype(BF16)
    per_chip = lambda grad: grad.reshape(chips, -1, grad.shape[-1])
    scatter = Scatter(
        table,
        [per_chip(grad) for grad in (grad_k, grad_v, grad_r, grad_o, grad_fr, grad_fk, grad_fv)],
        gather_views,
    )
    scatter.step(0)
    scatter.ahead((3, 0, 1), (2, 0, 1), (1, 1, 0))
    own1, other1, first1, share_grads1 = mix_back(
        core,
        (low_back(d_keys, weight_k), low_back(d_values, weight_v), low_back(d_recept_pre, weight_r)),
        zhat1, behind1, gain1, bias1, shares1, True,
    )
    swapped1 = swap(other1)
    first_sum = (first1 + swap(first1)) * keep[:, 0]
    scatter.step(1, [swapped1, first_sum])
    scatter.ahead((2, 0, 0), (1, 0, 1), (0, 1, 0))
    came1 = along_seq(first_sum, -1)
    scatter.step(2, [came1])
    scatter.ahead((0, 1, 1))
    input_grad, norm_grads1 = norm_back(
        core, (own1, swapped1), mine_of(came1[:, None]), zhat1, inverse1, gain1, d_middle, (F32,), True
    )
    pieces = (norm_grads1, share_grads1, decay_sum, bonus_sum, rate, norm_grads2, share_grads2)
    grads = run(
        vectors_kernel,
        out_shape=jax.ShapeDtypeStruct((devices, 11, own_rows), F32),
        in_specs=[pl.BlockSpec(memory_space=pltpu.SMEM)] + [whole_block(piece.shape) for piece in pieces],
        out_specs=whole_block((devices, 11, own_rows)),
    )(core.astype(jnp.int32).reshape(1), *pieces)
    scatter.step(3)
    scatter.ahead((1, 0, 0), most=1)
    scatter.step(4)
    (grads,) = hold(grads)
    grads = lax.all_to_all(grads, ALL, 0, 0, tiled=True)
    grads = run(
        vector_sums_kernel,
        out_shape=jax.ShapeDtypeStruct((11, own_rows), F32),
        in_specs=[whole_block(grads.shape)],
        out_specs=whole_block((11, own_rows)),
    )(grads)

    widths = [(half, own_rows)] * 3 + [(half, half), (hidden, hidden_rows)]
    emit_at = [(pl.ds(i * own_rows, own_rows), pl.ds(3 * half, half)) for i in range(2)]
    payload_at = [(pl.ds(0, pair_rows), pl.ds(5 * half + hidden + i * breadth, breadth)) for i in range(stack)]
    columns = [(0, 3 * half), (4 * half, half + hidden)]
    if rounds:
        mine, other, sum_o, sum_fv = scatter.finish(core, columns, [(False, emit_at), (True, payload_at)])
        other = swap(other)
        outs = [jax.ShapeDtypeStruct((own_rows, 2 * size), F32) for size, _ in widths]
        sum_k, sum_v, sum_r, sum_fr, sum_fk = whole_call(
            partial(join_kernel, [width for _, width in widths]), outs, core, (mine, other)
        )
    else:
        total = scatter.result()
        pair = jnp.concatenate([total[:, start : start + size] for start, size in columns], axis=1)
        pair = pair.reshape(2, own_rows, -1)
        mine, other = mine_of(pair), swap(other_of(pair))
        low, high = jnp.where(core == 0, mine, other), jnp.where(core == 0, other, mine)
        outs, at = [], 0
        for size, width in widths:
            pieces = [piece[:, at : at + size].reshape(own_rows, -1, 1, width) for piece in (low, high)]
            outs.append(jnp.concatenate(pieces, axis=2).reshape(own_rows, 2 * size))
            at += size
        sum_k, sum_v, sum_r, sum_fr, sum_fk = outs
        sum_o = jnp.concatenate([total[at] for at in emit_at], axis=1)
        sum_fv = jnp.concatenate([total[at] for at in payload_at], axis=0)

    return (
        block_output[None],
        input_grad[None],
        *(grads[i] for i in range(7)),
        sum_k,
        sum_v,
        sum_r,
        sum_o,
        *(grads[i] for i in range(7, 11)),
        sum_fk,
        sum_fv,
        sum_fr,
    )


def solution(mesh):
    parts, groups = mesh.shape["seq"], mesh.shape["rep"]
    width = groups // 2
    fine = Mesh(mesh.devices.reshape(parts // width, width, width, 2), ALL)
    tokens = P(("y", "c"), SEQ, None)
    vector = P(ALL)
    matrix = P(ALL, None)
    return jax.shard_map(
        per_device,
        mesh=fine,
        in_specs=(
            (tokens, P(("y", "c"), None), tokens)
            + (vector,) * 7
            + (matrix,) * 4
            + (vector,) * 4
            + (matrix,) * 3
        ),
        out_specs=(
            (tokens, tokens) + (vector,) * 7 + (matrix,) * 4 + (vector,) * 4 + (matrix,) * 3
        ),
        check_vma=False,
    )
```

```python
from functools import partial

import jax
import jax.numpy as jnp
from jax import lax
from jax.experimental import pallas as pl
from jax.experimental.pallas import tpu as pltpu
from jax.sharding import Mesh, PartitionSpec as P

EPSILON = 1e-05
F32 = jnp.float32
BF16 = jnp.bfloat16
CHIPS = ("z", "x", "y")
SEQ = ("z", "x")
ALL = ("z", "x", "y", "c")
TILE = 16
FREE = pl.CostEstimate(flops=0, bytes_accessed=0, transcendentals=0)


def ring(count, step=1):
    return [(i, (i + step) % count) for i in range(count)]


def swap(block):
    return lax.ppermute(block, "c", ring(2))


def along_seq(block, step, cross=False):
    pairs = ring(lax.axis_size(SEQ), step)
    if cross:
        return lax.ppermute(block, SEQ + ("c",), [(2 * i + c, 2 * j + 1 - c) for i, j in pairs for c in range(2)])
    return lax.ppermute(block, SEQ, pairs)


ROUNDS = (
    (("z", (0, 0, 0), (1, 0, 0)), ("y", (0, 0, 0), (0, 0, 1)), ("x", (0, 0, 0), (0, 1, 0))),
    (("z", (1, 0, 0), (2, 0, 0)), ("y", (1, 0, 0), (1, 0, 1)), ("x", (0, 0, 1), (0, 1, 1))),
    (("z", (2, 0, 0), (3, 0, 0)), ("y", (2, 0, 0), (2, 0, 1)), ("x", (1, 0, 0), (1, 1, 0))),
    (("z", (0, 1, 1), (1, 1, 1)), ("y", (3, 0, 0), (3, 0, 1)), ("x", (3, 0, 0), (3, 1, 0))),
    (("z", (1, 1, 1), (2, 1, 1)), ("y", (3, 1, 0), (3, 1, 1)), ("x", (2, 0, 0), (2, 1, 0))),
)


def in_rounds():
    return tuple(lax.axis_size(axis) for axis in CHIPS) == (4, 2, 2)


RELATIVES = tuple((z, x, y) for z in range(4) for x in range(2) for y in range(2))
ANYWHERE = pl.BlockSpec(memory_space=pl.ANY)


def chip_table():
    whole = jnp.asarray(RELATIVES, jnp.int32)
    total = jnp.zeros((len(RELATIVES),), jnp.int32)
    for i, axis in enumerate(CHIPS):
        count = lax.axis_size(axis)
        total = total * count + lax.rem(lax.axis_index(axis) + (count - whole[:, i]), count)
    return jnp.concatenate([total, lax.axis_index("c")[None]]).astype(jnp.int32)


def whole_block(shape):
    return pl.BlockSpec(shape, lambda *g: (0,) * len(shape))


def in_hbm(array):
    return pltpu.with_memory_space_constraint(array, pltpu.HBM)


LAST = []
HELD = []


def where_it_is(array):
    kinds = [kind for held, kind in HELD if held is array]
    return pltpu.with_memory_space_constraint(array, kinds[0]) if kinds else array


def run(
    kernel, *, out_shape, grid=(1,), in_specs=None, out_specs=None, grid_spec=None, hbm=(), vmem=(), **settings
):
    spec = grid_spec or dict(num_scalar_prefetch=0, grid=grid, in_specs=in_specs, out_specs=out_specs)
    spec.setdefault("scratch_shapes", settings.pop("scratch_shapes", ()))
    direct = not spec["grid"]
    single = isinstance(out_shape, jax.ShapeDtypeStruct)
    shapes = [out_shape] if single else list(out_shape)
    kinds = [pltpu.HBM if i in hbm else pltpu.VMEM if i in vmem else None for i in range(len(shapes))]
    shapes = [out if kind is None else kind(out.shape, out.dtype) for out, kind in zip(shapes, kinds)]

    def call(*operands):
        marks = [mark for mark in LAST if not any(mark is operand for operand in operands)]
        count = len(operands)
        outputs = count + len(marks) + len(shapes)

        def body(*refs):
            refs[outputs][...] = jnp.zeros_like(refs[outputs])
            kernel(*refs[:count], *refs[count + len(marks) : outputs], *refs[outputs + 1 :])

        out_specs = [spec["out_specs"]] if single else list(spec["out_specs"])
        *outs, token = pl.pallas_call(
            body,
            grid_spec=pltpu.PrefetchScalarGridSpec(
                **{
                    **spec,
                    "in_specs": list(spec["in_specs"]) + [ANYWHERE] * len(marks),
                    "out_specs": out_specs + [pl.BlockSpec(memory_space=pltpu.VMEM) if direct else whole_block((8, 128))],
                }
            ),
            out_shape=shapes + [jax.ShapeDtypeStruct((8, 128), F32) if direct else pltpu.HBM((8, 128), F32)],
            cost_estimate=FREE,
            **settings,
        )(*map(where_it_is, operands), *map(where_it_is, marks))
        LAST[:] = [token]
        HELD.extend((out, kind) for out, kind in zip(outs + [token], kinds + [None if direct else pltpu.HBM]) if kind is not None)
        return outs[0] if single else outs

    return call


def hold_kernel(*refs):
    pass


def hold(*arrays, kind=None):
    return run(
        hold_kernel,
        out_shape=[jax.ShapeDtypeStruct(array.shape, array.dtype) for array in arrays],
        vmem=range(len(arrays)) if kind else (),
        in_specs=[ANYWHERE] * len(arrays),
        out_specs=[ANYWHERE] * len(arrays),
        input_output_aliases={i: i for i in range(len(arrays))},
    )(*(pltpu.with_memory_space_constraint(array, kind) if kind else array for array in arrays))


def wait_for(*arrays):
    LAST.extend(arrays)
    run(hold_kernel, out_shape=[], in_specs=[], out_specs=[])()


def place_kernel(first, views, aliased, table_ref, *refs):
    blocks = refs[: len(first)]
    outs = refs[len(first) + aliased : -1]
    copies = []
    for i, block in enumerate(blocks):
        for number, (out, source, target) in enumerate(views[0]):
            copies.append(
                pltpu.make_async_copy(
                    block.at[source],
                    outs[out].at[(table_ref[first[i]],) + target],
                    refs[-1].at[i, number],
                )
            )
    for copy in copies:
        copy.start()
    for copy in copies:
        copy.wait()


def place_blocks(table, held, blocks, relatives, views):
    moves, shapes, _ = views
    chips = lax.axis_size(CHIPS)
    first = [RELATIVES.index(relative) for relative in relatives]
    operands = [table, *blocks]
    aliases = {}
    if held is not None:
        aliases = {len(operands) + i: i for i in range(len(shapes))}
        operands += held
    hbm = pl.BlockSpec(memory_space=pltpu.HBM)
    return run(
        partial(place_kernel, first, views, len(aliases)),
        grid=(1,),
        in_specs=[pl.BlockSpec(memory_space=pltpu.SMEM)]
        + [whole_block(block.shape) for block in blocks]
        + [hbm] * len(aliases),
        out_specs=[hbm] * len(shapes),
        out_shape=[jax.ShapeDtypeStruct((chips,) + shape, BF16) for shape in shapes],
        scratch_shapes=[pltpu.SemaphoreType.DMA((len(blocks), len(moves)))],
        input_output_aliases=aliases,
    )(*operands)


class GatherRounds:
    def __init__(self, table, block, views):
        self.table, self.views = table, views
        self.have = {(0, 0, 0): block}
        self.held, self.due = None, []

    def place(self, number):
        names = [(0, 0, 0)] if number < 0 else [received for _, _, received in ROUNDS[number]]
        blocks = [self.have[name] for name in names]
        self.held = place_blocks(self.table, self.held, blocks, names, self.views)

    def step(self, number):
        names = list({sent: None for _, sent, _ in ROUNDS[number]}) if number else []
        LAST.extend(array for array in self.due if not any(array is self.have[name] for name in names))
        if names:
            self.have.update(zip(names, hold(*(self.have[name] for name in names), kind=pltpu.VMEM)))
        for axis, sent, received in ROUNDS[number]:
            self.have[received] = lax.ppermute(self.have[sent], axis, ring(lax.axis_size(axis)))
        self.due = [self.have[received] for _, _, received in ROUNDS[number]]

    def last_blocks(self):
        names = [received for _, _, received in ROUNDS[-1]]
        return [RELATIVES.index(name) for name in names], [self.have[name] for name in names]


class GatherRings:
    def __init__(self, table, block, views):
        self.held = gather_rings(block, views)

    def place(self, number):
        pass

    def step(self, number):
        pass

    def last_blocks(self):
        return [], []


def gather_rings(block, views):
    have = []
    shape = block.shape
    for axis in CHIPS:
        count = lax.axis_size(axis)
        me = lax.axis_index(axis)
        have.append(axis)
        place = len(have) - 1
        whole = jnp.zeros(block.shape[:place] + (count,) + block.shape[place:], block.dtype)
        piece = block
        for step in range(count):
            if step:
                piece = lax.ppermute(piece, axis, ring(count))
            whole = lax.dynamic_update_index_in_dim(whole, piece, lax.rem(me - step + count, count), place)
        block = whole
    block = block.reshape((-1,) + shape)
    held = [jnp.zeros(block.shape[:1] + view, block.dtype) for view in views[1]]
    for out, source, target in views[0]:
        held[out] = held[out].at[(slice(None),) + target].set(block[(slice(None),) + source])
    return held


def sum_kernel(first, counts, views, passing, table_ref, *refs):
    arrays, wanted = len(views[1]), len(counts)
    inputs = arrays + sum(counts) + passing
    grads = refs[:arrays]
    received = refs[arrays : arrays + sum(counts)]
    outs = refs[inputs : inputs + wanted]
    *own, sems = refs[inputs + wanted + passing :]
    copies = [
        [
            pltpu.make_async_copy(grads[a].at[table_ref[chip]], own[a].at[i], sems.at[i, a])
            for a in range(arrays)
            if chip is not None
        ]
        for i, chip in enumerate(first)
    ]
    for copy in sum(copies, []):
        copy.start()
    at = 0
    for i, count in enumerate(counts):
        for copy in copies[i]:
            copy.wait()
        for out, source, target in pieces_of(views):
            terms = [] if first[i] is None else [own[out][(i,) + target].astype(F32)]
            terms += [received[j][source].astype(F32) for j in range(at, at + count)]
            outs[i][source] = sum(terms[1:], terms[0]).astype(outs[i].dtype)
        at += count


def pieces_of(views):
    moves, shapes, block_shape = views
    spans = lambda place, size: (place.start, place.size) if isinstance(place, pl.Slice) else (0, size)
    for out, source, target in moves:
        starts = [spans(place, size) for place, size in zip(source + target, block_shape + shapes[out])]
        (top, rows), (left, columns), (low, _), (first, _) = starts
        for i in range(0, rows, 32):
            for j in range(0, columns, 512):
                size = (min(32, rows - i), min(512, columns - j))
                place = lambda row, column: (pl.ds(row + i, size[0]), pl.ds(column + j, size[1]))
                yield out, place(top, left), place(low, first)


def sum_blocks(table, grads, relatives, received, views, passing=()):
    _, shapes, block_shape = views
    first = [None if relative is None else RELATIVES.index(relative) for relative in relatives]
    counts = [len(blocks) for blocks in received]
    flat = [block for blocks in received for block in blocks]
    vmem = pl.BlockSpec(memory_space=pltpu.VMEM)
    count = 1 + len(grads) + len(flat)
    return run(
        partial(sum_kernel, first, counts, views, len(passing)),
        grid=(),
        in_specs=[pl.BlockSpec(memory_space=pltpu.SMEM)]
        + [pl.BlockSpec(memory_space=pltpu.HBM)] * len(grads)
        + [vmem] * len(flat)
        + [ANYWHERE] * len(passing),
        out_specs=[vmem] * len(relatives) + [ANYWHERE] * len(passing),
        out_shape=[jax.ShapeDtypeStruct(block_shape, BF16)] * (len(relatives) + len(passing)),
        input_output_aliases={count + i: len(relatives) + i for i in range(len(passing))},
        scratch_shapes=[pltpu.VMEM((len(relatives),) + shape, BF16) for shape in shapes]
        + [pltpu.SemaphoreType.DMA((len(relatives), len(shapes)))],
        compiler_params=pltpu.CompilerParams(vmem_limit_bytes=8 << 20),
    )(table, *grads, *flat, *passing)


def finish_kernel(views, count, pieces, wholes, table_ref, *refs):
    grads, received = refs[: len(views[1])], refs[len(views[1]) : len(views[1]) + count]
    mine, other, *outs, total_ref = refs[len(views[1]) + count :]
    for out, source, target in pieces_of(views):
        total = grads[out][(0,) + target].astype(F32)
        for block in received:
            total += block[source].astype(F32)
        total_ref[source] = total
    core = table_ref[len(RELATIVES)]
    rows = mine.shape[0]
    at = 0
    for start, size in pieces:
        low, high = total_ref[:rows, start : start + size], total_ref[rows:, start : start + size]
        here = pl.ds(at, size)
        mine[:, here] = jnp.where(core == 0, low, high)
        other[:, here] = jnp.where(core == 0, high, low)
        at += size
    for out, (tall, parts) in zip(outs, wholes):
        at = 0
        for place in parts:
            size = place[0].size if tall else place[1].size
            out[(pl.ds(at, size), slice(None)) if tall else (slice(None), pl.ds(at, size))] = total_ref[place]
            at += size


class ScatterRounds:
    def __init__(self, table, grads, views):
        self.table, self.views = table, views
        self.grads = [in_hbm(grad) for grad in grads]
        self.arrived, self.made, self.due = {}, {}, []

    def ahead(self, *names, most=2):
        came = [self.arrived.pop(name, []) for name in names]
        self.arrived.update((name, blocks[most:]) for name, blocks in zip(names, came) if blocks[most:])
        came = [blocks[:most] for blocks in came]
        self.made.update(zip(names, sum_blocks(self.table, self.grads, names, came, self.views)))

    def step(self, number, others=()):
        moves = ROUNDS[len(ROUNDS) - 1 - number]
        names = [sent for _, _, sent in moves]
        ready = [name for name in names if name in self.made and name not in self.arrived]
        missing = [name for name in names if name not in ready]
        came = [[self.made[name]] if name in self.made else [] for name in missing]
        came = [blocks + self.arrived.pop(name, []) for blocks, name in zip(came, missing)]
        own = [None if name in self.made else name for name in missing]
        LAST.extend(self.due + list(others))
        blocks = sum_blocks(
            self.table, self.grads, own, came, self.views, [self.made[name] for name in ready]
        )
        self.made.update(zip(missing + ready, blocks))
        self.due = []
        for axis, target, sent in moves:
            self.due.append(lax.ppermute(self.made[sent], axis, ring(lax.axis_size(axis), -1)))
            self.arrived.setdefault(target, []).append(self.due[-1])

    def finish(self, core, pieces, wholes):
        own = (0, 0, 0)
        came = self.arrived.pop(own)
        rows = self.views[2][0] // 2
        shapes = [(rows, sum(size for _, size in pieces))] * 2 + [
            (sum(r.size for r, _ in parts), parts[0][1].size) if tall else (parts[0][0].size, sum(c.size for _, c in parts))
            for tall, parts in wholes
        ]
        blocks = [
            pl.BlockSpec((1,) + shape, lambda g, table: (table[0],) + (0,) * len(shape)) for shape in self.views[1]
        ]
        return run(
            partial(finish_kernel, self.views, len(came), pieces, wholes),
            grid_spec=dict(
                num_scalar_prefetch=1,
                grid=(1,),
                in_specs=blocks + [whole_block(block.shape) for block in came],
                out_specs=[whole_block(shape) for shape in shapes],
                scratch_shapes=[pltpu.VMEM(self.views[2], F32)],
            ),
            out_shape=[jax.ShapeDtypeStruct(shape, F32) for shape in shapes],
            compiler_params=pltpu.CompilerParams(vmem_limit_bytes=16 << 20),
        )(self.table, *self.grads, *came)


class ScatterRings:
    def __init__(self, table, grads, views):
        self.sums = scatter_rings(grads, views)
        self.views = views

    def ahead(self, *names, most=2):
        pass

    def step(self, number, others=()):
        pass

    def result(self):
        moves, _, block_shape = self.views
        block = jnp.zeros(block_shape, F32)
        for out, source, target in moves:
            block = block.at[source].set(self.sums[out][target])
        return block


def picked(width, core):
    source = lax.broadcasted_iota(jnp.int32, (256, 128), 0)
    target = lax.broadcasted_iota(jnp.int32, (256, 128), 1)
    wanted = (target // width) * (2 * width) + core * width + target % width
    return jnp.where(source == wanted, 1.0, 0.0).astype(BF16)


def pick_kernel(widths, core_ref, *refs):
    matrices, outs = refs[: len(widths)], refs[len(widths) :]
    core = core_ref[0]
    for out, wanted in zip(outs, (core, 1 - core)):
        at = 0
        for width, matrix in zip(widths, matrices):
            half = matrix.shape[1] // 2
            if width == half:
                out[:, at : at + half] = jnp.where(wanted == 0, matrix[:, :half], matrix[:, half:])
            else:
                choice = picked(width, wanted)
                for i in range(half // 128):
                    columns = dot(matrix[:, i * 256 : (i + 1) * 256], choice)
                    out[:, at + i * 128 : at + (i + 1) * 128] = columns.astype(BF16)
            at += half


def pack_kernel(half, core_ref, mine, other, emit, payload, block):
    rows, breadth = emit.shape
    core = core_ref[0]
    split = 3 * half
    last = half + mine.shape[1]
    for i, (own, its) in enumerate(((mine, other), (other, mine))):
        here = pl.ds(i * rows, rows)
        block[here, :split] = jnp.where(core == 0, own[:, :split], its[:, :split])
        block[here, split : split + half] = emit[:, i * half : (i + 1) * half]
        block[here, split + half : last] = jnp.where(core == 0, own[:, split:], its[:, split:])
    height = 2 * rows
    for i in range(payload.shape[0] // height):
        block[:, last + i * breadth : last + (i + 1) * breadth] = payload[i * height : (i + 1) * height, :]


def stack_kernel(*refs):
    for i, piece in enumerate(refs[:-1]):
        for device in range(refs[-1].shape[0]):
            refs[-1][device, i : i + 1, :] = piece[...]


def join_kernel(widths, core_ref, mine, other, *outs):
    core = core_ref[0]
    rows = mine.shape[0]
    at = 0
    for width, out in zip(widths, outs):
        half = out.shape[1] // 2
        low = jnp.where(core == 0, mine[:, at : at + half], other[:, at : at + half])
        high = jnp.where(core == 0, other[:, at : at + half], mine[:, at : at + half])
        if width == half:
            out[:, :half] = low
            out[:, half:] = high
        elif width == 128:
            for i in range(half // 128):
                out[:, i * 256 : i * 256 + 128] = low[:, i * 128 : (i + 1) * 128]
                out[:, i * 256 + 128 : (i + 1) * 256] = high[:, i * 128 : (i + 1) * 128]
        else:
            for i in range(half // 128):
                total = jnp.zeros((rows, 256), F32)
                for number, part in enumerate((low, high)):
                    rest = part[:, i * 128 : (i + 1) * 128]
                    for _ in range(3):
                        piece = rest.astype(BF16)
                        total += dot_back(piece, picked(width, number))
                        rest = rest - piece.astype(F32)
                out[:, i * 256 : (i + 1) * 256] = total
        at += half


def whole_call(kernel, shapes, scalar, operands, hbm=()):
    return run(
        kernel,
        grid=(1,),
        out_shape=shapes,
        in_specs=[pl.BlockSpec(memory_space=pltpu.SMEM)] + [whole_block(operand.shape) for operand in operands],
        out_specs=[whole_block(out.shape) for out in shapes],
        hbm=hbm,
        compiler_params=pltpu.CompilerParams(vmem_limit_bytes=16 << 20),
    )(scalar.astype(jnp.int32).reshape(1), *operands)


def sum_axis(block, axis, place):
    count = lax.axis_size(axis)
    me = lax.axis_index(axis)

    def part(step):
        return lax.dynamic_index_in_dim(block, lax.rem(me + step, count), place, keepdims=False)

    total = part(1)
    for step in range(2, count + 1):
        moved = lax.ppermute(total.astype(BF16), axis, ring(count, -1))
        total = moved.astype(F32) + part(step).astype(F32)
    return total


def sum_along_z(block):
    return lax.psum_scatter(block.astype(BF16), "z", scatter_dimension=0).astype(F32)


def scatter_rings(grads, views):
    sizes = tuple(lax.axis_size(axis) for axis in CHIPS)
    sums = []
    for grad in grads:
        block = grad.reshape(sizes + grad.shape[1:])
        sums.append(sum_along_z(sum_axis(sum_axis(block, "x", 1), "y", 1)))
    return sums


def dot(left, right):
    return jnp.dot(left, right, preferred_element_type=F32)


def dot_back(grad, weight):
    return lax.dot_general(grad, weight, (((1,), (1,)), ((), ())), preferred_element_type=F32)


def outer(left, right):
    return lax.dot_general(left, right, (((0,), (0,)), ((), ())), preferred_element_type=F32)


def norm_parts(rows):
    center = jnp.mean(rows, axis=-1, keepdims=True)
    deviation = rows - center
    variance = jnp.mean(deviation * deviation, axis=-1, keepdims=True)
    inverse = lax.rsqrt(variance + EPSILON)
    return deviation * inverse, inverse


def last_row(rows):
    return lax.broadcasted_iota(jnp.int32, rows.shape, 0) == rows.shape[0] - 1


def first_row(rows):
    return lax.broadcasted_iota(jnp.int32, rows.shape, 0) == 0


def both_kernel(core_ref, *refs):
    count = len(refs) // 3
    for i in range(count):
        refs[2 * count + i][...] = jnp.where(core_ref[0] == pl.program_id(0), refs[2 * i][...], refs[2 * i + 1][...])


def both_groups(core, *pairs):
    rows, breadth = pairs[0][0].shape
    return run(
        both_kernel,
        grid=(2,),
        in_specs=[pl.BlockSpec(memory_space=pltpu.SMEM)]
        + [pl.BlockSpec((rows, breadth), lambda g: (0, 0))] * (2 * len(pairs)),
        out_specs=[pl.BlockSpec((rows, breadth), lambda g: (g, 0))] * len(pairs),
        out_shape=[jax.ShapeDtypeStruct((2 * rows, breadth), pair[0].dtype) for pair in pairs],
        hbm=range(len(pairs)),
        compiler_params=pltpu.CompilerParams(vmem_limit_bytes=16 << 20),
    )(core.astype(jnp.int32).reshape(1), *(part for pair in pairs for part in pair))


def parameters_kernel(
    core_ref, got, behind, keep, gain1, bias1, shares1, gain2, bias2, shares2, rate, bonus, behind1, *befores
):
    core = core_ref[0]
    own_rows = got.shape[-1]
    targets = ((gain1, 0, 1), (bias1, 1, 2), (shares1, 2, 5), (gain2, 5, 6), (bias2, 6, 7), (shares2, 7, 9))
    for chip in range(got.shape[0] // 2):
        pieces = [got[2 * chip + i].astype(F32) for i in range(2)]
        for i, piece in enumerate(pieces):
            for out, start, stop in targets:
                out[:, (2 * chip + i) * own_rows : (2 * chip + i + 1) * own_rows] = piece[start:stop]
        piece = jnp.exp(jnp.where(core == 0, pieces[0][9:], pieces[1][9:]))
        for i, out in enumerate((rate, bonus)):
            out[:, chip * own_rows : (chip + 1) * own_rows] = piece[i : i + 1]
    rows = [[] for _ in befores]
    for group in range(2):
        normed = norm_parts(behind[group].astype(F32))[0] * gain1[...] + bias1[...]
        behind1[group : group + 1, :] = normed[1:] * keep[group : group + 1, :]
        for i in range(len(befores)):
            rows[i].append(normed[1:] - (normed[1:] - normed[:1]) * (1.0 - shares1[i : i + 1, :]))
    for before, pair in zip(befores, rows):
        zeros = jnp.zeros((before.shape[0] - 2, before.shape[1]), F32)
        before[...] = jnp.concatenate(pair + [zeros], axis=0).astype(BF16)


def vectors_kernel(
    core_ref, norm1, shares1, decay, first, rate_ref, norm2, shares2, out
):
    core = core_ref[0]
    own_rows = out.shape[-1]
    devices = out.shape[0]
    rate = rate_ref[...]
    grad_decay = -rate * jnp.exp(-rate) * jnp.sum(decay[...], axis=0, keepdims=True)
    grad_first = jnp.sum(first[...], axis=0, keepdims=True)
    norms2 = jnp.where(core == 0, norm2[0], norm2[1])
    for device in range(devices):
        here = slice(device * own_rows, (device + 1) * own_rows)
        chip, owner = device // 2, device % 2
        out[device, 0:2, :] = norm1[0][:, here]
        out[device, 2:5, :] = shares1[:, here]
        channels = slice(chip * own_rows, (chip + 1) * own_rows)
        out[device, 5:6, :] = jnp.where(core == owner, grad_decay[:, channels], 0.0)
        out[device, 6:7, :] = jnp.where(core == owner, grad_first[:, channels], 0.0)
        out[device, 7:9, :] = norms2[:, here]
        out[device, 9:11, :] = shares2[:, here]


def vector_sums_kernel(parts, out):
    total = parts[0]
    for i in range(1, parts.shape[0]):
        total = total + parts[i]
    out[...] = total


def outer_kernel(count, *refs):
    for i in range(count):
        refs[2 * count + i][...] = outer(refs[2 * i][...], refs[2 * i + 1][...]).astype(BF16)


def outer_call(*pairs):
    half = lambda array: (array.shape[0], array.shape[1] // 2)
    outs = [jax.ShapeDtypeStruct((left.shape[1], right.shape[1]), BF16) for left, right in pairs]
    return run(
        partial(outer_kernel, len(pairs)),
        grid=(2,),
        in_specs=[
            spec
            for left, right in pairs
            for spec in (whole_block(left.shape), pl.BlockSpec(half(right), lambda i: (0, i)))
        ],
        out_specs=[pl.BlockSpec(half(out), lambda i: (0, i)) for out in outs],
        out_shape=outs,
        hbm=range(len(pairs)),
        compiler_params=pltpu.CompilerParams(vmem_limit_bytes=24 << 20),
    )(*(array for pair in pairs for array in pair))


def norm_mix_kernel(terms, behind, gain, bias, shares, *refs):
    rows = terms[0][...].astype(F32)
    for term in terms[1:]:
        rows = rows + term[...].astype(F32)
    outs = list(refs)
    if len(terms) > 1:
        outs.pop(0)[...] = rows
    zhat, inverse = norm_parts(rows)
    outs.pop(0)[...] = zhat.astype(BF16)
    outs.pop(0)[...] = inverse
    normed = zhat * gain[...] + bias[...]
    group = pl.program_id(0)
    before = jnp.where(group == 0, behind[:1, :], behind[1:, :])
    step = normed - jnp.where(first_row(normed), before, shift_rows(normed, 1))
    for i, out in enumerate(outs):
        out[...] = (normed - step * (1.0 - shares[i : i + 1, :])).astype(BF16)


def norm_mix(terms, behind, gain, bias, shares, hbm):
    rows, breadth = terms[0].shape
    block = pl.BlockSpec((rows // 2, breadth), lambda g: (g, 0))
    whole = lambda element: pl.BlockSpec(element.shape, lambda g: (0, 0))
    shape = lambda kind: jax.ShapeDtypeStruct((rows, breadth), kind)
    wide = [shape(F32)] * (len(terms) > 1) + [shape(BF16)]

    def body(*refs):
        norm_mix_kernel(refs[: len(terms)], *refs[len(terms) :])

    return run(
        body,
        grid=(2,),
        in_specs=[block] * len(terms) + [whole(element) for element in (behind, gain, bias, shares)],
        out_specs=[block] * len(wide)
        + [pl.BlockSpec((rows // 2, 1), lambda g: (g, 0))]
        + [block] * shares.shape[0],
        out_shape=wide + [jax.ShapeDtypeStruct((rows, 1), F32)] + [shape(BF16)] * shares.shape[0],
        hbm=hbm,
        compiler_params=pltpu.CompilerParams(vmem_limit_bytes=18 << 20),
    )(*terms, behind, gain, bias, shares)


def norm_back_kernel(count, table, *refs):
    parts = refs[:count]
    came, zhat_ref, inverse_ref, gain, base = refs[count : count + 5]
    outs = refs[count + 5 :]
    grad = parts[0][...].astype(F32)
    for part in parts[1:]:
        grad = grad + part[...].astype(F32)
    group = pl.program_id(0)
    grad = grad + jnp.where(last_row(grad), jnp.where(group == 0, came[:1, :], came[-1:, :]), 0.0)
    zhat = zhat_ref[...].astype(F32)
    scaled = grad * gain[...]
    middle = jnp.mean(scaled, axis=-1, keepdims=True)
    slope = jnp.mean(scaled * zhat, axis=-1, keepdims=True)
    total = base[...].astype(F32) + inverse_ref[...] * (scaled - middle - zhat * slope)
    for out in outs[:-1]:
        out[...] = total.astype(out.dtype)
    outs[-1][0, :1, :] = jnp.sum(grad * zhat, axis=0, keepdims=True)
    outs[-1][0, 1:, :] = jnp.sum(grad, axis=0, keepdims=True)


def norm_back(core, parts, came, zhat, inverse, gain, base, kinds, own):
    breadth = zhat.shape[1]
    rows = zhat.shape[0] // 2
    groups = 1 if own else 2
    pick = lambda width: pl.BlockSpec((rows, width), lambda g, table: (table[0] if own else g, 0))
    block = pl.BlockSpec((rows, breadth), lambda g, table: (g, 0))
    whole = lambda element: pl.BlockSpec(element.shape, lambda g, table: (0, 0))
    return run(
        partial(norm_back_kernel, len(parts)),
        grid_spec=dict(
            num_scalar_prefetch=1,
            grid=(groups,),
            in_specs=[block] * len(parts)
            + [whole(came), pick(breadth), pick(1), whole(gain), pick(breadth)],
            out_specs=[block] * len(kinds) + [pl.BlockSpec((1, 2, breadth), lambda g, table: (g, 0, 0))],
        ),
        out_shape=[jax.ShapeDtypeStruct((groups * rows, breadth), kind) for kind in kinds]
        + [jax.ShapeDtypeStruct((groups, 2, breadth), F32)],
        hbm=() if own else (0,),
        compiler_params=pltpu.CompilerParams(vmem_limit_bytes=16 << 20),
    )(core.astype(jnp.int32).reshape(1), *parts, came, zhat, inverse, gain, base)


def output_kernel(core_ref, part, swapped, gate_own, gate_other, cot_ref, middle, out, d_value, d_gate):
    core = core_ref[0]
    half = gate_own.shape[1]
    value = part[...].astype(F32) + swapped[...].astype(F32)
    cot = cot_ref[...].astype(F32)
    own, other = gate_own[...], gate_other[...]
    for i in range(2):
        gate = jnp.where(core == i, own, other)
        here = pl.ds(i * half, half)
        out[:, here] = (middle[:, here] + gate * value[:, i * half : (i + 1) * half]).astype(BF16)
        d_value[:, here] = (cot[:, i * half : (i + 1) * half] * gate).astype(BF16)
    mine = lambda rows: jnp.where(core == 0, rows[:, :half], rows[:, half:])
    d_gate[...] = (mine(cot) * mine(value) * own * (1.0 - own)).astype(BF16)


def output(core, part, swapped, gate_own, gate_other, cot, middle):
    rows, breadth = part.shape
    block = lambda width: pl.BlockSpec((rows // 2, width), lambda g: (g, 0))
    half = breadth // 2
    return run(
        output_kernel,
        grid=(2,),
        in_specs=[pl.BlockSpec(memory_space=pltpu.SMEM)]
        + [block(width) for width in (breadth, breadth, half, half, breadth, breadth)],
        out_specs=[block(breadth), block(breadth), block(half)],
        out_shape=[jax.ShapeDtypeStruct((rows, width), BF16) for width in (breadth, breadth, half)],
        compiler_params=pltpu.CompilerParams(vmem_limit_bytes=16 << 20),
    )(core.astype(jnp.int32).reshape(1), part, swapped, gate_own, gate_other, cot, middle)


def shift_rows(rows, distance):
    return pltpu.roll(rows, distance % rows.shape[0], 0)


def fade_tables(rate, reverse):
    breadth = rate.shape[-1]
    place = lax.broadcasted_iota(jnp.int32, (TILE, breadth), 0)
    if reverse:
        place = TILE - 1 - place
    steps = []
    distance = 1
    while distance < TILE:
        factor = jnp.where(place >= distance, jnp.exp(-rate * float(distance)), 0.0)
        steps.append((distance, factor))
        distance *= 2
    passed = jnp.exp(-rate * place.astype(F32))
    before = (place >= 1).astype(F32)
    return steps, passed, before


def scan_tile(terms, steps, reverse):
    for distance, factor in steps:
        terms = terms + factor * shift_rows(terms, -distance if reverse else distance)
    return terms


def entering(reach, distance, ends, rate, rows, groups):
    totals = [[0.0, 0.0] for _ in range(groups)]
    for device in range(ends.shape[0]):
        fade = jnp.exp(-rate * (float(rows) * distance[device]))
        for group in range(groups):
            for i in range(2):
                term = ends[device, i, group : group + 1, :] * fade
                totals[group][i] += jnp.where(reach[group, device] > 0.5, term, 0.0)
    return [total for pair in totals for total in pair]


def wkv_kernel(
    groups, reach, distance, key_ref, value_ref, recept_ref, key_old, value_old, recept_old, rate_ref, bonus_ref,
    ends_ref, emit_ref, sent_ref, gated_ref, prior_num_ref, prior_den_ref,
):
    rows = key_ref.shape[0] // groups
    rate = rate_ref[...]
    bonus = bonus_ref[...]
    steps, passed, before = fade_tables(rate, False)
    tile_fade = jnp.exp(-rate * float(TILE))

    def body(index, carry):
        states = []
        for group in range(groups):
            num, den = carry[2 * group], carry[2 * group + 1]
            at = pl.ds(pl.multiple_of(group * rows + index * TILE, TILE), TILE)
            grown = jnp.exp(key_ref[at, :].astype(F32))
            product = grown * value_ref[at, :].astype(F32)
            inner_num = scan_tile(product, steps, False)
            inner_den = scan_tile(grown, steps, False)
            prior_num = shift_rows(inner_num, 1) * before + passed * num
            prior_den = shift_rows(inner_den, 1) * before + passed * den
            prior_num_ref[at, :] = prior_num
            prior_den_ref[at, :] = prior_den
            wkv = (prior_num + bonus * product) / (prior_den + bonus * grown)
            gated_ref[at, :] = (recept_ref[at, :] * wkv.astype(BF16).astype(F32)).astype(BF16)
            states.append(inner_num[TILE - 1 :, :] + tile_fade * num)
            states.append(inner_den[TILE - 1 :, :] + tile_fade * den)
        return tuple(states)

    start = entering(reach, distance, ends_ref, rate, rows, groups)
    lax.fori_loop(0, rows // TILE, body, tuple(start))
    attended = dot(gated_ref[...], emit_ref[...])
    sent_ref[: groups * rows, :] = attended.astype(BF16)
    pad = lambda rows: jnp.concatenate(rows + [jnp.zeros((TILE - groups, rate.shape[-1]), F32)], axis=0)
    grown = jnp.exp(key_old[...].astype(F32))
    product = grown * value_old[...].astype(F32)
    unfade = jnp.exp(rate)
    num = (pad(start[::2]) - product) * unfade + bonus * product
    den = (pad(start[1::2]) - grown) * unfade + bonus * grown
    old = (recept_old[...] * (num / den).astype(BF16).astype(F32)).astype(BF16)
    attended = dot(old, emit_ref[...])
    sent_ref[groups * rows :, :] = attended.astype(BF16)


def wkv_back_kernel(
    groups, reach, distance, key_ref, value_ref, prior_num_ref, prior_den_ref, weighted_ref, rate_ref, bonus_ref,
    ends_ref, drecept_ref, *refs,
):
    mixes, (dkey_ref, dvalue_ref, decay_ref, first_ref, late_ref), grads = refs[:3], refs[3:8], refs[8:]
    rows = key_ref.shape[0] // groups
    rate = rate_ref[...]
    bonus = bonus_ref[...]
    steps, passed, before = fade_tables(rate, True)
    tile_fade = jnp.exp(-rate * float(TILE))
    decay_ref[...] = jnp.zeros_like(decay_ref)
    first_ref[...] = jnp.zeros_like(first_ref)

    def body(step, carry):
        index = rows // TILE - 1 - step
        states = []
        for group in range(groups):
            num, den = carry[2 * group], carry[2 * group + 1]
            at = pl.ds(pl.multiple_of(group * rows + index * TILE, TILE), TILE)
            grown = jnp.exp(key_ref[at, :].astype(F32))
            value = value_ref[at, :].astype(F32)
            prior_num = prior_num_ref[at, :]
            prior_den = prior_den_ref[at, :]
            wkv_den = prior_den + bonus * grown
            wkv = (prior_num + bonus * grown * value) / wkv_den
            grad = weighted_ref[at, :].astype(F32) / wkv_den
            inner_num = scan_tile(grad, steps, True)
            inner_den = scan_tile(-grad * wkv, steps, True)
            lam_num = shift_rows(inner_num, -1) * before + passed * num
            lam_den = shift_rows(inner_den, -1) * before + passed * den
            bonus_grad = bonus * grad
            dvalue_ref[at, :] = (grown * (bonus_grad + lam_num)).astype(BF16)
            direct = bonus_grad * (value - wkv)
            dkey_ref[at, :] = (grown * (direct + lam_num * value + lam_den)).astype(BF16)
            first_ref[...] += grown * direct
            decay_ref[...] += lam_num * prior_num + lam_den * prior_den
            states.append(inner_num[:1, :] + tile_fade * num)
            states.append(inner_den[:1, :] + tile_fade * den)
        return tuple(states)

    late_ref[...] = drecept_ref[...]
    grads[2][...] = outer(mixes[2][...], drecept_ref[...]).astype(BF16)
    start = entering(reach, distance, ends_ref, rate, rows, groups)
    lax.fori_loop(0, rows // TILE, body, tuple(start))
    grads[0][...] = outer(mixes[0][...], dkey_ref[...]).astype(BF16)
    grads[1][...] = outer(mixes[1][...], dvalue_ref[...]).astype(BF16)


def wkv_start_kernel(
    groups, grad_ref, recept_ref, key_ref, value_ref, prior_num_ref, prior_den_ref, rate_ref, bonus_ref,
    weighted_ref, accept_ref, begin_ref,
):
    rows = key_ref.shape[0] // groups
    rate = rate_ref[...]
    bonus = bonus_ref[...]
    place = lax.broadcasted_iota(jnp.int32, (TILE, rate.shape[-1]), 0).astype(F32)
    tile_fade = jnp.exp(-rate * float(TILE))

    def body(index, carry):
        fade, sums = carry[0], []
        for group in range(groups):
            at = pl.ds(pl.multiple_of(group * rows + index * TILE, TILE), TILE)
            grown = bonus * jnp.exp(key_ref[at, :].astype(F32))
            wkv_den = prior_den_ref[at, :] + grown
            wkv = (prior_num_ref[at, :] + grown * value_ref[at, :].astype(F32)) / wkv_den
            recept = recept_ref[at, :]
            grad = grad_ref[at, :]
            kept = grad * recept
            weighted = kept.astype(BF16)
            weighted_ref[at, :] = weighted
            accept_ref[at, :] = (kept * wkv.astype(BF16).astype(F32) * (1.0 - recept)).astype(BF16)
            faded = fade * (weighted.astype(F32) / wkv_den)
            sums += [carry[1 + 2 * group] + faded, carry[2 + 2 * group] - faded * wkv]
        return (fade * tile_fade, *sums)

    zero = jnp.zeros((TILE, rate.shape[-1]), F32)
    _, *sums = lax.fori_loop(0, rows // TILE, body, (jnp.exp(-rate * place),) + (zero,) * (2 * groups))
    for group in range(groups):
        for i in range(2):
            total = jnp.sum(sums[2 * group + i], axis=0, keepdims=True)
            for device in range(begin_ref.shape[0]):
                begin_ref[device, i, group : group + 1, :] = total


def keys_start_kernel(chips, table, *refs):
    mixes, befores, weights = refs[:3], refs[3:6], refs[6:9]
    parts, lates, held = refs[9:12], refs[12:15], refs[15]
    height = lates[0].shape[1] // max(len(chips), 1)
    breadth = held.shape[0]
    tokens = mixes[0].shape[0]
    for i in range(3):
        held[...] = weights[i][...]
        for chip in chips:
            here = pl.ds(pl.multiple_of(table[chip] * height, height), height)
            held[here, :] = jnp.zeros((height, held.shape[1]), BF16)
        for rows, mixed in ((pl.ds(0, tokens), mixes[i]), (pl.ds(tokens, TILE), befores[i])):
            parts[i][rows, :] = dot(mixed[...], held[...])

    @pl.when(pl.program_id(0) == 0)
    def _():
        row = lax.broadcasted_iota(jnp.int32, (breadth, lates[0].shape[1]), 0)
        column = lax.broadcasted_iota(jnp.int32, (breadth, lates[0].shape[1]), 1)
        start = jnp.zeros_like(column)
        for j, chip in enumerate(chips):
            start = jnp.where(column // height == j, table[chip] * height, start)
        chosen = jnp.where(row == start + column % height, 1.0, 0.0).astype(BF16)
        for i in range(3):
            for rows, mixed in ((pl.ds(0, tokens), mixes[i]), (pl.ds(tokens, TILE), befores[i])):
                lates[i][rows, :] = dot(mixed[...], chosen).astype(BF16)


def keys_end_kernel(groups, blocks, *refs):
    parts, lates, late = refs[:3], refs[3:6], refs[6 : 6 + 3 * blocks]
    rate = refs[6 + 3 * blocks]
    *outs, ends = refs[7 + 3 * blocks :]
    tokens = outs[0].shape[0]
    for i in range(3):
        product = parts[i][...]
        if blocks:
            rows = jnp.concatenate([block[...] for block in late[i * blocks : (i + 1) * blocks]], axis=0)
            product = product + dot(lates[i][...], rows)
        if i == 2:
            product = jax.nn.sigmoid(product)
        outs[i][...] = product[:tokens].astype(outs[i].dtype)
        outs[3 + i][...] = product[tokens:].astype(outs[i].dtype)
    keys, values = outs[:2]
    rows = tokens // groups
    left = (rows - 1 - lax.broadcasted_iota(jnp.int32, (rows, keys.shape[1]), 0)).astype(F32)
    fades = jnp.exp(-rate[...] * left)
    for group in range(groups):
        here = pl.ds(group * rows, rows)
        grown = jnp.exp(keys[here, :].astype(F32)) * fades
        num = jnp.sum(grown * values[here, :].astype(F32), axis=0, keepdims=True)
        den = jnp.sum(grown, axis=0, keepdims=True)
        for device in range(ends.shape[0]):
            ends[device, 0, group : group + 1, :] = num
            ends[device, 1, group : group + 1, :] = den


def keys_start(table, mixes, befores, weights, chips):
    rows, breadth = mixes[0].shape
    columns = weights[0].shape[1]
    block = min(256, columns)
    late = max(len(chips), 1) * (breadth // lax.axis_size(CHIPS))
    wide = lambda height: pl.BlockSpec((height, block), lambda i, table: (0, i))
    return run(
        partial(keys_start_kernel, chips),
        grid_spec=dict(
            num_scalar_prefetch=1,
            grid=(columns // block,),
            in_specs=[whole_block((rows, breadth))] * 3 + [whole_block((TILE, breadth))] * 3 + [wide(breadth)] * 3,
            out_specs=[wide(rows + TILE)] * 3 + [whole_block((rows + TILE, late))] * 3,
            scratch_shapes=[pltpu.VMEM((breadth, block), BF16)],
        ),
        out_shape=[jax.ShapeDtypeStruct((rows + TILE, columns), F32)] * 3
        + [jax.ShapeDtypeStruct((rows + TILE, late), BF16)] * 3,
        hbm=range(6),
        compiler_params=pltpu.CompilerParams(vmem_limit_bytes=24 << 20),
    )(table, *mixes, *befores, *map(in_hbm, weights))


def keys_end(started, blocks, rate, parts):
    rows, columns = started[0].shape
    block = min(256, columns)
    steps = columns // block
    wide = lambda height: pl.BlockSpec((height, block), lambda i: (0, i))
    part = lambda number: pl.BlockSpec((blocks[0].shape[0], block), lambda i: (0, number * steps + i))
    shape = lambda height, kind: jax.ShapeDtypeStruct((height, columns), kind)
    kinds = (BF16, BF16, F32)
    return run(
        partial(keys_end_kernel, 2, len(blocks)),
        grid=(steps,),
        in_specs=[wide(rows)] * 3
        + [whole_block(started[3].shape)] * 3
        + [part(number) for number in range(3) for _ in blocks]
        + [wide(1)],
        out_specs=[wide(rows - TILE)] * 3 + [wide(TILE)] * 3 + [pl.BlockSpec((parts, 2, 2, block), lambda i: (0, 0, 0, i))],
        out_shape=[shape(rows - TILE, kind) for kind in kinds]
        + [shape(TILE, kind) for kind in kinds]
        + [jax.ShapeDtypeStruct((parts, 2, 2, columns), F32)],
        hbm=(0, 1, 2),
        compiler_params=pltpu.CompilerParams(vmem_limit_bytes=24 << 20),
    )(*started, *(list(blocks) * 3), rate)


def wkv_call(kernel, groups, shapes, operands, hbm=(), columns=1, scalars=(), wholes=()):
    def block(array):
        shape = array.shape[:-1] + (array.shape[-1] // columns,)
        return pl.BlockSpec(shape, lambda i: (0,) * (len(shape) - 1) + (i,))

    return run(
        partial(kernel, groups),
        grid=(columns,),
        out_shape=shapes,
        in_specs=[pl.BlockSpec(memory_space=pltpu.SMEM)] * len(scalars)
        + [block(operand) for operand in operands]
        + [whole_block(whole.shape) for whole in wholes],
        out_specs=[block(out) for out in shapes],
        hbm=hbm,
        compiler_params=pltpu.CompilerParams(vmem_limit_bytes=(20 if wholes else 14) << 20),
    )(*scalars, *operands, *wholes)


def mix_back_kernel(groups, count, core_ref, *refs):
    grads = refs[:count]
    zhat, behind, gain, bias, shares = refs[count : count + 5]
    *parts, first, sums = refs[count + 5 :]
    rows = zhat.shape[0] // groups
    totals = [0.0] * count
    for group in range(groups):
        here = pl.ds(group * rows, rows)
        normed = zhat[here, :].astype(F32) * gain[...] + bias[...]
        step = normed - jnp.where(first_row(normed), behind[group : group + 1, :], shift_rows(normed, 1))
        direct, shifted = 0.0, 0.0
        for i in range(count):
            grad = grads[i][here, :].astype(F32)
            moved = grad * (1.0 - shares[i : i + 1, :])
            direct += grad - moved
            shifted += moved
            totals[i] += jnp.sum(grad * step, axis=0, keepdims=True)
        first[group : group + 1, :] = shifted[:1, :]
        part = direct + jnp.where(last_row(shifted), 0.0, shift_rows(shifted, -1))
        if parts[0].shape == zhat.shape:
            parts[0][here, :] = part.astype(BF16)
        else:
            for i in range(2):

                @pl.when((core_ref[0] == group) == (i == 0))
                def _():
                    parts[i][...] = part.astype(parts[i].dtype)
    for i in range(count):
        sums[i : i + 1, :] = totals[i]


def mix_back(core, grads, zhat, behind, gain, bias, shares, apart):
    rows, breadth = zhat.shape
    count = len(grads)
    block = min(256, breadth)
    column = lambda height: pl.BlockSpec((height, block), lambda i: (0, i))
    outs = [(rows // 2, BF16)] * 2 if apart else [(rows, BF16)]
    outs += [(2, F32), (count, F32)]
    return run(
        partial(mix_back_kernel, 2, count),
        grid=(breadth // block,),
        in_specs=[pl.BlockSpec(memory_space=pltpu.SMEM)]
        + [column(rows)] * (count + 1)
        + [column(2), column(1), column(1), column(count)],
        out_specs=[column(height) for height, _ in outs],
        out_shape=[jax.ShapeDtypeStruct((height, breadth), kind) for height, kind in outs],
        compiler_params=pltpu.CompilerParams(vmem_limit_bytes=14 << 20),
    )(core.astype(jnp.int32).reshape(1), *grads, zhat, behind, gain, bias, shares)


def per_device(
    layer_incoming,
    series_extents,
    emitted_adjoint,
    norm1_scaling,
    norm1_offset,
    mixer_lookup_portion,
    mixer_payload_portion,
    mixer_accept_portion,
    temporal_fading_log,
    present_step_reward,
    mixer_lookup_matrix,
    mixer_payload_matrix,
    mixer_accept_matrix,
    mixer_emit_matrix,
    norm2_scaling,
    norm2_offset,
    feedforward_lookup_portion,
    feedforward_accept_portion,
    feedforward_lookup_matrix,
    feedforward_payload_matrix,
    feedforward_accept_matrix,
):
    LAST.clear()
    HELD.clear()
    devices = lax.axis_size(ALL)
    chips = lax.axis_size(CHIPS)
    parts = lax.axis_size(SEQ)
    core = lax.axis_index("c")
    place = lax.axis_index(SEQ)
    rows, breadth = layer_incoming.shape[1:]
    own_rows = mixer_lookup_matrix.shape[0]
    hidden_rows = feedforward_payload_matrix.shape[0]

    half = breadth // 2
    blocks = max(half // 256, 1)
    hidden = feedforward_lookup_matrix.shape[1] // 2
    both = lambda own, other: jnp.where(core == 0, jnp.stack([own, other]), jnp.stack([other, own]))
    mine_of = lambda pair: lax.dynamic_index_in_dim(pair, core, 0, keepdims=False)
    other_of = lambda pair: lax.dynamic_index_in_dim(pair, 1 - core, 0, keepdims=False)
    pair_rows = 2 * own_rows
    every = slice(None)
    mix_views = (
        tuple((i, (every, pl.ds(i * half, half)), (every, every)) for i in range(3))
        + tuple(
            (3, (pl.ds(i * own_rows, own_rows), pl.ds(3 * half, half)), (every, pl.ds(i * half, half)))
            for i in range(2)
        )
        + ((4, (every, pl.ds(4 * half, half)), (every, every)),),
        ((pair_rows, half),) * 3 + ((own_rows, breadth), (pair_rows, half)),
        (pair_rows, 5 * half),
    )
    stack = hidden_rows // pair_rows
    ffn_views = (
        ((0, (every, pl.ds(0, hidden)), (every, every)),)
        + tuple(
            (1, (every, pl.ds(hidden + i * breadth, breadth)), (pl.ds(i * pair_rows, pair_rows), every))
            for i in range(stack)
        ),
        ((pair_rows, hidden), (hidden_rows, breadth)),
        (pair_rows, hidden + stack * breadth),
    )
    gather_views = (
        mix_views[0]
        + tuple(
            (5 + out, (every, pl.ds(5 * half + source[1].start, source[1].size)), target)
            for out, source, target in ffn_views[0]
        ),
        mix_views[1] + ffn_views[1],
        (pair_rows, 5 * half + ffn_views[2][1]),
    )

    begins = jnp.cumsum(series_extents[0]) - series_extents[0]
    starts = jnp.any(jnp.arange(parts)[:, None] * rows == begins[None, :], axis=1)
    joined = jnp.where(starts, 0.0, 1.0).astype(F32)
    joined = both(joined, swap(joined))

    own_in, own_cot = in_hbm(layer_incoming[0]), in_hbm(emitted_adjoint[0])
    ends_of = lambda element: element.reshape(2, rows, -1)[:, rows - 2 :]

    rounds = in_rounds()
    table = chip_table() if rounds else jnp.zeros((1,), jnp.int32)
    split_up = (
        mixer_lookup_matrix, mixer_payload_matrix, mixer_accept_matrix,
        feedforward_accept_matrix, feedforward_lookup_matrix,
    )
    widths = (own_rows, own_rows, own_rows, half, hidden_rows)
    picks = jax.ShapeDtypeStruct((own_rows, 4 * half + hidden), BF16)
    both_inputs = lambda: both_groups(core, (own_in, swap(own_in)), (own_cot, swap(own_cot)))
    if rounds:
        mine, other = whole_call(partial(pick_kernel, widths), (picks, picks), core, tuple(map(in_hbm, split_up)))
        other = swap(other)
        (block,) = whole_call(
            partial(pack_kernel, half), [jax.ShapeDtypeStruct(gather_views[2], BF16)],
            core, (mine, other, in_hbm(mixer_emit_matrix), in_hbm(feedforward_payload_matrix)),
        )
    else:
        halves = jnp.concatenate(
            [
                matrix.reshape(own_rows, -1, 2, width).transpose(2, 0, 1, 3).reshape(2, own_rows, -1)
                for matrix, width in zip(split_up, widths)
            ],
            axis=-1,
        )
        pair = both(mine_of(halves), swap(other_of(halves))).reshape(pair_rows, -1)
        emit = jnp.concatenate([mixer_emit_matrix[:, :half], mixer_emit_matrix[:, half:]], axis=0)
        payload = [feedforward_payload_matrix[i * pair_rows : (i + 1) * pair_rows] for i in range(stack)]
        block = jnp.concatenate([pair[:, : 3 * half], emit, pair[:, 3 * half :], *payload], axis=1)
    Gather, Scatter = (GatherRounds, ScatterRounds) if rounds else (GatherRings, ScatterRings)
    weights = Gather(table, block, gather_views)
    weights.step(0)
    inputs, cotangent = both_inputs()
    weights.place(-1)
    pieces = (
        norm1_scaling, norm1_offset, mixer_lookup_portion, mixer_payload_portion,
        mixer_accept_portion, norm2_scaling, norm2_offset, feedforward_lookup_portion,
        feedforward_accept_portion, temporal_fading_log, present_step_reward,
    )
    pieces = [piece.reshape(1, own_rows) for piece in pieces]
    vectors = run(
        stack_kernel,
        out_shape=jax.ShapeDtypeStruct((devices, len(pieces), own_rows), BF16),
        in_specs=[whole_block(piece.shape) for piece in pieces],
        out_specs=whole_block((devices, len(pieces), own_rows)),
    )(*pieces)
    vectors = lax.all_to_all(vectors, ALL, 0, 0, tiled=True)
    (edge,) = hold(ends_of(inputs))
    behind = along_seq(edge, 1)
    LAST.append(joined)
    weights.step(1)
    LAST.extend([behind, vectors])
    weights.step(2)
    weights.place(0)

    keep = lax.dynamic_index_in_dim(joined, place, 1)[:, :, None]
    index = jnp.arange(parts)
    began = jnp.where((joined == 0.0) & (index[None] <= place), index[None], -1).max(axis=1)
    reach = ((index[None] < place) & (index[None] >= began[:, None])).astype(F32)
    begun = jnp.where((joined == 0.0) & (index[None] > place), index[None], parts).min(axis=1)
    reach_back = ((index[None] > place) & (index[None] < begun[:, None])).astype(F32)

    def spread(ends):
        return lax.all_to_all(ends, SEQ, 0, 0, tiled=True)

    distances = lambda places: jnp.maximum(places, 0).astype(F32)
    heights = [(height, breadth) for height in (1, 1, 3, 1, 1, 2)] + [(1, half), (1, half), (2, breadth)]
    shapes = [jax.ShapeDtypeStruct(shape, F32) for shape in heights] + [jax.ShapeDtypeStruct((TILE, breadth), BF16)] * 3
    gain1, bias1, shares1, gain2, bias2, shares2, rate, bonus, behind1, *mixed_before = run(
        parameters_kernel,
        out_shape=shapes,
        in_specs=[pl.BlockSpec(memory_space=pltpu.SMEM)]
        + [whole_block(array.shape) for array in (vectors, behind, keep[:, 0])],
        out_specs=[whole_block(shape.shape) for shape in shapes],
    )(core.astype(jnp.int32).reshape(1), vectors, behind, keep[:, 0])
    weights.place(1)
    zhat1, inverse1, mixed_k, mixed_v, mixed_r = norm_mix(
        [inputs], behind1, gain1, bias1, shares1, range(5)
    )
    weights.step(3)
    weights.place(2)
    weights.step(4)
    weights.place(3)
    whole = lambda held: held.reshape(-1, held.shape[-1])
    weight_k, weight_v, weight_r, *_ = map(whole, weights.held)
    chips_late, blocks_late = weights.last_blocks()
    started = keys_start(
        table, (mixed_k, mixed_v, mixed_r), mixed_before, (weight_k, weight_v, weight_r), chips_late
    )
    keys, values, recept, *before, ends = keys_end(started, blocks_late, rate, parts)
    weights.place(4)
    weight_k, weight_v, weight_r, weight_o, weight_fr, weight_fk, weight_fv = map(whole, weights.held)

    shape = lambda kind: jax.ShapeDtypeStruct((2 * rows, half), kind)
    sent, gated, prior_num, prior_den = wkv_call(
        wkv_kernel, 2,
        (
            jax.ShapeDtypeStruct((2 * rows + TILE, breadth), BF16),
            shape(BF16), shape(F32), shape(F32),
        ),
        (keys, values, recept, *before, rate, bonus, spread(ends), in_hbm(weight_o)), (1, 2, 3),
        scalars=(reach, distances(place - 1 - index)),
    )
    swapped = swap(sent)
    HELD.append((swapped, pltpu.HBM))
    before2 = behind[:, 1].astype(F32) + (sent[2 * rows :].astype(F32) + swapped[2 * rows :].astype(F32))[:2]
    behind2 = jnp.where(keep[:, 0] > 0.5, norm_parts(before2)[0] * gain2 + bias2, 0.0)
    middle, zhat2, inverse2, ffn_k, ffn_r = norm_mix(
        [inputs, sent, swapped], behind2, gain2, bias2, shares2, ()
    )
    gate_own = jax.nn.sigmoid(dot(ffn_r, weight_fr))
    gate_other = swap(gate_own)
    pre_hidden = jax.nn.relu(dot(ffn_k, weight_fk))
    hidden_act = jnp.square(pre_hidden).astype(BF16)
    value_part = dot(hidden_act, weight_fv).astype(BF16)
    block_output, d_value_out, d_gate_pre = output(
        core, value_part, swap(value_part), gate_own, gate_other, cotangent, middle
    )
    block_output = mine_of(block_output.reshape(2, rows, breadth))

    d_hidden = dot_back(d_value_out, weight_fv)
    d_pre_hidden = (d_hidden * 2.0 * pre_hidden).astype(BF16)
    low_back = lambda grad, weight: dot_back(grad, weight).astype(BF16)

    def came_back(first):
        first = first * keep[:, 0]
        return along_seq(first, -1) + along_seq(first, -1, True)

    part2, first2, share_grads2 = mix_back(
        core, (low_back(d_pre_hidden, weight_fk), low_back(d_gate_pre, weight_fr)),
        zhat2, behind2, gain2, bias2, shares2, False,
    )
    grad_fv, grad_fr = outer_call((hidden_act, d_value_out), (ffn_r, d_gate_pre))
    swapped2 = swap(part2)
    HELD.append((swapped2, pltpu.HBM))
    d_middle, d_attended, norm_grads2 = norm_back(
        core, (part2, swapped2), came_back(first2), zhat2, inverse2, gain2, cotangent,
        (F32, BF16), False,
    )

    d_gated = dot_back(d_attended, weight_o)
    d_weighted, d_recept_pre, begins_back = wkv_call(
        wkv_start_kernel, 2,
        (shape(BF16), shape(BF16), jax.ShapeDtypeStruct((parts, 2, 2, half), F32)),
        (d_gated, recept, keys, values, prior_num, prior_den, rate, bonus), columns=blocks,
    )
    grad_fk, grad_o = outer_call((in_hbm(ffn_k), in_hbm(d_pre_hidden)), (gated, d_attended))
    begins_back = spread(begins_back)
    small = jax.ShapeDtypeStruct((TILE, half), F32)
    grad = jax.ShapeDtypeStruct((breadth, half), BF16)
    d_keys, d_values, decay_sum, bonus_sum, d_recept_pre, grad_k, grad_v, grad_r = wkv_call(
        wkv_back_kernel, 2, (shape(BF16), shape(BF16), small, small, shape(BF16), grad, grad, grad),
        (keys, values, prior_num, prior_den, d_weighted, rate, bonus, begins_back, d_recept_pre),
        (5, 6, 7), columns=blocks, scalars=(reach_back, distances(index - place - 1)),
        wholes=(mixed_k, mixed_v, mixed_r),
    )
    per_chip = lambda grad: grad.reshape(chips, -1, grad.shape[-1])
    scatter = Scatter(
        table,
        [per_chip(grad) for grad in (grad_k, grad_v, grad_r, grad_o, grad_fr, grad_fk, grad_fv)],
        gather_views,
    )
    scatter.step(0)
    scatter.ahead((3, 0, 1), (2, 0, 1), (1, 1, 0))
    own1, other1, first1, share_grads1 = mix_back(
        core,
        (low_back(d_keys, weight_k), low_back(d_values, weight_v), low_back(d_recept_pre, weight_r)),
        zhat1, behind1, gain1, bias1, shares1, True,
    )
    swapped1 = swap(other1)
    first_sum = (first1 + swap(first1)) * keep[:, 0]
    scatter.step(1, [swapped1, first_sum])
    scatter.ahead((2, 0, 0), (1, 0, 1), (0, 1, 0))
    came1 = along_seq(first_sum, -1)
    scatter.step(2, [came1])
    scatter.ahead((0, 1, 1))
    input_grad, norm_grads1 = norm_back(
        core, (own1, swapped1), mine_of(came1[:, None]), zhat1, inverse1, gain1, d_middle, (F32,), True
    )
    pieces = (norm_grads1, share_grads1, decay_sum, bonus_sum, rate, norm_grads2, share_grads2)
    grads = run(
        vectors_kernel,
        out_shape=jax.ShapeDtypeStruct((devices, 11, own_rows), F32),
        in_specs=[pl.BlockSpec(memory_space=pltpu.SMEM)] + [whole_block(piece.shape) for piece in pieces],
        out_specs=whole_block((devices, 11, own_rows)),
    )(core.astype(jnp.int32).reshape(1), *pieces)
    scatter.step(3)
    scatter.ahead((1, 0, 0), most=1)
    scatter.step(4)
    (grads,) = hold(grads)
    grads = lax.all_to_all(grads, ALL, 0, 0, tiled=True)
    grads = run(
        vector_sums_kernel,
        out_shape=jax.ShapeDtypeStruct((11, own_rows), F32),
        in_specs=[whole_block(grads.shape)],
        out_specs=whole_block((11, own_rows)),
    )(grads)

    widths = [(half, own_rows)] * 3 + [(half, half), (hidden, hidden_rows)]
    emit_at = [(pl.ds(i * own_rows, own_rows), pl.ds(3 * half, half)) for i in range(2)]
    payload_at = [(pl.ds(0, pair_rows), pl.ds(5 * half + hidden + i * breadth, breadth)) for i in range(stack)]
    columns = [(0, 3 * half), (4 * half, half + hidden)]
    if rounds:
        mine, other, sum_o, sum_fv = scatter.finish(core, columns, [(False, emit_at), (True, payload_at)])
        other = swap(other)
        outs = [jax.ShapeDtypeStruct((own_rows, 2 * size), F32) for size, _ in widths]
        sum_k, sum_v, sum_r, sum_fr, sum_fk = whole_call(
            partial(join_kernel, [width for _, width in widths]), outs, core, (mine, other)
        )
    else:
        total = scatter.result()
        pair = jnp.concatenate([total[:, start : start + size] for start, size in columns], axis=1)
        pair = pair.reshape(2, own_rows, -1)
        mine, other = mine_of(pair), swap(other_of(pair))
        low, high = jnp.where(core == 0, mine, other), jnp.where(core == 0, other, mine)
        outs, at = [], 0
        for size, width in widths:
            pieces = [piece[:, at : at + size].reshape(own_rows, -1, 1, width) for piece in (low, high)]
            outs.append(jnp.concatenate(pieces, axis=2).reshape(own_rows, 2 * size))
            at += size
        sum_k, sum_v, sum_r, sum_fr, sum_fk = outs
        sum_o = jnp.concatenate([total[at] for at in emit_at], axis=1)
        sum_fv = jnp.concatenate([total[at] for at in payload_at], axis=0)

    return (
        block_output[None],
        input_grad[None],
        *(grads[i] for i in range(7)),
        sum_k,
        sum_v,
        sum_r,
        sum_o,
        *(grads[i] for i in range(7, 11)),
        sum_fk,
        sum_fv,
        sum_fr,
    )


def solution(mesh):
    parts, groups = mesh.shape["seq"], mesh.shape["rep"]
    width = groups // 2
    fine = Mesh(mesh.devices.reshape(parts // width, width, width, 2), ALL)
    tokens = P(("y", "c"), SEQ, None)
    vector = P(ALL)
    matrix = P(ALL, None)
    return jax.shard_map(
        per_device,
        mesh=fine,
        in_specs=(
            (tokens, P(("y", "c"), None), tokens)
            + (vector,) * 7
            + (matrix,) * 4
            + (vector,) * 4
            + (matrix,) * 3
        ),
        out_specs=(
            (tokens, tokens) + (vector,) * 7 + (matrix,) * 4 + (vector,) * 4 + (matrix,) * 3
        ),
        check_vma=False,
    )
```
